256 devices in a mesh: blk: 16 (over x, y_lo, core), rep: 16 (over y_hi, z).
Axes of the slice: x: 4, y: 4 (y_hi: 2, y_lo: 2; y = y_hi * 2 + y_lo), z: 8, core: 2. Of those that a mesh axis runs over, the one named last changes fastest.
Arguments:
- kinematics: float32 [6, 65536], P(None, 'blk'), may hold values from -6 to 6
- derivatives: float32 [6, 65536], P(None, 'blk'), may hold values from -6 to 6
- masses: float32 [65536], P('blk'), may hold values from 0.2 to 5
- last_time: float32 [65536], P('blk'), may hold values from -0.25 to -0.0625
- block_list: int32 [2, 16, 16, 2], replicated, may hold values from 0 to 31, as said below
- block_count: int32 [2, 16, 16], replicated, may hold values from 0 to 2, as said below
Outputs:
- new_kinematics: float32 [6, 65536], P(None, 'blk')
- new_derivatives: float32 [6, 65536], P(None, 'blk')
The draws below stay inside these ranges and needn't reach their ends.
Inputs may be any that keep to these rules, and one draw needn't show every extreme that they name: `block_list`: for each step and blk index the 32 listed block numbers are distinct. Slots at or past a device's count are ignored. `block_count`: in every step some device's count is 2.
All inputs are finite; a program needn't handle non-finite values.
Results may differ from the reference program's by a relative error of at most 0.0003.
Values sent between devices are 32-bit elements; how exact they have to be, the bound alone decides.
No kernel may reach another device: no remote copies, remote signals or barrier semaphores. Data moves between devices by JAX's collectives and lax.ppermute only.
A program may use at most 64 MiB of HBM per device.

```python
import math
import jax
import jax.numpy as jnp
from jax import lax

J_DEV = 4096
BLOCK = 128
CAP = 2
STEPS = 2
N = 65536
N_BLK = 16
N_REP = 16


def draw_block_list(key, part):
    key = jax.random.fold_in(key, 11)
    keys = jax.random.split(key, STEPS * N_BLK)
    orders = jax.vmap(lambda single: jax.random.permutation(single, J_DEV // BLOCK))(keys)
    taken = orders[:, :N_REP * CAP]
    return taken.reshape(STEPS, N_BLK, N_REP, CAP).astype(jnp.int32)


def draw_block_count(key, part):
    key = jax.random.fold_in(key, 23)
    first_key, second_key = jax.random.split(key)
    levels = jax.random.randint(first_key, (STEPS, N_BLK * N_REP), 0, 8)
    counted = (levels >= 4).astype(jnp.int32) + (levels >= 7).astype(jnp.int32)
    counted = jnp.minimum(counted, CAP)
    busiest = jax.random.randint(second_key, (STEPS, 1), 0, N_BLK * N_REP)
    places = jnp.arange(N_BLK * N_REP, dtype=jnp.int32)[None, :]
    counted = jnp.where(places == busiest, CAP, counted)
    return counted.reshape(STEPS, N_BLK, N_REP).astype(jnp.int32)


def block_levels(key, dims, cuts, low, largest):
    loudness, own = 1.0, jax.random.fold_in(key, 6)
    for dim, shards_of in cuts:
        steps = jnp.exp(jax.random.uniform(jax.random.fold_in(own, dim), (shards_of,), jnp.float32, low / len(cuts), largest / len(cuts)))
        loudness = loudness * jnp.repeat(steps, dims[dim] // shards_of).reshape([-1 if axis == dim else 1 for axis in range(len(dims))])
    return loudness


def centred(stream_key, extent, deviation, limit, cuts=(), kind=jnp.bfloat16):
    level = block_levels(stream_key, extent, cuts, -0.22, 0.18) if cuts else 1.0
    entries = jax.random.normal(stream_key, extent, jnp.float32) * deviation * level
    return jnp.minimum(jnp.maximum(entries, -limit), limit).astype(kind)


def setup_inputs(seed: int = 0) -> dict:
    splits = jax.random.split(jax.random.key(seed), 7)
    kinematics = centred(splits[0], (6, N), 1.0, 6.0, ((1, 16),), jnp.float32)
    derivatives = centred(splits[1], (6, N), 1.0, 6.0, ((1, 16),), jnp.float32)
    masses = jnp.clip(jnp.exp(math.log(5.0) - 3.218876 * jax.random.uniform(splits[2], (N,), jnp.float32) ** block_levels(splits[2], (N,), ((0, 16),), -0.2, 0.2)), 0.2, 5.0)
    last_time = jnp.clip(-0.25 + 0.1875 * jax.random.uniform(splits[3], (N,), jnp.float32) ** block_levels(splits[3], (N,), ((0, 16),), -0.2, 0.2), -0.25, -0.0625)
    block_list = draw_block_list(jax.random.fold_in(splits[6], 71), 0)
    block_count = draw_block_count(jax.random.fold_in(splits[6], 71), 0)
    return dict(kinematics=kinematics, derivatives=derivatives, masses=masses, last_time=last_time, block_list=block_list, block_count=block_count)


step_length = 0.125
softening = 0.0025

def predict(kinematics, derivatives, interval):
    position = kinematics[:3]
    velocity = kinematics[3:]
    acceleration = derivatives[:3]
    jerk_old = derivatives[3:]
    new_position = position + interval * (velocity + interval * (acceleration * 0.5 + interval * jerk_old / 6.0))
    new_velocity = velocity + interval * (acceleration + interval * jerk_old * 0.5)
    return jnp.concatenate([new_position, new_velocity], axis=0)

def pair_forces(targets, sources):
    delta_x = sources[0][None, :] - targets[0][:, None]
    delta_y = sources[1][None, :] - targets[1][:, None]
    delta_z = sources[2][None, :] - targets[2][:, None]
    delta_u = sources[3][None, :] - targets[3][:, None]
    delta_v = sources[4][None, :] - targets[4][:, None]
    delta_w = sources[5][None, :] - targets[5][:, None]
    radius_sq = delta_x * delta_x + delta_y * delta_y + delta_z * delta_z + softening
    inverse = lax.rsqrt(radius_sq)
    inverse_sq = inverse * inverse
    weight = sources[6][None, :] * inverse * inverse_sq
    radial = 3.0 * (delta_x * delta_u + delta_y * delta_v + delta_z * delta_w) * inverse_sq
    components = [lax.optimization_barrier(jnp.sum(weight * delta_x, axis=1)), lax.optimization_barrier(jnp.sum(weight * delta_y, axis=1)), lax.optimization_barrier(jnp.sum(weight * delta_z, axis=1)), lax.optimization_barrier(jnp.sum(weight * (delta_u - radial * delta_x), axis=1)), lax.optimization_barrier(jnp.sum(weight * (delta_v - radial * delta_y), axis=1)), lax.optimization_barrier(jnp.sum(weight * (delta_w - radial * delta_z), axis=1))]
    return jnp.stack(components, axis=0)

def field_forces(targets, sources, shard_width):
    pieces = sources.reshape(7, -1, shard_width).transpose(1, 0, 2)

    def add_piece(gathered_sum, incoming):
        return (gathered_sum + pair_forces(targets, incoming), None)
    initial = jnp.zeros((6, targets.shape[1]), jnp.float32)
    result, unused = lax.scan(add_piece, initial, pieces)
    return result

def correct(predicted, old_deriv, forces, interval):
    change = old_deriv[:3] - forces[:3]
    second_term = -6.0 * change - interval * (4.0 * old_deriv[3:] + 2.0 * forces[3:])
    third_term = 12.0 * change + 6.0 * interval * (old_deriv[3:] + forces[3:])
    new_position = predicted[:3] + interval * interval * (second_term / 24.0 + third_term / 120.0)
    new_velocity = predicted[3:] + interval * (second_term / 6.0 + third_term / 24.0)
    return jnp.concatenate([new_position, new_velocity], axis=0)

def reference(kinematics, derivatives, masses, last_time, block_list, block_count):
    block_total = N // BLOCK
    scaled = masses / N
    for step_number in range(STEPS):
        time_now = step_number * step_length
        predicted = predict(kinematics, derivatives, time_now - last_time)
        sources = jnp.concatenate([predicted, scaled[None, :]], axis=0)
        owners = jnp.arange(N_BLK, dtype=jnp.int32)[:, None, None] * (J_DEV // BLOCK)
        block_ids = (owners + block_list[step_number]).reshape(-1).astype(jnp.int32)
        column_slot = jnp.arange(CAP, dtype=jnp.int32)[None, None, :]
        is_valid = (column_slot < block_count[step_number][:, :, None]).reshape(-1)
        pred_blocks = predicted.reshape(6, block_total, BLOCK)

        def one_block(slot_entry):
            block_index, is_active = slot_entry
            targets = lax.dynamic_index_in_dim(pred_blocks, block_index, 1, keepdims=False)
            return lax.cond(is_active, lambda: field_forces(targets, sources, J_DEV), lambda: jnp.zeros((6, BLOCK), jnp.float32))
        forces = lax.map(one_block, (block_ids, is_valid))
        kin_blocks = kinematics.reshape(6, block_total, BLOCK)
        der_blocks = derivatives.reshape(6, block_total, BLOCK)
        last_blocks = last_time.reshape(block_total, BLOCK)
        pred_rows = jnp.take(pred_blocks, block_ids, axis=1).transpose(1, 0, 2)
        old_deriv = jnp.take(der_blocks, block_ids, axis=1).transpose(1, 0, 2)
        old_kin = jnp.take(kin_blocks, block_ids, axis=1).transpose(1, 0, 2)
        old_last = jnp.take(last_blocks, block_ids, axis=0)
        corrected = jax.vmap(correct)(pred_rows, old_deriv, forces, time_now - old_last)
        keep_mask = is_valid[:, None, None]
        kin_blocks = kin_blocks.at[:, block_ids].set(jnp.where(keep_mask, corrected, old_kin).transpose(1, 0, 2))
        der_blocks = der_blocks.at[:, block_ids].set(jnp.where(keep_mask, forces, old_deriv).transpose(1, 0, 2))
        last_blocks = last_blocks.at[block_ids].set(jnp.where(is_valid[:, None], time_now, old_last))
        kinematics = kin_blocks.reshape(6, N)
        derivatives = der_blocks.reshape(6, N)
        last_time = last_blocks.reshape(N)
    return (kinematics, derivatives)
```

```python
import functools

import jax
import jax.numpy as jnp
from jax import lax
from jax.experimental import pallas as pl
from jax.experimental.pallas import tpu as pltpu
from jax.sharding import PartitionSpec as P

BLOCK = 128
CAP = 2
STEPS = 2
ROWS = 8
F32 = jnp.float32
BF16 = jnp.bfloat16

step_length = 0.125
softening = 0.0025
grid_shift = 1.5 * 2.0**16
piece_rows = 128
chunk = 256
prep_width = 512


def predict(position, velocity, acceleration, jerk_old, interval):
    new_position = position + interval * (
        velocity + interval * (acceleration * 0.5 + interval * jerk_old / 6.0)
    )
    new_velocity = velocity + interval * (acceleration + interval * jerk_old * 0.5)
    return jnp.concatenate([new_position, new_velocity], axis=0)


def correct(predicted, old_deriv, forces, interval):
    change = old_deriv[:3] - forces[:3]
    second_term = -6.0 * change - interval * (4.0 * old_deriv[3:] + 2.0 * forces[3:])
    third_term = 12.0 * change + 6.0 * interval * (old_deriv[3:] + forces[3:])
    new_position = predicted[:3] + interval * interval * (second_term / 24.0 + third_term / 120.0)
    new_velocity = predicted[3:] + interval * (second_term / 6.0 + third_term / 24.0)
    return jnp.concatenate([new_position, new_velocity], axis=0)


def round_short(value):
    return value.astype(BF16).astype(F32)


def split_three(value):
    high = round_short(value)
    rest = value - high
    middle = round_short(rest)
    return high, middle, rest - middle


def stack_three(value):
    return jnp.concatenate(split_three(value), axis=0)


def star_pieces(stars):
    position, velocity = stars[0:3], stars[3:6]
    coarse = (position + grid_shift) - grid_shift
    coarse_a = round_short(coarse)
    coarse_b = coarse - coarse_a
    fine = position - coarse
    fine_a = round_short(fine)
    fine_b = round_short(fine - fine_a)
    fine = fine_a + fine_b
    square = jnp.sum(coarse * coarse, axis=0, keepdims=True)
    cross = jnp.sum(2.0 * coarse * fine + fine * fine, axis=0, keepdims=True)
    mixed = jnp.sum(position * velocity, axis=0, keepdims=True)
    return coarse_a, coarse_b, fine_a, fine_b, square, cross, mixed


def source_pieces(stars):
    ca, cb, fa, fb, square, cross, mixed = star_pieces(stars)
    va, vb, vc = split_three(stars[3:6])
    width = stars.shape[1]
    one = jnp.ones((3, width), F32)
    rows = [ca, ca, cb, cb, stack_three(square), one, jnp.zeros((6, width), F32)]
    rows += [ca, ca, cb, cb, fa, fa, fb, fb, fa, fa, stack_three(cross), one]
    rows += [va, va, va, vb, vb, vc, stack_three(mixed), one]
    rows += [jnp.zeros((piece_rows - 84, width), F32)]
    return jnp.concatenate(rows, axis=0)


def target_pieces(stars):
    ca, cb, fa, fb, square, cross, mixed = star_pieces(stars)
    va, vb, vc = split_three(stars[3:6])
    xa, xb, xc = split_three(stars[0:3])
    width = stars.shape[1]
    one = jnp.ones((3, width), F32)
    zero = jnp.zeros((3, width), F32)
    da, db = -2.0 * ca, -2.0 * cb
    ea, eb = -2.0 * fa, -2.0 * fb
    tail = jnp.zeros((piece_rows - 84, width), F32)
    radius = [da, db, da, db, one, stack_three(square), zero, zero]
    radius += [ea, eb, ea, eb, da, db, da, db, ea, eb, one, stack_three(cross + softening)]
    radius += [zero] * 8 + [tail]
    moving = [-va, -vb, -va, -vb, zero, zero, zero, zero]
    moving += [-vc, zero, zero, zero, -va, -vb, -va, zero, zero, zero, zero, zero]
    moving += [-xa, -xb, -xc, -xa, -xb, -xa, one, stack_three(mixed), tail]
    both = [jnp.concatenate(radius, axis=0), jnp.concatenate(moving, axis=0)]
    return jnp.concatenate(both, axis=1).astype(BF16)


def block_at(number):
    return pl.ds(pl.multiple_of(number * BLOCK, BLOCK), BLOCK)


def predicted_block(kin_ref, der_ref, last_ref, where, time_now):
    kin, der = kin_ref[:, where], der_ref[:, where]
    return predict(kin[:3], kin[3:], der[:3], der[3:], time_now - last_ref[:, where])


def list_place(step, blk, rep, slot, n_blk, n_rep):
    return ((step * n_blk + blk) * n_rep + rep) * CAP + slot


def write_targets(step, n_blk, n_rep, list_ref, kin_ref, der_ref, last_ref, out_ref):
    blk, rep = lax.axis_index("blk"), lax.axis_index("rep")
    rows = []
    for slot in range(CAP):
        number = list_ref[list_place(step, blk, rep, slot, n_blk, n_rep)]
        rows.append(predicted_block(kin_ref, der_ref, last_ref, block_at(number), step * step_length))
        rows.append(jnp.zeros((ROWS - 6, BLOCK), F32))
    mine = jnp.concatenate(rows, axis=0)
    for other in range(n_blk):
        out_ref[other] = mine


def targets_kernel(step, n_blk, n_rep, list_ref, kin_ref, der_ref, last_ref, out_ref):
    write_targets(step, n_blk, n_rep, list_ref, kin_ref, der_ref, last_ref, out_ref)


def forces_kernel(
    step, n_blk, n_rep, count_ref, target_ref, kin_ref, der_ref, last_ref, mass_ref,
    out_ref, pred_ref, piece_ref, moment_ref,
):
    rep = lax.axis_index("rep")
    width = kin_ref.shape[1]
    total = jnp.zeros((6, prep_width), F32)
    for part in range(width // prep_width):
        where = pl.ds(part * prep_width, prep_width)
        stars = predicted_block(kin_ref, der_ref, last_ref, where, step * step_length)
        pred_ref[:, where] = stars
        total = total + stars
    centre = jnp.sum(total, axis=1, keepdims=True) / width
    for part in range(width // prep_width):
        where = pl.ds(part * prep_width, prep_width)
        stars = pred_ref[:, where] - centre
        piece_ref[where, :] = source_pieces(stars).T.astype(BF16)
        scaled = mass_ref[:, where] / (width * n_blk)
        ones = jnp.ones((1, prep_width), F32)
        moments = jnp.concatenate([stars, ones, jnp.zeros_like(ones)], axis=0) * scaled
        moments = jnp.concatenate([stack_three(moments), jnp.zeros((8, prep_width), F32)], axis=0)
        moment_ref[:, where] = moments.astype(BF16)

    def one_slot(place, carry):
        blk = place // CAP
        slot = place % CAP
        active = slot < count_ref[(step * n_blk + blk) * n_rep + rep]

        @pl.when(active)
        def _():
            stars = target_ref[place][0:6] - centre
            against = target_pieces(stars)
            acc = jnp.zeros((32, 2 * BLOCK), F32)
            for part in range(width // chunk):
                where = pl.ds(part * chunk, chunk)
                both = jnp.dot(piece_ref[where, :], against, preferred_element_type=F32)
                inverse = lax.rsqrt(both[:, :BLOCK])
                inverse_sq = inverse * inverse
                weight = inverse * inverse_sq
                radial = weight * (inverse_sq * both[:, BLOCK:])
                pair = jnp.concatenate([weight, radial], axis=1)
                high = pair.astype(BF16)
                low = (pair - high.astype(F32)).astype(BF16)
                moments = moment_ref[:, where]
                acc = acc + jnp.dot(moments, high, preferred_element_type=F32)
                acc = acc + jnp.dot(moments, low, preferred_element_type=F32)
            acc = acc[0:8] + acc[8:16] + acc[16:24]
            by_weight, by_radial = acc[:, :BLOCK], acc[:, BLOCK:]
            sums = by_weight[0:6] - stars * by_weight[6:7]
            pull = by_radial[0:3] - stars[0:3] * by_radial[6:7]
            out_ref[place] = jnp.concatenate(
                [sums[0:3], sums[3:6] - 3.0 * pull, jnp.zeros((ROWS - 6, BLOCK), F32)], axis=0
            )

        @pl.when(jnp.logical_not(active))
        def _():
            out_ref[place] = jnp.zeros((ROWS, BLOCK), F32)

        return carry

    lax.fori_loop(0, n_blk * CAP, one_slot, 0)


def total_kernel(n_blk, n_rep, part_ref, out_ref):
    total = part_ref[0]
    for other in range(1, n_blk):
        total = total + part_ref[other]
    for other in range(n_rep):
        out_ref[other] = total


def update_kernel(
    step, n_blk, n_rep, list_ref, count_ref, force_ref, kin_ref, der_ref, last_ref,
    new_kin_ref, new_der_ref, new_last_ref, *next_refs,
):
    blk = lax.axis_index("blk")
    time_now = step * step_length
    new_kin_ref[...] = kin_ref[...]
    new_der_ref[...] = der_ref[...]
    new_last_ref[...] = last_ref[...]

    def one_slot(place, carry):
        rep = place // CAP
        slot = place % CAP

        @pl.when(slot < count_ref[(step * n_blk + blk) * n_rep + rep])
        def _():
            number = list_ref[list_place(step, blk, rep, slot, n_blk, n_rep)]
            where = block_at(number)
            predicted = predicted_block(kin_ref, der_ref, last_ref, where, time_now)
            forces = force_ref[place][0:6]
            interval = time_now - last_ref[:, where]
            new_kin_ref[:, where] = correct(predicted, der_ref[:, where], forces, interval)
            new_der_ref[:, where] = forces
            new_last_ref[:, where] = jnp.full((1, BLOCK), time_now, F32)

        return carry

    lax.fori_loop(0, n_rep * CAP, one_slot, 0)
    if next_refs:
        write_targets(
            step + 1, n_blk, n_rep, list_ref, new_kin_ref, new_der_ref, new_last_ref, next_refs[0]
        )


def shape_of(*sizes):
    return jax.ShapeDtypeStruct(sizes, F32)


def run_kernel(body, scalars, arrays, out_shape, scratch=()):
    return pl.pallas_call(
        body,
        out_shape=out_shape,
        in_specs=[pl.BlockSpec(memory_space=pltpu.SMEM)] * len(scalars)
        + [pl.BlockSpec(memory_space=pltpu.VMEM)] * len(arrays),
        out_specs=jax.tree.map(lambda leaf: pl.BlockSpec(memory_space=pltpu.VMEM), out_shape),
        scratch_shapes=list(scratch),
        compiler_params=pltpu.CompilerParams(vmem_limit_bytes=32 * 2**20),
    )(*scalars, *arrays)


def per_device(kinematics, derivatives, masses, last_time, block_list, block_count):
    width = kinematics.shape[1]
    n_blk = lax.axis_size("blk")
    n_rep = lax.axis_size("rep")
    flat_list = block_list.reshape(-1)
    flat_count = block_count.reshape(-1)
    mass = masses.reshape(1, width)
    last = last_time.reshape(1, width)
    targets = run_kernel(
        functools.partial(targets_kernel, 0, n_blk, n_rep),
        [flat_list],
        [kinematics, derivatives, last],
        shape_of(n_blk, CAP * ROWS, BLOCK),
    )
    for step in range(STEPS):
        gathered = lax.all_to_all(targets, "blk", 0, 0, tiled=True)
        partial_forces = run_kernel(
            functools.partial(forces_kernel, step, n_blk, n_rep),
            [flat_count],
            [gathered.reshape(n_blk * CAP, ROWS, BLOCK), kinematics, derivatives, last, mass],
            shape_of(n_blk * CAP, ROWS, BLOCK),
            [
                pltpu.VMEM((6, width), F32),
                pltpu.VMEM((width, piece_rows), BF16),
                pltpu.VMEM((32, width), BF16),
            ],
        )
        partial_forces = partial_forces.reshape(n_blk, CAP * ROWS, BLOCK)
        spread = lax.all_to_all(partial_forces, "blk", 0, 0, tiled=True)
        mine = run_kernel(
            functools.partial(total_kernel, n_blk, n_rep),
            [],
            [spread],
            shape_of(n_rep, CAP * ROWS, BLOCK),
        )
        forces = lax.all_to_all(mine, "rep", 0, 0, tiled=True)
        out_shape = [shape_of(6, width), shape_of(6, width), shape_of(1, width)]
        if step + 1 < STEPS:
            out_shape.append(shape_of(n_blk, CAP * ROWS, BLOCK))
        kinematics, derivatives, last, *rest = run_kernel(
            functools.partial(update_kernel, step, n_blk, n_rep),
            [flat_list, flat_count],
            [forces.reshape(n_rep * CAP, ROWS, BLOCK), kinematics, derivatives, last],
            out_shape,
        )
        if rest:
            targets = rest[0]
    return (kinematics, derivatives)


def solution(mesh):
    return jax.shard_map(
        per_device,
        mesh=mesh,
        in_specs=(P(None, "blk"), P(None, "blk"), P("blk"), P("blk"), P(), P()),
        out_specs=(P(None, "blk"), P(None, "blk")),
        check_vma=False,
    )
```

```python
import functools

import jax
import jax.numpy as jnp
from jax import lax
from jax.experimental import pallas as pl
from jax.experimental.pallas import tpu as pltpu
from jax.sharding import PartitionSpec as P

BLOCK = 128
CAP = 2
STEPS = 2
ROWS = 8
F32 = jnp.float32
BF16 = jnp.bfloat16

step_length = 0.125
softening = 0.0025
grid_shift = 1.5 * 2.0**16
piece_rows = 128
chunk = 256
prep_width = 512


def predict(position, velocity, acceleration, jerk_old, interval):
    new_position = position + interval * (
        velocity + interval * (acceleration * 0.5 + interval * jerk_old / 6.0)
    )
    new_velocity = velocity + interval * (acceleration + interval * jerk_old * 0.5)
    return jnp.concatenate([new_position, new_velocity], axis=0)


def correct(predicted, old_deriv, forces, interval):
    change = old_deriv[:3] - forces[:3]
    second_term = -6.0 * change - interval * (4.0 * old_deriv[3:] + 2.0 * forces[3:])
    third_term = 12.0 * change + 6.0 * interval * (old_deriv[3:] + forces[3:])
    new_position = predicted[:3] + interval * interval * (second_term / 24.0 + third_term / 120.0)
    new_velocity = predicted[3:] + interval * (second_term / 6.0 + third_term / 24.0)
    return jnp.concatenate([new_position, new_velocity], axis=0)


def round_short(value):
    return value.astype(BF16).astype(F32)


def split_three(value):
    high = round_short(value)
    rest = value - high
    middle = round_short(rest)
    return high, middle, rest - middle


def stack_three(value):
    return jnp.concatenate(split_three(value), axis=0)


def star_pieces(stars):
    position, velocity = stars[0:3], stars[3:6]
    coarse = (position + grid_shift) - grid_shift
    coarse_a = round_short(coarse)
    coarse_b = coarse - coarse_a
    fine = position - coarse
    fine_a = round_short(fine)
    fine_b = round_short(fine - fine_a)
    fine = fine_a + fine_b
    square = jnp.sum(coarse * coarse, axis=0, keepdims=True)
    cross = jnp.sum(2.0 * coarse * fine + fine * fine, axis=0, keepdims=True)
    mixed = jnp.sum(position * velocity, axis=0, keepdims=True)
    return coarse_a, coarse_b, fine_a, fine_b, square, cross, mixed


def source_pieces(stars):
    ca, cb, fa, fb, square, cross, mixed = star_pieces(stars)
    va, vb, vc = split_three(stars[3:6])
    width = stars.shape[1]
    one = jnp.ones((3, width), F32)
    rows = [ca, ca, cb, cb, stack_three(square), one, jnp.zeros((6, width), F32)]
    rows += [ca, ca, cb, cb, fa, fa, fb, fb, fa, fa, stack_three(cross), one]
    rows += [va, va, va, vb, vb, vc, stack_three(mixed), one]
    rows += [jnp.zeros((piece_rows - 84, width), F32)]
    return jnp.concatenate(rows, axis=0)


def target_pieces(stars):
    ca, cb, fa, fb, square, cross, mixed = star_pieces(stars)
    va, vb, vc = split_three(stars[3:6])
    xa, xb, xc = split_three(stars[0:3])
    width = stars.shape[1]
    one = jnp.ones((3, width), F32)
    zero = jnp.zeros((3, width), F32)
    da, db = -2.0 * ca, -2.0 * cb
    ea, eb = -2.0 * fa, -2.0 * fb
    tail = jnp.zeros((piece_rows - 84, width), F32)
    radius = [da, db, da, db, one, stack_three(square), zero, zero]
    radius += [ea, eb, ea, eb, da, db, da, db, ea, eb, one, stack_three(cross + softening)]
    radius += [zero] * 8 + [tail]
    moving = [-va, -vb, -va, -vb, zero, zero, zero, zero]
    moving += [-vc, zero, zero, zero, -va, -vb, -va, zero, zero, zero, zero, zero]
    moving += [-xa, -xb, -xc, -xa, -xb, -xa, one, stack_three(mixed), tail]
    both = [jnp.concatenate(radius, axis=0), jnp.concatenate(moving, axis=0)]
    return jnp.concatenate(both, axis=1).astype(BF16)


def block_at(number):
    return pl.ds(pl.multiple_of(number * BLOCK, BLOCK), BLOCK)


def predicted_block(kin_ref, der_ref, last_ref, where, time_now):
    kin, der = kin_ref[:, where], der_ref[:, where]
    return predict(kin[:3], kin[3:], der[:3], der[3:], time_now - last_ref[:, where])


def list_place(step, blk, rep, slot, n_blk, n_rep):
    return ((step * n_blk + blk) * n_rep + rep) * CAP + slot


def write_targets(step, n_blk, n_rep, list_ref, kin_ref, der_ref, last_ref, out_ref):
    blk, rep = lax.axis_index("blk"), lax.axis_index("rep")
    rows = []
    for slot in range(CAP):
        number = list_ref[list_place(step, blk, rep, slot, n_blk, n_rep)]
        rows.append(predicted_block(kin_ref, der_ref, last_ref, block_at(number), step * step_length))
        rows.append(jnp.zeros((ROWS - 6, BLOCK), F32))
    mine = jnp.concatenate(rows, axis=0)
    for other in range(n_blk):
        out_ref[other] = mine


def targets_kernel(step, n_blk, n_rep, list_ref, kin_ref, der_ref, last_ref, out_ref):
    write_targets(step, n_blk, n_rep, list_ref, kin_ref, der_ref, last_ref, out_ref)


def forces_kernel(
    step, n_blk, n_rep, count_ref, target_ref, kin_ref, der_ref, last_ref, mass_ref,
    out_ref, pred_ref, piece_ref, moment_ref,
):
    rep = lax.axis_index("rep")
    width = kin_ref.shape[1]
    total = jnp.zeros((6, prep_width), F32)
    for part in range(width // prep_width):
        where = pl.ds(part * prep_width, prep_width)
        stars = predicted_block(kin_ref, der_ref, last_ref, where, step * step_length)
        pred_ref[:, where] = stars
        total = total + stars
    centre = jnp.sum(total, axis=1, keepdims=True) / width
    for part in range(width // prep_width):
        where = pl.ds(part * prep_width, prep_width)
        stars = pred_ref[:, where] - centre
        piece_ref[where, :] = source_pieces(stars).T.astype(BF16)
        scaled = mass_ref[:, where] / (width * n_blk)
        ones = jnp.ones((1, prep_width), F32)
        moments = jnp.concatenate([stars, ones, jnp.zeros_like(ones)], axis=0) * scaled
        moments = jnp.concatenate([stack_three(moments), jnp.zeros((8, prep_width), F32)], axis=0)
        moment_ref[:, where] = moments.astype(BF16)

    def one_slot(place, carry):
        blk = place // CAP
        slot = place % CAP
        active = slot < count_ref[(step * n_blk + blk) * n_rep + rep]

        @pl.when(active)
        def _():
            stars = target_ref[place][0:6] - centre
            against = target_pieces(stars)
            acc = jnp.zeros((32, 2 * BLOCK), F32)
            for part in range(width // chunk):
                where = pl.ds(part * chunk, chunk)
                both = jnp.dot(piece_ref[where, :], against, preferred_element_type=F32)
                inverse = lax.rsqrt(both[:, :BLOCK])
                inverse_sq = inverse * inverse
                weight = inverse * inverse_sq
                radial = weight * (inverse_sq * both[:, BLOCK:])
                pair = jnp.concatenate([weight, radial], axis=1)
                high = pair.astype(BF16)
                low = (pair - high.astype(F32)).astype(BF16)
                moments = moment_ref[:, where]
                acc = acc + jnp.dot(moments, high, preferred_element_type=F32)
                acc = acc + jnp.dot(moments, low, preferred_element_type=F32)
            acc = acc[0:8] + acc[8:16] + acc[16:24]
            by_weight, by_radial = acc[:, :BLOCK], acc[:, BLOCK:]
            sums = by_weight[0:6] - stars * by_weight[6:7]
            pull = by_radial[0:3] - stars[0:3] * by_radial[6:7]
            out_ref[place] = jnp.concatenate(
                [sums[0:3], sums[3:6] - 3.0 * pull, jnp.zeros((ROWS - 6, BLOCK), F32)], axis=0
            )

        @pl.when(jnp.logical_not(active))
        def _():
            out_ref[place] = jnp.zeros((ROWS, BLOCK), F32)

        return carry

    lax.fori_loop(0, n_blk * CAP, one_slot, 0)


def total_kernel(n_blk, n_rep, part_ref, out_ref):
    total = part_ref[0]
    for other in range(1, n_blk):
        total = total + part_ref[other]
    for other in range(n_rep):
        out_ref[other] = total


def update_kernel(
    step, n_blk, n_rep, list_ref, count_ref, force_ref, kin_ref, der_ref, last_ref,
    new_kin_ref, new_der_ref, new_last_ref, *next_refs,
):
    blk = lax.axis_index("blk")
    time_now = step * step_length
    new_kin_ref[...] = kin_ref[...]
    new_der_ref[...] = der_ref[...]
    new_last_ref[...] = last_ref[...]

    def one_slot(place, carry):
        rep = place // CAP
        slot = place % CAP

        @pl.when(slot < count_ref[(step * n_blk + blk) * n_rep + rep])
        def _():
            number = list_ref[list_place(step, blk, rep, slot, n_blk, n_rep)]
            where = block_at(number)
            predicted = predicted_block(kin_ref, der_ref, last_ref, where, time_now)
            forces = force_ref[place][0:6]
            interval = time_now - last_ref[:, where]
            new_kin_ref[:, where] = correct(predicted, der_ref[:, where], forces, interval)
            new_der_ref[:, where] = forces
            new_last_ref[:, where] = jnp.full((1, BLOCK), time_now, F32)

        return carry

    lax.fori_loop(0, n_rep * CAP, one_slot, 0)
    if next_refs:
        write_targets(
            step + 1, n_blk, n_rep, list_ref, new_kin_ref, new_der_ref, new_last_ref, next_refs[0]
        )


def lane_iota(rows):
    return lax.broadcasted_iota(jnp.int32, (rows, BLOCK), 1)


def active_rows(step, n_blk, n_rep, list_ref, count_ref):
    lanes = lane_iota(n_rep)
    diagonal = lax.broadcasted_iota(jnp.int32, (n_rep, n_rep), 0) == lax.broadcasted_iota(
        jnp.int32, (n_rep, n_rep), 1
    )
    rows = []
    for blk in range(n_blk):
        counted = count_ref[step, pl.ds(blk, 1), :].astype(F32)
        counted = jnp.sum(jnp.where(diagonal, counted, 0.0), axis=1, keepdims=True)
        listed = list_ref[step, blk]
        hit = jnp.zeros((n_rep, BLOCK), F32)
        for slot in range(CAP):
            same = (listed[:, slot : slot + 1] == lanes) & (counted > slot)
            hit = jnp.where(same, 1.0, hit)
        rows.append(jnp.max(hit, axis=0, keepdims=True))
    return jnp.concatenate(rows, axis=0)


def whole_sum(value):
    return jnp.sum(jnp.sum(value, axis=1, keepdims=True), axis=0, keepdims=True)


def share_blocks(n_blk, n_rep, list_ref, count_ref, table_ref):
    blk, rep = lax.axis_index("blk"), lax.axis_index("rep")
    first = active_rows(0, n_blk, n_rep, list_ref, count_ref)
    second = active_rows(1, n_blk, n_rep, list_ref, count_ref)
    in_both = first * second
    kinds = [in_both, first - in_both, second - in_both]
    earlier = lax.broadcasted_iota(jnp.int32, (BLOCK, BLOCK), 0) < lax.broadcasted_iota(
        jnp.int32, (BLOCK, BLOCK), 1
    )
    earlier = jnp.where(earlier, 1.0, 0.0).astype(BF16)
    above = lax.broadcasted_iota(jnp.int32, (n_blk, n_blk), 0) > lax.broadcasted_iota(
        jnp.int32, (n_blk, n_blk), 1
    )
    above = jnp.where(above, 1.0, 0.0).astype(BF16)
    own_row = lax.broadcasted_iota(jnp.int32, (n_blk, BLOCK), 0) == blk
    lanes = lane_iota(1)
    order = lanes * n_rep + rep
    start = jnp.zeros((1, 1), F32)
    fits = jnp.ones((1, 1), jnp.bool_)
    own_kind, own_place, own_number, finish, owner = [], [], [], [], []
    for kind in kinds:
        short = kind.astype(BF16)
        rank = jnp.dot(short, earlier, preferred_element_type=F32)
        before = jnp.dot(above, short, preferred_element_type=F32)
        before = jnp.sum(before, axis=1, keepdims=True) + start
        amount = jnp.sum(kind, axis=1, keepdims=True)
        fits = fits & (jnp.max(amount, axis=0, keepdims=True) <= n_rep)
        ends = (before + amount).astype(jnp.int32)
        owner.append(jnp.sum(jnp.where(ends <= order, 1, 0), axis=0, keepdims=True))
        place = jnp.sum(jnp.where(own_row, before + rank, 0.0), axis=0, keepdims=True)
        own_place.append(place.astype(jnp.int32))
        own_kind.append(jnp.sum(jnp.where(own_row, kind, 0.0), axis=0, keepdims=True) > 0.5)
        finish.append((jnp.max(before + amount, axis=0, keepdims=True)).astype(jnp.int32))
        if len(finish) == 1:
            start = jnp.sum(amount, axis=0, keepdims=True)
    both_end = finish[0]
    total = [jnp.maximum(finish[0], finish[1]), jnp.maximum(finish[0], finish[2])]
    for one in total:
        fits = fits & (one <= n_rep * n_rep)
    handler = [jnp.bitwise_and(place, n_rep - 1) for place in own_place]
    home = []
    for step in range(STEPS):
        code = jnp.where(own_kind[0], handler[0] * 2, -1)
        home.append(jnp.where(own_kind[1 + step], handler[1 + step] * 2 + 1, code))
    places = []
    for step in range(STEPS):
        is_both = order < both_end
        places.append(jnp.where(is_both, owner[0] * 4, owner[1 + step] * 4 + 2 + step))
    scalars = jnp.where(lanes == 0, jnp.where(fits, 1, 0), 0)
    for index in range(3):
        mine = own_kind[index] & (handler[index] == rep)
        number = jnp.max(jnp.where(mine, lanes, -1), axis=1, keepdims=True)
        scalars = jnp.where(lanes == 1 + index, number, scalars)
        spot = jnp.max(jnp.where(mine, own_place[index] // n_rep, 0), axis=1, keepdims=True)
        scalars = jnp.where(lanes == 4 + index, spot, scalars)
    for step in range(STEPS):
        amount = (total[step] - rep + n_rep - 1) // n_rep
        scalars = jnp.where(lanes == 7 + step, amount, scalars)
    amount = (both_end - rep + n_rep - 1) // n_rep
    scalars = jnp.where(lanes == 9, amount, scalars)
    rows = [home[0], home[1], scalars, places[0], places[1], jnp.zeros((3, BLOCK), jnp.int32)]
    table_ref[...] = jnp.concatenate(rows, axis=0)


def share_kernel(
    n_blk, n_rep, list_ref, count_ref, kin_ref, der_ref, last_ref,
    table_ref, out_ref, scalar_ref, semaphore,
):
    share_blocks(n_blk, n_rep, list_ref, count_ref, table_ref)
    copy = pltpu.make_async_copy(table_ref, scalar_ref, semaphore)
    copy.start()
    copy.wait()
    where = [block_at(jnp.maximum(scalar_ref[2, 1 + index], 0)) for index in range(3)]
    gap = jnp.zeros((2, BLOCK), F32)
    rows = [
        predicted_block(kin_ref, der_ref, last_ref, where[0], 0.0),
        0.0 - last_ref[:, where[0]],
        gap[0:1],
        der_ref[:, where[0]],
        gap,
        predicted_block(kin_ref, der_ref, last_ref, where[1], 0.0),
        gap,
        predicted_block(kin_ref, der_ref, last_ref, where[2], step_length),
        gap,
    ]
    mine = jnp.concatenate(rows, axis=0)
    for other in range(n_blk):
        out_ref[other] = mine


def write_pieces(n_blk, width, kin_ref, der_ref, last_ref, mass_ref, time_now, pred_ref, piece_ref, moment_ref):
    total = jnp.zeros((6, prep_width), F32)
    for part in range(width // prep_width):
        where = pl.ds(part * prep_width, prep_width)
        stars = predicted_block(kin_ref, der_ref, last_ref, where, time_now)
        pred_ref[:, where] = stars
        total = total + stars
    centre = jnp.sum(total, axis=1, keepdims=True) / width
    for part in range(width // prep_width):
        where = pl.ds(part * prep_width, prep_width)
        stars = pred_ref[:, where] - centre
        piece_ref[where, :] = source_pieces(stars).T.astype(BF16)
        scaled = mass_ref[:, where] / (width * n_blk)
        ones = jnp.ones((1, prep_width), F32)
        moments = jnp.concatenate([stars, ones, jnp.zeros_like(ones)], axis=0) * scaled
        moments = jnp.concatenate([stack_three(moments), jnp.zeros((8, prep_width), F32)], axis=0)
        moment_ref[:, where] = moments.astype(BF16)
    return centre


def block_forces(stars, piece_ref, moment_ref):
    against = target_pieces(stars)
    acc = jnp.zeros((32, 2 * BLOCK), F32)
    for part in range(piece_ref.shape[0] // chunk):
        where = pl.ds(part * chunk, chunk)
        both = jnp.dot(piece_ref[where, :], against, preferred_element_type=F32)
        inverse = lax.rsqrt(both[:, :BLOCK])
        inverse_sq = inverse * inverse
        weight = inverse * inverse_sq
        radial = weight * (inverse_sq * both[:, BLOCK:])
        pair = jnp.concatenate([weight, radial], axis=1)
        high = pair.astype(BF16)
        low = (pair - high.astype(F32)).astype(BF16)
        moments = moment_ref[:, where]
        acc = acc + jnp.dot(moments, high, preferred_element_type=F32)
        acc = acc + jnp.dot(moments, low, preferred_element_type=F32)
    acc = acc[0:8] + acc[8:16] + acc[16:24]
    by_weight, by_radial = acc[:, :BLOCK], acc[:, BLOCK:]
    sums = by_weight[0:6] - stars * by_weight[6:7]
    pull = by_radial[0:3] - stars[0:3] * by_radial[6:7]
    gap = jnp.zeros((ROWS - 6, BLOCK), F32)
    return jnp.concatenate([sums[0:3], sums[3:6] - 3.0 * pull, gap], axis=0)


def pieces_kernel(n_blk, kin_ref, der_ref, last_ref, mass_ref, piece_ref, moment_ref, centre_ref, pred_ref):
    width = kin_ref.shape[1]
    centre = write_pieces(
        n_blk, width, kin_ref, der_ref, last_ref, mass_ref, 0.0, pred_ref, piece_ref, moment_ref
    )
    centre_ref[...] = jnp.broadcast_to(centre, (6, BLOCK))


def first_forces_kernel(table_ref, target_ref, piece_ref, moment_ref, centre_ref, out_ref):
    out_ref[...] = jnp.zeros_like(out_ref)

    def one(index, carry):
        stars = target_ref[table_ref[3, index]][0:6] - centre_ref[...]
        out_ref[index] = block_forces(stars, piece_ref, moment_ref)
        return carry

    lax.fori_loop(0, table_ref[2, 7], one, 0)


def middle_kernel(n_rep, table_ref, force_ref, target_ref, share_ref, next_ref):
    own = jnp.concatenate([force_ref[table_ref[2, 4]], force_ref[table_ref[2, 5]]], axis=0)
    for other in range(n_rep):
        share_ref[other] = own

    def one(index, carry):
        place = table_ref[4, index]
        is_both = index < table_ref[2, 9]

        @pl.when(is_both)
        def _():
            head, deriv = target_ref[place], target_ref[place + 1][0:6]
            forces = force_ref[index][0:6]
            moved = correct(head[0:6], deriv, forces, head[6:7])
            ahead = predict(moved[:3], moved[3:], forces[:3], forces[3:], step_length)
            next_ref[index] = jnp.concatenate([ahead, head[6:8]], axis=0)

        @pl.when(jnp.logical_not(is_both))
        def _():
            next_ref[index] = target_ref[place]

        return carry

    lax.fori_loop(0, table_ref[2, 8], one, 0)


def move_shard(step, table_ref, force_ref, kin_ref, der_ref, last_ref, new_kin_ref, new_der_ref, new_last_ref):
    time_now = step * step_length
    new_kin_ref[...] = kin_ref[...]
    new_der_ref[...] = der_ref[...]
    if new_last_ref is not None:
        new_last_ref[...] = last_ref[...]

    def one(number, carry):
        code = table_ref[step, number]

        @pl.when(code >= 0)
        def _():
            where = block_at(number)
            predicted = predicted_block(kin_ref, der_ref, last_ref, where, time_now)
            forces = force_ref[code][0:6]
            interval = time_now - last_ref[:, where]
            new_kin_ref[:, where] = correct(predicted, der_ref[:, where], forces, interval)
            new_der_ref[:, where] = forces
            if new_last_ref is not None:
                new_last_ref[:, where] = jnp.full((1, BLOCK), time_now, F32)

        return carry

    lax.fori_loop(0, kin_ref.shape[1] // BLOCK, one, 0)


def second_forces_kernel(
    n_blk, table_ref, force_ref, target_ref, kin_ref, der_ref, last_ref, mass_ref,
    out_ref, new_kin_ref, new_der_ref, new_last_ref, pred_ref, piece_ref, moment_ref,
):
    width = kin_ref.shape[1]
    move_shard(0, table_ref, force_ref, kin_ref, der_ref, last_ref, new_kin_ref, new_der_ref, new_last_ref)
    centre = write_pieces(
        n_blk, width, new_kin_ref, new_der_ref, new_last_ref, mass_ref, step_length,
        pred_ref, piece_ref, moment_ref,
    )
    out_ref[...] = jnp.zeros_like(out_ref)

    def one(index, carry):
        stars = target_ref[index][0:6] - centre
        place = table_ref[4, index]
        out_ref[(place // 4) * 2 + place % 2] = block_forces(stars, piece_ref, moment_ref)
        return carry

    lax.fori_loop(0, table_ref[2, 8], one, 0)


def last_kernel(table_ref, force_ref, kin_ref, der_ref, last_ref, new_kin_ref, new_der_ref):
    move_shard(1, table_ref, force_ref, kin_ref, der_ref, last_ref, new_kin_ref, new_der_ref, None)


def shape_of(*sizes):
    return jax.ShapeDtypeStruct(sizes, F32)


def run_kernel(body, scalars, arrays, out_shape, scratch=(), cost=None):
    return pl.pallas_call(
        body,
        out_shape=out_shape,
        in_specs=[pl.BlockSpec(memory_space=pltpu.SMEM)] * len(scalars)
        + [pl.BlockSpec(memory_space=pltpu.VMEM)] * len(arrays),
        out_specs=jax.tree.map(lambda leaf: pl.BlockSpec(memory_space=pltpu.VMEM), out_shape),
        scratch_shapes=list(scratch),
        cost_estimate=cost,
        compiler_params=pltpu.CompilerParams(vmem_limit_bytes=32 * 2**20),
    )(*scalars, *arrays)


def plain_steps(kinematics, derivatives, mass, last, block_list, block_count):
    width = kinematics.shape[1]
    n_blk = lax.axis_size("blk")
    n_rep = lax.axis_size("rep")
    flat_list = block_list.reshape(-1)
    flat_count = block_count.reshape(-1)
    targets = run_kernel(
        functools.partial(targets_kernel, 0, n_blk, n_rep),
        [flat_list],
        [kinematics, derivatives, last],
        shape_of(n_blk, CAP * ROWS, BLOCK),
    )
    for step in range(STEPS):
        gathered = lax.all_to_all(targets, "blk", 0, 0, tiled=True)
        partial_forces = run_kernel(
            functools.partial(forces_kernel, step, n_blk, n_rep),
            [flat_count],
            [gathered.reshape(n_blk * CAP, ROWS, BLOCK), kinematics, derivatives, last, mass],
            shape_of(n_blk * CAP, ROWS, BLOCK),
            [
                pltpu.VMEM((6, width), F32),
                pltpu.VMEM((width, piece_rows), BF16),
                pltpu.VMEM((32, width), BF16),
            ],
        )
        partial_forces = partial_forces.reshape(n_blk, CAP * ROWS, BLOCK)
        spread = lax.all_to_all(partial_forces, "blk", 0, 0, tiled=True)
        mine = run_kernel(
            functools.partial(total_kernel, n_blk, n_rep),
            [],
            [spread],
            shape_of(n_rep, CAP * ROWS, BLOCK),
        )
        forces = lax.all_to_all(mine, "rep", 0, 0, tiled=True)
        out_shape = [shape_of(6, width), shape_of(6, width), shape_of(1, width)]
        if step + 1 < STEPS:
            out_shape.append(shape_of(n_blk, CAP * ROWS, BLOCK))
        kinematics, derivatives, last, *rest = run_kernel(
            functools.partial(update_kernel, step, n_blk, n_rep),
            [flat_list, flat_count],
            [forces.reshape(n_rep * CAP, ROWS, BLOCK), kinematics, derivatives, last],
            out_shape,
        )
        if rest:
            targets = rest[0]
    return (kinematics, derivatives)


def add_over_blk(value):
    n_blk = lax.axis_size("blk")

    def from_partner(distance):
        return lax.ppermute(value, "blk", [(i, i ^ distance) for i in range(n_blk)])

    value = value + from_partner(1)
    value = value + from_partner(2)
    return value + ((from_partner(4) + from_partner(12)) + from_partner(8))


def shared_steps(kinematics, derivatives, mass, last, table, gathered):
    width = kinematics.shape[1]
    n_blk = lax.axis_size("blk")
    n_rep = lax.axis_size("rep")
    piece_shapes = [
        jax.ShapeDtypeStruct((width, piece_rows), BF16),
        jax.ShapeDtypeStruct((32, width), BF16),
    ]
    piece_scratch = [pltpu.VMEM(leaf.shape, BF16) for leaf in piece_shapes]
    stars_scratch = pltpu.VMEM((6, width), F32)
    pieces, moments, centre = run_kernel(
        functools.partial(pieces_kernel, n_blk),
        [],
        [kinematics, derivatives, last, mass],
        piece_shapes + [shape_of(6, BLOCK)],
        [stars_scratch],
    )
    partial_forces = run_kernel(
        first_forces_kernel,
        [table],
        [gathered, pieces, moments, centre],
        shape_of(n_rep, ROWS, BLOCK),
    )
    forces = add_over_blk(partial_forces.reshape(n_rep * ROWS, BLOCK))
    shares, targets = run_kernel(
        functools.partial(middle_kernel, n_rep),
        [table],
        [forces.reshape(n_rep, ROWS, BLOCK), gathered],
        [shape_of(n_rep, 2 * ROWS, BLOCK), shape_of(n_rep, ROWS, BLOCK)],
    )
    shares = lax.all_to_all(shares, "rep", 0, 0, tiled=True)
    partial_forces, kinematics, derivatives, last = run_kernel(
        functools.partial(second_forces_kernel, n_blk),
        [table],
        [shares.reshape(n_rep * 2, ROWS, BLOCK), targets, kinematics, derivatives, last, mass],
        [shape_of(n_blk * 2, ROWS, BLOCK), shape_of(6, width), shape_of(6, width), shape_of(1, width)],
        [stars_scratch] + piece_scratch,
    )
    spread = lax.all_to_all(
        partial_forces.reshape(n_blk, 2 * ROWS, BLOCK), "blk", 0, 0, tiled=True
    )
    mine = run_kernel(
        functools.partial(total_kernel, n_blk, n_rep),
        [],
        [spread],
        shape_of(n_rep, 2 * ROWS, BLOCK),
    )
    shares = lax.all_to_all(mine, "rep", 0, 0, tiled=True)
    return run_kernel(
        last_kernel,
        [table],
        [shares.reshape(n_rep * 2, ROWS, BLOCK), kinematics, derivatives, last],
        [shape_of(6, width), shape_of(6, width)],
    )


def per_device(kinematics, derivatives, masses, last_time, block_list, block_count):
    width = kinematics.shape[1]
    n_blk = lax.axis_size("blk")
    n_rep = lax.axis_size("rep")
    mass = masses.reshape(1, width)
    last = last_time.reshape(1, width)
    table, targets = run_kernel(
        functools.partial(share_kernel, n_blk, n_rep),
        [],
        [block_list, block_count, kinematics, derivatives, last],
        [jax.ShapeDtypeStruct((8, BLOCK), jnp.int32), shape_of(n_blk, 4 * ROWS, BLOCK)],
        [pltpu.SMEM((8, BLOCK), jnp.int32), pltpu.SemaphoreType.DMA],
    )
    gathered = lax.all_to_all(targets, "blk", 0, 0, tiled=True)
    gathered = gathered.reshape(n_blk * 4, ROWS, BLOCK)
    return tuple(
        lax.cond(
            table[2, 0] > 0,
            lambda: tuple(shared_steps(kinematics, derivatives, mass, last, table, gathered)),
            lambda: tuple(
                plain_steps(kinematics, derivatives, mass, last, block_list, block_count)
            ),
        )
    )


def solution(mesh):
    return jax.shard_map(
        per_device,
        mesh=mesh,
        in_specs=(P(None, "blk"), P(None, "blk"), P("blk"), P("blk"), P(), P()),
        out_specs=(P(None, "blk"), P(None, "blk")),
        check_vma=False,
    )
```

```python
import functools

import jax
import jax.numpy as jnp
from jax import lax
from jax.experimental import pallas as pl
from jax.experimental.pallas import tpu as pltpu
from jax.sharding import PartitionSpec as P

BLOCK = 128
CAP = 2
STEPS = 2
ROWS = 8
F32 = jnp.float32
BF16 = jnp.bfloat16

step_length = 0.125
softening = 0.0025
grid_shift = 1.5 * 2.0**16
piece_rows = 128
chunk = 256
ahead_chunk = 1024
prep_width = 512
first_slots = 12


def predict(position, velocity, acceleration, jerk_old, interval):
    new_position = position + interval * (
        velocity + interval * (acceleration * 0.5 + interval * jerk_old / 6.0)
    )
    new_velocity = velocity + interval * (acceleration + interval * jerk_old * 0.5)
    return jnp.concatenate([new_position, new_velocity], axis=0)


def correct(predicted, old_deriv, forces, interval):
    change = old_deriv[:3] - forces[:3]
    second_term = -6.0 * change - interval * (4.0 * old_deriv[3:] + 2.0 * forces[3:])
    third_term = 12.0 * change + 6.0 * interval * (old_deriv[3:] + forces[3:])
    new_position = predicted[:3] + interval * interval * (second_term / 24.0 + third_term / 120.0)
    new_velocity = predicted[3:] + interval * (second_term / 6.0 + third_term / 24.0)
    return jnp.concatenate([new_position, new_velocity], axis=0)


def round_short(value):
    return value.astype(BF16).astype(F32)


def split_three(value):
    high = round_short(value)
    rest = value - high
    middle = round_short(rest)
    return high, middle, rest - middle


def stack_three(value):
    return jnp.concatenate(split_three(value), axis=0)


def star_pieces(stars):
    position, velocity = stars[0:3], stars[3:6]
    coarse = (position + grid_shift) - grid_shift
    coarse_a = round_short(coarse)
    coarse_b = coarse - coarse_a
    fine = position - coarse
    fine_a = round_short(fine)
    fine_b = round_short(fine - fine_a)
    fine = fine_a + fine_b
    square = jnp.sum(coarse * coarse, axis=0, keepdims=True)
    cross = jnp.sum(2.0 * coarse * fine + fine * fine, axis=0, keepdims=True)
    mixed = jnp.sum(position * velocity, axis=0, keepdims=True)
    return coarse_a, coarse_b, fine_a, fine_b, square, cross, mixed


def source_pieces(stars):
    ca, cb, fa, fb, square, cross, mixed = star_pieces(stars)
    va, vb, vc = split_three(stars[3:6])
    width = stars.shape[1]
    one = jnp.ones((3, width), F32)
    rows = [ca, ca, cb, cb, stack_three(square), one, jnp.zeros((6, width), F32)]
    rows += [ca, ca, cb, cb, fa, fa, fb, fb, fa, fa, stack_three(cross), one]
    rows += [va, va, va, vb, vb, vc, stack_three(mixed), one]
    rows += [jnp.zeros((piece_rows - 84, width), F32)]
    return jnp.concatenate(rows, axis=0)


def target_pieces(stars):
    ca, cb, fa, fb, square, cross, mixed = star_pieces(stars)
    va, vb, vc = split_three(stars[3:6])
    xa, xb, xc = split_three(stars[0:3])
    width = stars.shape[1]
    one = jnp.ones((3, width), F32)
    zero = jnp.zeros((3, width), F32)
    da, db = -2.0 * ca, -2.0 * cb
    ea, eb = -2.0 * fa, -2.0 * fb
    tail = jnp.zeros((piece_rows - 84, width), F32)
    radius = [da, db, da, db, one, stack_three(square), zero, zero]
    radius += [ea, eb, ea, eb, da, db, da, db, ea, eb, one, stack_three(cross + softening)]
    radius += [zero] * 8 + [tail]
    moving = [-va, -vb, -va, -vb, zero, zero, zero, zero]
    moving += [-vc, zero, zero, zero, -va, -vb, -va, zero, zero, zero, zero, zero]
    moving += [-xa, -xb, -xc, -xa, -xb, -xa, one, stack_three(mixed), tail]
    both = [jnp.concatenate(radius, axis=0), jnp.concatenate(moving, axis=0)]
    return jnp.concatenate(both, axis=1).astype(BF16)


def block_at(number):
    return pl.ds(pl.multiple_of(number * BLOCK, BLOCK), BLOCK)


def predicted_block(kin_ref, der_ref, last_ref, where, time_now):
    kin, der = kin_ref[:, where], der_ref[:, where]
    return predict(kin[:3], kin[3:], der[:3], der[3:], time_now - last_ref[:, where])


def list_place(step, blk, rep, slot, n_blk, n_rep):
    return ((step * n_blk + blk) * n_rep + rep) * CAP + slot


def write_targets(step, n_blk, n_rep, list_ref, kin_ref, der_ref, last_ref, out_ref):
    blk, rep = lax.axis_index("blk"), lax.axis_index("rep")
    rows = []
    for slot in range(CAP):
        number = list_ref[list_place(step, blk, rep, slot, n_blk, n_rep)]
        rows.append(predicted_block(kin_ref, der_ref, last_ref, block_at(number), step * step_length))
        rows.append(jnp.zeros((ROWS - 6, BLOCK), F32))
    mine = jnp.concatenate(rows, axis=0)
    for other in range(n_blk):
        out_ref[other] = mine


def targets_kernel(step, n_blk, n_rep, list_ref, kin_ref, der_ref, last_ref, out_ref):
    write_targets(step, n_blk, n_rep, list_ref, kin_ref, der_ref, last_ref, out_ref)


def forces_kernel(
    step, n_blk, n_rep, count_ref, target_ref, kin_ref, der_ref, last_ref, mass_ref,
    out_ref, pred_ref, piece_ref, moment_ref,
):
    rep = lax.axis_index("rep")
    width = kin_ref.shape[1]
    total = jnp.zeros((6, prep_width), F32)
    for part in range(width // prep_width):
        where = pl.ds(part * prep_width, prep_width)
        stars = predicted_block(kin_ref, der_ref, last_ref, where, step * step_length)
        pred_ref[:, where] = stars
        total = total + stars
    centre = jnp.sum(total, axis=1, keepdims=True) / width
    for part in range(width // prep_width):
        where = pl.ds(part * prep_width, prep_width)
        stars = pred_ref[:, where] - centre
        piece_ref[where, :] = source_pieces(stars).T.astype(BF16)
        scaled = mass_ref[:, where] / (width * n_blk)
        ones = jnp.ones((1, prep_width), F32)
        moments = jnp.concatenate([stars, ones, jnp.zeros_like(ones)], axis=0) * scaled
        moments = jnp.concatenate([stack_three(moments), jnp.zeros((8, prep_width), F32)], axis=0)
        moment_ref[:, where] = moments.astype(BF16)

    def one_slot(place, carry):
        blk = place // CAP
        slot = place % CAP
        active = slot < count_ref[(step * n_blk + blk) * n_rep + rep]

        @pl.when(active)
        def _():
            stars = target_ref[place][0:6] - centre
            against = target_pieces(stars)
            acc = jnp.zeros((32, 2 * BLOCK), F32)
            for part in range(width // chunk):
                where = pl.ds(part * chunk, chunk)
                both = jnp.dot(piece_ref[where, :], against, preferred_element_type=F32)
                inverse = lax.rsqrt(both[:, :BLOCK])
                inverse_sq = inverse * inverse
                weight = inverse * inverse_sq
                radial = weight * (inverse_sq * both[:, BLOCK:])
                pair = jnp.concatenate([weight, radial], axis=1)
                high = pair.astype(BF16)
                low = (pair - high.astype(F32)).astype(BF16)
                moments = moment_ref[:, where]
                acc = acc + jnp.dot(moments, high, preferred_element_type=F32)
                acc = acc + jnp.dot(moments, low, preferred_element_type=F32)
            acc = acc[0:8] + acc[8:16] + acc[16:24]
            by_weight, by_radial = acc[:, :BLOCK], acc[:, BLOCK:]
            sums = by_weight[0:6] - stars * by_weight[6:7]
            pull = by_radial[0:3] - stars[0:3] * by_radial[6:7]
            out_ref[place] = jnp.concatenate(
                [sums[0:3], sums[3:6] - 3.0 * pull, jnp.zeros((ROWS - 6, BLOCK), F32)], axis=0
            )

        @pl.when(jnp.logical_not(active))
        def _():
            out_ref[place] = jnp.zeros((ROWS, BLOCK), F32)

        return carry

    lax.fori_loop(0, n_blk * CAP, one_slot, 0)


def total_kernel(n_blk, n_rep, part_ref, out_ref):
    total = part_ref[0]
    for other in range(1, n_blk):
        total = total + part_ref[other]
    for other in range(n_rep):
        out_ref[other] = total


def update_kernel(
    step, n_blk, n_rep, list_ref, count_ref, force_ref, kin_ref, der_ref, last_ref,
    new_kin_ref, new_der_ref, new_last_ref, *next_refs,
):
    blk = lax.axis_index("blk")
    time_now = step * step_length
    new_kin_ref[...] = kin_ref[...]
    new_der_ref[...] = der_ref[...]
    new_last_ref[...] = last_ref[...]

    def one_slot(place, carry):
        rep = place // CAP
        slot = place % CAP

        @pl.when(slot < count_ref[(step * n_blk + blk) * n_rep + rep])
        def _():
            number = list_ref[list_place(step, blk, rep, slot, n_blk, n_rep)]
            where = block_at(number)
            predicted = predicted_block(kin_ref, der_ref, last_ref, where, time_now)
            forces = force_ref[place][0:6]
            interval = time_now - last_ref[:, where]
            new_kin_ref[:, where] = correct(predicted, der_ref[:, where], forces, interval)
            new_der_ref[:, where] = forces
            new_last_ref[:, where] = jnp.full((1, BLOCK), time_now, F32)

        return carry

    lax.fori_loop(0, n_rep * CAP, one_slot, 0)
    if next_refs:
        write_targets(
            step + 1, n_blk, n_rep, list_ref, new_kin_ref, new_der_ref, new_last_ref, next_refs[0]
        )


def lane_iota(rows):
    return lax.broadcasted_iota(jnp.int32, (rows, BLOCK), 1)


def active_rows(n_blk, n_rep, list_ref, count_ref):
    per_row = BLOCK // n_rep
    parts = BLOCK * n_rep // BLOCK // 4
    lanes = lane_iota(n_blk)
    steps = []
    for step in range(STEPS):
        counted = count_ref[step]
        tiled = []
        for slot in range(CAP):
            listed = jnp.where(counted > slot, list_ref[step, :, slot, :], -1)
            tiled.append(jnp.concatenate([listed] * per_row, axis=1))
        hits = []
        for part in range(parts):
            number = lanes // n_rep + part * per_row
            hit = (tiled[0] == number) | (tiled[1] == number)
            hits.append(jnp.where(hit, 1.0, 0.0))
        steps.append(jnp.concatenate(hits, axis=1))
    hits = jnp.concatenate(steps, axis=0).astype(BF16)
    width = parts * BLOCK
    rows = lax.broadcasted_iota(jnp.int32, (width, BLOCK), 0) // n_rep
    spread = jnp.where(rows == lax.broadcasted_iota(jnp.int32, (width, BLOCK), 1), 1.0, 0.0)
    return jnp.dot(hits, spread.astype(BF16), preferred_element_type=F32)


def share_blocks(n_blk, n_rep, list_ref, count_ref, table_ref):
    blk, rep = lax.axis_index("blk"), lax.axis_index("rep")
    flags = active_rows(n_blk, n_rep, list_ref, count_ref)
    first, second = flags[:n_blk], flags[n_blk:]
    in_both = first * second
    kinds = [in_both, first - in_both, second - in_both]
    earlier = lax.broadcasted_iota(jnp.int32, (BLOCK, BLOCK), 0) < lax.broadcasted_iota(
        jnp.int32, (BLOCK, BLOCK), 1
    )
    earlier = jnp.where(earlier, 1.0, 0.0).astype(BF16)
    above = lax.broadcasted_iota(jnp.int32, (n_blk, n_blk), 0) > lax.broadcasted_iota(
        jnp.int32, (n_blk, n_blk), 1
    )
    above = jnp.where(above, 1.0, 0.0).astype(BF16)
    own_row = lax.broadcasted_iota(jnp.int32, (n_blk, BLOCK), 0) == blk
    lanes = lane_iota(1)
    order = lanes * n_rep + rep
    start = jnp.zeros((1, 1), F32)
    fits = jnp.ones((1, 1), jnp.bool_)
    own_kind, own_place, own_number, finish, owner = [], [], [], [], []
    for kind in kinds:
        short = kind.astype(BF16)
        rank = jnp.dot(short, earlier, preferred_element_type=F32)
        before = jnp.dot(above, short, preferred_element_type=F32)
        before = jnp.sum(before, axis=1, keepdims=True) + start
        amount = jnp.sum(kind, axis=1, keepdims=True)
        fits = fits & (jnp.max(amount, axis=0, keepdims=True) <= n_rep)
        ends = (before + amount).astype(jnp.int32)
        owner.append(jnp.sum(jnp.where(ends <= order, 1, 0), axis=0, keepdims=True))
        place = jnp.sum(jnp.where(own_row, before + rank, 0.0), axis=0, keepdims=True)
        own_place.append(place.astype(jnp.int32))
        own_kind.append(jnp.sum(jnp.where(own_row, kind, 0.0), axis=0, keepdims=True) > 0.5)
        finish.append((jnp.max(before + amount, axis=0, keepdims=True)).astype(jnp.int32))
        if len(finish) == 1:
            start = jnp.sum(amount, axis=0, keepdims=True)
    both_end = finish[0]
    total = [jnp.maximum(finish[0], finish[1]), jnp.maximum(finish[0], finish[2])]
    fits = fits & (total[0] <= n_rep * first_slots) & (total[1] <= n_rep * n_rep)
    handler = [jnp.bitwise_and(place, n_rep - 1) for place in own_place]
    home = []
    for step in range(STEPS):
        code = jnp.where(own_kind[0], handler[0] * 2, -1)
        home.append(jnp.where(own_kind[1 + step], handler[1 + step] * 2 + 1, code))
    places = []
    for step in range(STEPS):
        is_both = order < both_end
        places.append(jnp.where(is_both, owner[0] * 4, owner[1 + step] * 4 + 2 + step))
    scalars = jnp.where(lanes == 0, jnp.where(fits, 1, 0), 0)
    numbers = []
    for index in range(3):
        mine = own_kind[index] & (handler[index] == rep)
        numbers.append(jnp.sum(jnp.where(mine, lanes.astype(F32), 0.0)).astype(jnp.int32))
        spot = jnp.max(jnp.where(mine, own_place[index] // n_rep, 0), axis=1, keepdims=True)
        scalars = jnp.where(lanes == 4 + index, spot, scalars)
    for step in range(STEPS):
        amount = (total[step] - rep + n_rep - 1) // n_rep
        scalars = jnp.where(lanes == 7 + step, amount, scalars)
    amount = (both_end - rep + n_rep - 1) // n_rep
    scalars = jnp.where(lanes == 9, amount, scalars)
    rows = [home[0], home[1], scalars, places[0], places[1], jnp.zeros((3, BLOCK), jnp.int32)]
    table_ref[...] = jnp.concatenate(rows, axis=0)
    return numbers


def share_kernel(n_blk, n_rep, list_ref, count_ref, kin_ref, der_ref, last_ref, table_ref, out_ref):
    numbers = share_blocks(n_blk, n_rep, list_ref, count_ref, table_ref)
    where = [block_at(number) for number in numbers]
    gap = jnp.zeros((2, BLOCK), F32)
    rows = [
        predicted_block(kin_ref, der_ref, last_ref, where[0], 0.0),
        0.0 - last_ref[:, where[0]],
        gap[0:1],
        der_ref[:, where[0]],
        gap,
        predicted_block(kin_ref, der_ref, last_ref, where[1], 0.0),
        gap,
        predicted_block(kin_ref, der_ref, last_ref, where[2], step_length),
        gap,
    ]
    mine = jnp.concatenate(rows, axis=0)
    for other in range(n_blk):
        out_ref[other] = mine


def write_pieces(n_blk, width, kin_ref, der_ref, last_ref, mass_ref, time_now, pred_ref, piece_ref, moment_ref):
    total = jnp.zeros((6, prep_width), F32)
    for part in range(width // prep_width):
        where = pl.ds(part * prep_width, prep_width)
        stars = predicted_block(kin_ref, der_ref, last_ref, where, time_now)
        pred_ref[:, where] = stars
        total = total + stars
    centre = jnp.sum(total, axis=1, keepdims=True) / width
    for part in range(width // prep_width):
        where = pl.ds(part * prep_width, prep_width)
        stars = pred_ref[:, where] - centre
        piece_ref[where, :] = source_pieces(stars).T.astype(BF16)
        scaled = mass_ref[:, where] / (width * n_blk)
        ones = jnp.ones((1, prep_width), F32)
        moments = jnp.concatenate([stars, ones, jnp.zeros_like(ones)], axis=0) * scaled
        moments = jnp.concatenate([stack_three(moments), jnp.zeros((8, prep_width), F32)], axis=0)
        moment_ref[:, where] = moments.astype(BF16)
    return centre


def block_forces(stars, piece_ref, moment_ref):
    against = target_pieces(stars)
    by_weight = jnp.zeros((32, 2 * BLOCK), F32)
    by_radial = jnp.zeros((32, 2 * BLOCK), F32)
    parts = piece_ref.shape[0] // ahead_chunk

    def meet(part):
        where = pl.ds(part * ahead_chunk, ahead_chunk)
        return jnp.dot(piece_ref[where, :], against, preferred_element_type=F32)

    def halves(value):
        high = value.astype(BF16)
        low = (value - high.astype(F32)).astype(BF16)
        return jnp.concatenate([high, low], axis=1)

    both = meet(0)
    for part in range(parts):
        ahead = meet(part + 1) if part + 1 < parts else None
        inverse = lax.rsqrt(both[:, :BLOCK])
        inverse_sq = inverse * inverse
        weight = inverse * inverse_sq
        radial = weight * (inverse_sq * both[:, BLOCK:])
        moments = moment_ref[:, pl.ds(part * ahead_chunk, ahead_chunk)]
        by_weight = by_weight + jnp.dot(moments, halves(weight), preferred_element_type=F32)
        by_radial = by_radial + jnp.dot(moments, halves(radial), preferred_element_type=F32)
        both = ahead

    def gather_up(value):
        value = value[0:8] + value[8:16] + value[16:24]
        return value[:, :BLOCK] + value[:, BLOCK:]

    by_weight, by_radial = gather_up(by_weight), gather_up(by_radial)
    sums = by_weight[0:6] - stars * by_weight[6:7]
    pull = by_radial[0:3] - stars[0:3] * by_radial[6:7]
    gap = jnp.zeros((ROWS - 6, BLOCK), F32)
    return jnp.concatenate([sums[0:3], sums[3:6] - 3.0 * pull, gap], axis=0)


def pieces_kernel(n_blk, kin_ref, der_ref, last_ref, mass_ref, piece_ref, moment_ref, centre_ref, pred_ref):
    width = kin_ref.shape[1]
    centre = write_pieces(
        n_blk, width, kin_ref, der_ref, last_ref, mass_ref, 0.0, pred_ref, piece_ref, moment_ref
    )
    centre_ref[...] = jnp.broadcast_to(centre, (6, BLOCK))


def first_forces_kernel(table_ref, target_ref, piece_ref, moment_ref, centre_ref, out_ref):
    out_ref[...] = jnp.zeros_like(out_ref)

    def one(index, carry):
        stars = target_ref[table_ref[3, index]][0:6] - centre_ref[...]
        out_ref[index] = block_forces(stars, piece_ref, moment_ref)
        return carry

    lax.fori_loop(0, table_ref[2, 7], one, 0)


def flag_rows():
    rows = lax.broadcasted_iota(jnp.int32, (CAP * ROWS, BLOCK), 0)
    return jnp.bitwise_and(rows, ROWS - 1) == 6


def flagged_total_kernel(n_blk, n_rep, part_ref, out_ref):
    total = part_ref[0]
    for other in range(1, n_blk):
        total = total + part_ref[other]
    total = jnp.where(flag_rows(), 1.0, total)
    for other in range(n_rep):
        out_ref[other] = total


def middle_kernel(n_rep, table_ref, force_ref, target_ref, share_ref, next_ref):
    own = jnp.concatenate([force_ref[table_ref[2, 4]], force_ref[table_ref[2, 5]]], axis=0)
    own = jnp.where(flag_rows(), 1.0, own)
    for other in range(n_rep):
        share_ref[other] = own

    def one(index, carry):
        place = table_ref[4, index]
        is_both = index < table_ref[2, 9]

        @pl.when(is_both)
        def _():
            head, deriv = target_ref[place], target_ref[place + 1][0:6]
            forces = force_ref[index][0:6]
            moved = correct(head[0:6], deriv, forces, head[6:7])
            ahead = predict(moved[:3], moved[3:], forces[:3], forces[3:], step_length)
            next_ref[index] = jnp.concatenate([ahead, head[6:8]], axis=0)

        @pl.when(jnp.logical_not(is_both))
        def _():
            next_ref[index] = target_ref[place]

        return carry

    lax.fori_loop(0, table_ref[2, 8], one, 0)


def place_forces(step, table_ref, force_ref, placed_ref):
    for number in range(placed_ref.shape[1] // BLOCK):
        code = table_ref[step, number]
        tile = force_ref[jnp.maximum(code, 0)]
        tile = tile * jnp.where(code >= 0, 1.0, 0.0)
        placed_ref[:, pl.ds(number * BLOCK, BLOCK)] = tile


def moved_part(step, where, placed_ref, kin_ref, der_ref, last_ref):
    time_now = step * step_length
    placed = placed_ref[:, where]
    forces, moved = placed[0:6], placed[6:7] > 0.5
    kin, der, last = kin_ref[:, where], der_ref[:, where], last_ref[:, where]
    interval = time_now - last
    predicted = predict(kin[:3], kin[3:], der[:3], der[3:], interval)
    corrected = correct(predicted, der, forces, interval)
    return (
        jnp.where(moved, corrected, kin),
        jnp.where(moved, forces, der),
        jnp.where(moved, time_now, last),
    )


def second_forces_kernel(
    n_blk, table_ref, force_ref, target_ref, kin_ref, der_ref, last_ref, mass_ref,
    out_ref, new_kin_ref, new_der_ref, new_last_ref, placed_ref, pred_ref, piece_ref, moment_ref,
):
    width = kin_ref.shape[1]
    place_forces(0, table_ref, force_ref, placed_ref)
    for part in range(width // prep_width):
        where = pl.ds(part * prep_width, prep_width)
        kin, der, last = moved_part(0, where, placed_ref, kin_ref, der_ref, last_ref)
        new_kin_ref[:, where] = kin
        new_der_ref[:, where] = der
        new_last_ref[:, where] = last
    centre = write_pieces(
        n_blk, width, new_kin_ref, new_der_ref, new_last_ref, mass_ref, step_length,
        pred_ref, piece_ref, moment_ref,
    )
    out_ref[...] = jnp.zeros_like(out_ref)

    def one(index, carry):
        stars = target_ref[index][0:6] - centre
        place = table_ref[4, index]
        out_ref[(place // 4) * 2 + place % 2] = block_forces(stars, piece_ref, moment_ref)
        return carry

    lax.fori_loop(0, table_ref[2, 8], one, 0)


def last_kernel(
    table_ref, force_ref, kin_ref, der_ref, last_ref, new_kin_ref, new_der_ref, placed_ref
):
    place_forces(1, table_ref, force_ref, placed_ref)
    for part in range(kin_ref.shape[1] // prep_width):
        where = pl.ds(part * prep_width, prep_width)
        kin, der, last = moved_part(1, where, placed_ref, kin_ref, der_ref, last_ref)
        new_kin_ref[:, where] = kin
        new_der_ref[:, where] = der


def shape_of(*sizes):
    return jax.ShapeDtypeStruct(sizes, F32)


def run_kernel(body, scalars, arrays, out_shape, scratch=(), cost=None):
    return pl.pallas_call(
        body,
        out_shape=out_shape,
        in_specs=[pl.BlockSpec(memory_space=pltpu.SMEM)] * len(scalars)
        + [pl.BlockSpec(memory_space=pltpu.VMEM)] * len(arrays),
        out_specs=jax.tree.map(lambda leaf: pl.BlockSpec(memory_space=pltpu.VMEM), out_shape),
        scratch_shapes=list(scratch),
        cost_estimate=cost,
        compiler_params=pltpu.CompilerParams(vmem_limit_bytes=32 * 2**20),
    )(*scalars, *arrays)


def plain_steps(kinematics, derivatives, mass, last, block_list, block_count):
    width = kinematics.shape[1]
    n_blk = lax.axis_size("blk")
    n_rep = lax.axis_size("rep")
    flat_list = block_list.reshape(-1)
    flat_count = block_count.reshape(-1)
    targets = run_kernel(
        functools.partial(targets_kernel, 0, n_blk, n_rep),
        [flat_list],
        [kinematics, derivatives, last],
        shape_of(n_blk, CAP * ROWS, BLOCK),
    )
    for step in range(STEPS):
        gathered = lax.all_to_all(targets, "blk", 0, 0, tiled=True)
        partial_forces = run_kernel(
            functools.partial(forces_kernel, step, n_blk, n_rep),
            [flat_count],
            [gathered.reshape(n_blk * CAP, ROWS, BLOCK), kinematics, derivatives, last, mass],
            shape_of(n_blk * CAP, ROWS, BLOCK),
            [
                pltpu.VMEM((6, width), F32),
                pltpu.VMEM((width, piece_rows), BF16),
                pltpu.VMEM((32, width), BF16),
            ],
        )
        partial_forces = partial_forces.reshape(n_blk, CAP * ROWS, BLOCK)
        spread = lax.all_to_all(partial_forces, "blk", 0, 0, tiled=True)
        mine = run_kernel(
            functools.partial(total_kernel, n_blk, n_rep),
            [],
            [spread],
            shape_of(n_rep, CAP * ROWS, BLOCK),
        )
        forces = lax.all_to_all(mine, "rep", 0, 0, tiled=True)
        out_shape = [shape_of(6, width), shape_of(6, width), shape_of(1, width)]
        if step + 1 < STEPS:
            out_shape.append(shape_of(n_blk, CAP * ROWS, BLOCK))
        kinematics, derivatives, last, *rest = run_kernel(
            functools.partial(update_kernel, step, n_blk, n_rep),
            [flat_list, flat_count],
            [forces.reshape(n_rep * CAP, ROWS, BLOCK), kinematics, derivatives, last],
            out_shape,
        )
        if rest:
            targets = rest[0]
    return (kinematics, derivatives)


def add_over_blk(value):
    n_blk = lax.axis_size("blk")

    def from_partner(distance):
        return lax.ppermute(value, "blk", [(i, i ^ distance) for i in range(n_blk)])

    value = value + from_partner(1)
    value = value + from_partner(2)
    return value + ((from_partner(4) + from_partner(12)) + from_partner(8))


def shared_steps(kinematics, derivatives, mass, last, table, gathered, pieces, moments, centre):
    width = kinematics.shape[1]
    n_blk = lax.axis_size("blk")
    n_rep = lax.axis_size("rep")
    piece_scratch = [pltpu.VMEM((width, piece_rows), BF16), pltpu.VMEM((32, width), BF16)]
    stars_scratch = pltpu.VMEM((6, width), F32)
    partial_forces = run_kernel(
        first_forces_kernel,
        [table],
        [gathered, pieces, moments, centre],
        shape_of(first_slots, ROWS, BLOCK),
    )
    forces = add_over_blk(partial_forces.reshape(first_slots * ROWS, BLOCK))
    shares, targets = run_kernel(
        functools.partial(middle_kernel, n_rep),
        [table],
        [forces.reshape(first_slots, ROWS, BLOCK), gathered],
        [shape_of(n_rep, 2 * ROWS, BLOCK), shape_of(n_rep, ROWS, BLOCK)],
    )
    shares = lax.all_to_all(shares, "rep", 0, 0, tiled=True)
    partial_forces, kinematics, derivatives, last = run_kernel(
        functools.partial(second_forces_kernel, n_blk),
        [table],
        [shares.reshape(n_rep * 2, ROWS, BLOCK), targets, kinematics, derivatives, last, mass],
        [shape_of(n_blk * 2, ROWS, BLOCK), shape_of(6, width), shape_of(6, width), shape_of(1, width)],
        [pltpu.VMEM((ROWS, width), F32), stars_scratch] + piece_scratch,
    )
    spread = lax.all_to_all(
        partial_forces.reshape(n_blk, 2 * ROWS, BLOCK), "blk", 0, 0, tiled=True
    )
    mine = run_kernel(
        functools.partial(flagged_total_kernel, n_blk, n_rep),
        [],
        [spread],
        shape_of(n_rep, 2 * ROWS, BLOCK),
    )
    shares = lax.all_to_all(mine, "rep", 0, 0, tiled=True)
    return run_kernel(
        last_kernel,
        [table],
        [shares.reshape(n_rep * 2, ROWS, BLOCK), kinematics, derivatives, last],
        [shape_of(6, width), shape_of(6, width)],
        [pltpu.VMEM((ROWS, width), F32)],
    )


def per_device(kinematics, derivatives, masses, last_time, block_list, block_count):
    width = kinematics.shape[1]
    n_blk = lax.axis_size("blk")
    n_rep = lax.axis_size("rep")
    mass = masses.reshape(1, width)
    last = last_time.reshape(1, width)
    table, targets = run_kernel(
        functools.partial(share_kernel, n_blk, n_rep),
        [],
        [block_list.transpose(0, 1, 3, 2), block_count, kinematics, derivatives, last],
        [jax.ShapeDtypeStruct((8, BLOCK), jnp.int32), shape_of(n_blk, 4 * ROWS, BLOCK)],
    )
    gathered = lax.all_to_all(targets, "blk", 0, 0, tiled=True)
    gathered = gathered.reshape(n_blk * 4, ROWS, BLOCK)
    pieces, moments, centre = run_kernel(
        functools.partial(pieces_kernel, n_blk),
        [],
        [kinematics, derivatives, last, mass],
        [
            jax.ShapeDtypeStruct((width, piece_rows), BF16),
            jax.ShapeDtypeStruct((32, width), BF16),
            shape_of(6, BLOCK),
        ],
        [pltpu.VMEM((6, width), F32)],
    )
    return tuple(
        lax.cond(
            table[2, 0] > 0,
            lambda: tuple(
                shared_steps(
                    kinematics, derivatives, mass, last, table, gathered, pieces, moments, centre
                )
            ),
            lambda: tuple(
                plain_steps(kinematics, derivatives, mass, last, block_list, block_count)
            ),
        )
    )


def solution(mesh):
    return jax.shard_map(
        per_device,
        mesh=mesh,
        in_specs=(P(None, "blk"), P(None, "blk"), P("blk"), P("blk"), P(), P()),
        out_specs=(P(None, "blk"), P(None, "blk")),
        check_vma=False,
    )
```

```python
import functools

import jax
import jax.numpy as jnp
from jax import lax
from jax.experimental import pallas as pl
from jax.experimental.pallas import tpu as pltpu
from jax.sharding import PartitionSpec as P

BLOCK = 128
CAP = 2
STEPS = 2
ROWS = 8
F32 = jnp.float32
BF16 = jnp.bfloat16

step_length = 0.125
softening = 0.0025
grid_shift = 1.5 * 2.0**16
piece_rows = 128
chunk = 256
ahead_chunk = 1024
prep_width = 512
first_slots = 12


def predict(position, velocity, acceleration, jerk_old, interval):
    new_position = position + interval * (
        velocity + interval * (acceleration * 0.5 + interval * jerk_old / 6.0)
    )
    new_velocity = velocity + interval * (acceleration + interval * jerk_old * 0.5)
    return jnp.concatenate([new_position, new_velocity], axis=0)


def correct(predicted, old_deriv, forces, interval):
    change = old_deriv[:3] - forces[:3]
    second_term = -6.0 * change - interval * (4.0 * old_deriv[3:] + 2.0 * forces[3:])
    third_term = 12.0 * change + 6.0 * interval * (old_deriv[3:] + forces[3:])
    new_position = predicted[:3] + interval * interval * (second_term / 24.0 + third_term / 120.0)
    new_velocity = predicted[3:] + interval * (second_term / 6.0 + third_term / 24.0)
    return jnp.concatenate([new_position, new_velocity], axis=0)


def round_short(value):
    return value.astype(BF16).astype(F32)


def split_three(value):
    high = round_short(value)
    rest = value - high
    middle = round_short(rest)
    return high, middle, rest - middle


def stack_three(value):
    return jnp.concatenate(split_three(value), axis=0)


def star_pieces(stars):
    position, velocity = stars[0:3], stars[3:6]
    coarse = (position + grid_shift) - grid_shift
    coarse_a = round_short(coarse)
    coarse_b = coarse - coarse_a
    fine = position - coarse
    fine_a = round_short(fine)
    fine_b = round_short(fine - fine_a)
    fine = fine_a + fine_b
    square = jnp.sum(coarse * coarse, axis=0, keepdims=True)
    cross = jnp.sum(2.0 * coarse * fine + fine * fine, axis=0, keepdims=True)
    mixed = jnp.sum(position * velocity, axis=0, keepdims=True)
    return coarse_a, coarse_b, fine_a, fine_b, square, cross, mixed


def source_pieces(stars):
    ca, cb, fa, fb, square, cross, mixed = star_pieces(stars)
    va, vb, vc = split_three(stars[3:6])
    width = stars.shape[1]
    one = jnp.ones((3, width), F32)
    rows = [ca, ca, cb, cb, stack_three(square), one, jnp.zeros((6, width), F32)]
    rows += [ca, ca, cb, cb, fa, fa, fb, fb, fa, fa, stack_three(cross), one]
    rows += [va, va, va, vb, vb, vc, stack_three(mixed), one]
    rows += [jnp.zeros((piece_rows - 84, width), F32)]
    return jnp.concatenate(rows, axis=0)


def target_pieces(stars):
    ca, cb, fa, fb, square, cross, mixed = star_pieces(stars)
    va, vb, vc = split_three(stars[3:6])
    xa, xb, xc = split_three(stars[0:3])
    width = stars.shape[1]
    one = jnp.ones((3, width), F32)
    zero = jnp.zeros((3, width), F32)
    da, db = -2.0 * ca, -2.0 * cb
    ea, eb = -2.0 * fa, -2.0 * fb
    tail = jnp.zeros((piece_rows - 84, width), F32)
    radius = [da, db, da, db, one, stack_three(square), zero, zero]
    radius += [ea, eb, ea, eb, da, db, da, db, ea, eb, one, stack_three(cross + softening)]
    radius += [zero] * 8 + [tail]
    moving = [-va, -vb, -va, -vb, zero, zero, zero, zero]
    moving += [-vc, zero, zero, zero, -va, -vb, -va, zero, zero, zero, zero, zero]
    moving += [-xa, -xb, -xc, -xa, -xb, -xa, one, stack_three(mixed), tail]
    both = [jnp.concatenate(radius, axis=0), jnp.concatenate(moving, axis=0)]
    return jnp.concatenate(both, axis=1).astype(BF16)


def block_at(number):
    return pl.ds(pl.multiple_of(number * BLOCK, BLOCK), BLOCK)


def predicted_block(kin_ref, der_ref, last_ref, where, time_now):
    kin, der = kin_ref[:, where], der_ref[:, where]
    return predict(kin[:3], kin[3:], der[:3], der[3:], time_now - last_ref[:, where])


def list_place(step, blk, rep, slot, n_blk, n_rep):
    return ((step * n_blk + blk) * n_rep + rep) * CAP + slot


def write_targets(step, n_blk, n_rep, list_ref, kin_ref, der_ref, last_ref, out_ref):
    blk, rep = lax.axis_index("blk"), lax.axis_index("rep")
    rows = []
    for slot in range(CAP):
        number = list_ref[list_place(step, blk, rep, slot, n_blk, n_rep)]
        rows.append(predicted_block(kin_ref, der_ref, last_ref, block_at(number), step * step_length))
        rows.append(jnp.zeros((ROWS - 6, BLOCK), F32))
    mine = jnp.concatenate(rows, axis=0)
    for other in range(n_blk):
        out_ref[other] = mine


def targets_kernel(step, n_blk, n_rep, list_ref, kin_ref, der_ref, last_ref, out_ref):
    write_targets(step, n_blk, n_rep, list_ref, kin_ref, der_ref, last_ref, out_ref)


def forces_kernel(
    step, n_blk, n_rep, count_ref, target_ref, kin_ref, der_ref, last_ref, mass_ref,
    out_ref, pred_ref, piece_ref, moment_ref,
):
    rep = lax.axis_index("rep")
    width = kin_ref.shape[1]
    total = jnp.zeros((6, prep_width), F32)
    for part in range(width // prep_width):
        where = pl.ds(part * prep_width, prep_width)
        stars = predicted_block(kin_ref, der_ref, last_ref, where, step * step_length)
        pred_ref[:, where] = stars
        total = total + stars
    centre = jnp.sum(total, axis=1, keepdims=True) / width
    for part in range(width // prep_width):
        where = pl.ds(part * prep_width, prep_width)
        stars = pred_ref[:, where] - centre
        piece_ref[where, :] = source_pieces(stars).T.astype(BF16)
        scaled = mass_ref[:, where] / (width * n_blk)
        ones = jnp.ones((1, prep_width), F32)
        moments = jnp.concatenate([stars, ones, jnp.zeros_like(ones)], axis=0) * scaled
        moments = jnp.concatenate([stack_three(moments), jnp.zeros((8, prep_width), F32)], axis=0)
        moment_ref[:, where] = moments.astype(BF16)

    def one_slot(place, carry):
        blk = place // CAP
        slot = place % CAP
        active = slot < count_ref[(step * n_blk + blk) * n_rep + rep]

        @pl.when(active)
        def _():
            stars = target_ref[place][0:6] - centre
            against = target_pieces(stars)
            acc = jnp.zeros((32, 2 * BLOCK), F32)
            for part in range(width // chunk):
                where = pl.ds(part * chunk, chunk)
                both = jnp.dot(piece_ref[where, :], against, preferred_element_type=F32)
                inverse = lax.rsqrt(both[:, :BLOCK])
                inverse_sq = inverse * inverse
                weight = inverse * inverse_sq
                radial = weight * (inverse_sq * both[:, BLOCK:])
                pair = jnp.concatenate([weight, radial], axis=1)
                high = pair.astype(BF16)
                low = (pair - high.astype(F32)).astype(BF16)
                moments = moment_ref[:, where]
                acc = acc + jnp.dot(moments, high, preferred_element_type=F32)
                acc = acc + jnp.dot(moments, low, preferred_element_type=F32)
            acc = acc[0:8] + acc[8:16] + acc[16:24]
            by_weight, by_radial = acc[:, :BLOCK], acc[:, BLOCK:]
            sums = by_weight[0:6] - stars * by_weight[6:7]
            pull = by_radial[0:3] - stars[0:3] * by_radial[6:7]
            out_ref[place] = jnp.concatenate(
                [sums[0:3], sums[3:6] - 3.0 * pull, jnp.zeros((ROWS - 6, BLOCK), F32)], axis=0
            )

        @pl.when(jnp.logical_not(active))
        def _():
            out_ref[place] = jnp.zeros((ROWS, BLOCK), F32)

        return carry

    lax.fori_loop(0, n_blk * CAP, one_slot, 0)


def total_kernel(n_blk, n_rep, part_ref, out_ref):
    total = part_ref[0]
    for other in range(1, n_blk):
        total = total + part_ref[other]
    for other in range(n_rep):
        out_ref[other] = total


def update_kernel(
    step, n_blk, n_rep, list_ref, count_ref, force_ref, kin_ref, der_ref, last_ref,
    new_kin_ref, new_der_ref, new_last_ref, *next_refs,
):
    blk = lax.axis_index("blk")
    time_now = step * step_length
    new_kin_ref[...] = kin_ref[...]
    new_der_ref[...] = der_ref[...]
    new_last_ref[...] = last_ref[...]

    def one_slot(place, carry):
        rep = place // CAP
        slot = place % CAP

        @pl.when(slot < count_ref[(step * n_blk + blk) * n_rep + rep])
        def _():
            number = list_ref[list_place(step, blk, rep, slot, n_blk, n_rep)]
            where = block_at(number)
            predicted = predicted_block(kin_ref, der_ref, last_ref, where, time_now)
            forces = force_ref[place][0:6]
            interval = time_now - last_ref[:, where]
            new_kin_ref[:, where] = correct(predicted, der_ref[:, where], forces, interval)
            new_der_ref[:, where] = forces
            new_last_ref[:, where] = jnp.full((1, BLOCK), time_now, F32)

        return carry

    lax.fori_loop(0, n_rep * CAP, one_slot, 0)
    if next_refs:
        write_targets(
            step + 1, n_blk, n_rep, list_ref, new_kin_ref, new_der_ref, new_last_ref, next_refs[0]
        )


def lane_iota(rows):
    return lax.broadcasted_iota(jnp.int32, (rows, BLOCK), 1)


def active_rows(n_blk, n_rep, list_ref, count_ref):
    per_row = BLOCK // n_rep
    parts = BLOCK * n_rep // BLOCK // 4
    lanes = lane_iota(n_blk)
    steps = []
    for step in range(STEPS):
        counted = count_ref[step]
        tiled = []
        for slot in range(CAP):
            listed = jnp.where(counted > slot, list_ref[step, :, slot, :], -1)
            tiled.append(jnp.concatenate([listed] * per_row, axis=1))
        hits = []
        for part in range(parts):
            number = lanes // n_rep + part * per_row
            hit = (tiled[0] == number) | (tiled[1] == number)
            hits.append(jnp.where(hit, 1.0, 0.0))
        steps.append(jnp.concatenate(hits, axis=1))
    hits = jnp.concatenate(steps, axis=0).astype(BF16)
    width = parts * BLOCK
    rows = lax.broadcasted_iota(jnp.int32, (width, BLOCK), 0) // n_rep
    spread = jnp.where(rows == lax.broadcasted_iota(jnp.int32, (width, BLOCK), 1), 1.0, 0.0)
    return jnp.dot(hits, spread.astype(BF16), preferred_element_type=F32)


def share_blocks(n_blk, n_rep, list_ref, count_ref, table_ref):
    blk, rep = lax.axis_index("blk"), lax.axis_index("rep")
    flags = active_rows(n_blk, n_rep, list_ref, count_ref)
    first, second = flags[:n_blk], flags[n_blk:]
    in_both = first * second
    kinds = [in_both, first - in_both, second - in_both]
    earlier = lax.broadcasted_iota(jnp.int32, (BLOCK, BLOCK), 0) < lax.broadcasted_iota(
        jnp.int32, (BLOCK, BLOCK), 1
    )
    earlier = jnp.where(earlier, 1.0, 0.0).astype(BF16)
    above = lax.broadcasted_iota(jnp.int32, (n_blk, n_blk), 0) > lax.broadcasted_iota(
        jnp.int32, (n_blk, n_blk), 1
    )
    above = jnp.where(above, 1.0, 0.0).astype(BF16)
    own_row = lax.broadcasted_iota(jnp.int32, (n_blk, BLOCK), 0) == blk
    lanes = lane_iota(1)
    order = lanes * n_rep + rep
    start = jnp.zeros((1, 1), F32)
    fits = jnp.ones((1, 1), jnp.bool_)
    own_kind, own_place, own_number, finish, owner = [], [], [], [], []
    for kind in kinds:
        short = kind.astype(BF16)
        rank = jnp.dot(short, earlier, preferred_element_type=F32)
        before = jnp.dot(above, short, preferred_element_type=F32)
        before = jnp.sum(before, axis=1, keepdims=True) + start
        amount = jnp.sum(kind, axis=1, keepdims=True)
        fits = fits & (jnp.max(amount, axis=0, keepdims=True) <= n_rep)
        ends = (before + amount).astype(jnp.int32)
        owner.append(jnp.sum(jnp.where(ends <= order, 1, 0), axis=0, keepdims=True))
        place = jnp.sum(jnp.where(own_row, before + rank, 0.0), axis=0, keepdims=True)
        own_place.append(place.astype(jnp.int32))
        own_kind.append(jnp.sum(jnp.where(own_row, kind, 0.0), axis=0, keepdims=True) > 0.5)
        finish.append((jnp.max(before + amount, axis=0, keepdims=True)).astype(jnp.int32))
        if len(finish) == 1:
            start = jnp.sum(amount, axis=0, keepdims=True)
    both_end = finish[0]
    total = [jnp.maximum(finish[0], finish[1]), jnp.maximum(finish[0], finish[2])]
    fits = fits & (total[0] <= n_rep * first_slots) & (total[1] <= n_rep * n_rep)
    handler = [jnp.bitwise_and(place, n_rep - 1) for place in own_place]
    home = []
    for step in range(STEPS):
        code = jnp.where(own_kind[0], handler[0] * 2, -1)
        home.append(jnp.where(own_kind[1 + step], handler[1 + step] * 2 + 1, code))
    places = []
    for step in range(STEPS):
        is_both = order < both_end
        places.append(jnp.where(is_both, owner[0] * 4, owner[1 + step] * 4 + 2 + step))
    scalars = jnp.where(lanes == 0, jnp.where(fits, 1, 0), 0)
    numbers = []
    for index in range(3):
        mine = own_kind[index] & (handler[index] == rep)
        numbers.append(jnp.sum(jnp.where(mine, lanes.astype(F32), 0.0)).astype(jnp.int32))
        spot = jnp.max(jnp.where(mine, own_place[index] // n_rep, 0), axis=1, keepdims=True)
        scalars = jnp.where(lanes == 4 + index, spot, scalars)
    for step in range(STEPS):
        amount = (total[step] - rep + n_rep - 1) // n_rep
        scalars = jnp.where(lanes == 7 + step, amount, scalars)
    amount = (both_end - rep + n_rep - 1) // n_rep
    scalars = jnp.where(lanes == 9, amount, scalars)
    rows = [home[0], home[1], scalars, places[0], places[1], jnp.zeros((3, BLOCK), jnp.int32)]
    table_ref[...] = jnp.concatenate(rows, axis=0)
    return numbers


def share_kernel(n_blk, n_rep, list_ref, count_ref, kin_ref, der_ref, last_ref, table_ref, out_ref):
    numbers = share_blocks(n_blk, n_rep, list_ref, count_ref, table_ref)
    where = [block_at(number) for number in numbers]
    gap = jnp.zeros((2, BLOCK), F32)
    rows = [
        predicted_block(kin_ref, der_ref, last_ref, where[0], 0.0),
        0.0 - last_ref[:, where[0]],
        gap[0:1],
        der_ref[:, where[0]],
        gap,
        predicted_block(kin_ref, der_ref, last_ref, where[1], 0.0),
        gap,
        predicted_block(kin_ref, der_ref, last_ref, where[2], step_length),
        gap,
    ]
    mine = jnp.concatenate(rows, axis=0)
    for other in range(n_blk):
        out_ref[other] = mine


def write_pieces(n_blk, width, kin_ref, der_ref, last_ref, mass_ref, time_now, pred_ref, piece_ref, moment_ref):
    total = jnp.zeros((6, prep_width), F32)
    for part in range(width // prep_width):
        where = pl.ds(part * prep_width, prep_width)
        stars = predicted_block(kin_ref, der_ref, last_ref, where, time_now)
        pred_ref[:, where] = stars
        total = total + stars
    centre = jnp.sum(total, axis=1, keepdims=True) / width
    for part in range(width // prep_width):
        where = pl.ds(part * prep_width, prep_width)
        stars = pred_ref[:, where] - centre
        piece_ref[where, :] = source_pieces(stars).T.astype(BF16)
        scaled = mass_ref[:, where] / (width * n_blk)
        ones = jnp.ones((1, prep_width), F32)
        moments = jnp.concatenate([stars, ones, jnp.zeros_like(ones)], axis=0) * scaled
        moments = jnp.concatenate([stack_three(moments), jnp.zeros((8, prep_width), F32)], axis=0)
        moment_ref[:, where] = moments.astype(BF16)
    return centre


def block_forces(blocks, piece_ref, moment_ref):
    against = [target_pieces(stars) for stars in blocks]
    parts = piece_ref.shape[0] // ahead_chunk
    order = [(index, part) for index in range(len(blocks)) for part in range(parts)]
    by_weight = [jnp.zeros((32, 2 * BLOCK), F32) for stars in blocks]
    by_radial = [jnp.zeros((32, 2 * BLOCK), F32) for stars in blocks]

    def meet(index, part):
        where = pl.ds(part * ahead_chunk, ahead_chunk)
        return jnp.dot(piece_ref[where, :], against[index], preferred_element_type=F32)

    def halves(value):
        high = value.astype(BF16)
        low = (value - high.astype(F32)).astype(BF16)
        return jnp.concatenate([high, low], axis=1)

    both = meet(*order[0])
    for turn, (index, part) in enumerate(order):
        ahead = meet(*order[turn + 1]) if turn + 1 < len(order) else None
        inverse = lax.rsqrt(both[:, :BLOCK])
        inverse_sq = inverse * inverse
        weight = inverse * inverse_sq
        radial = weight * (inverse_sq * both[:, BLOCK:])
        moments = moment_ref[:, pl.ds(part * ahead_chunk, ahead_chunk)]
        by_weight[index] += jnp.dot(moments, halves(weight), preferred_element_type=F32)
        by_radial[index] += jnp.dot(moments, halves(radial), preferred_element_type=F32)
        both = ahead

    def gather_up(value):
        value = value[0:8] + value[8:16] + value[16:24]
        return value[:, :BLOCK] + value[:, BLOCK:]

    results = []
    for index, stars in enumerate(blocks):
        on_weight, on_radial = gather_up(by_weight[index]), gather_up(by_radial[index])
        sums = on_weight[0:6] - stars * on_weight[6:7]
        pull = on_radial[0:3] - stars[0:3] * on_radial[6:7]
        gap = jnp.zeros((ROWS - 6, BLOCK), F32)
        results.append(jnp.concatenate([sums[0:3], sums[3:6] - 3.0 * pull, gap], axis=0))
    return results


def all_forces(amount, stars_of, store, piece_ref, moment_ref):
    def some(first, size):
        blocks = [stars_of(first + index) for index in range(size)]
        results = block_forces(blocks, piece_ref, moment_ref)
        for index, result in enumerate(results):
            store(first + index, result)

    pairs = amount // 2

    def two(pair, carry):
        some(pair * 2, 2)
        return carry

    lax.fori_loop(0, pairs, two, 0)

    @pl.when(amount > pairs * 2)
    def _():
        some(pairs * 2, 1)


def pieces_kernel(n_blk, kin_ref, der_ref, last_ref, mass_ref, piece_ref, moment_ref, centre_ref, pred_ref):
    width = kin_ref.shape[1]
    centre = write_pieces(
        n_blk, width, kin_ref, der_ref, last_ref, mass_ref, 0.0, pred_ref, piece_ref, moment_ref
    )
    centre_ref[...] = jnp.broadcast_to(centre, (6, BLOCK))


def first_forces_kernel(table_ref, target_ref, piece_ref, moment_ref, centre_ref, out_ref):
    out_ref[...] = jnp.zeros_like(out_ref)

    def stars_of(index):
        return target_ref[table_ref[3, index]][0:6] - centre_ref[...]

    def store(index, result):
        out_ref[index] = result

    all_forces(table_ref[2, 7], stars_of, store, piece_ref, moment_ref)


def flag_rows():
    rows = lax.broadcasted_iota(jnp.int32, (CAP * ROWS, BLOCK), 0)
    return jnp.bitwise_and(rows, ROWS - 1) == 6


def flagged_total_kernel(n_blk, n_rep, part_ref, out_ref):
    total = part_ref[0]
    for other in range(1, n_blk):
        total = total + part_ref[other]
    total = jnp.where(flag_rows(), 1.0, total)
    for other in range(n_rep):
        out_ref[other] = total


def middle_kernel(
    n_rep, table_ref, term_a, term_b, term_c, term_d, target_ref, share_ref, next_ref, force_ref
):
    force_ref[...] = term_a[...] + ((term_b[...] + term_c[...]) + term_d[...])
    own = jnp.concatenate([force_ref[table_ref[2, 4]], force_ref[table_ref[2, 5]]], axis=0)
    own = jnp.where(flag_rows(), 1.0, own)
    for other in range(n_rep):
        share_ref[other] = own

    def one(index, carry):
        place = table_ref[4, index]
        is_both = index < table_ref[2, 9]

        @pl.when(is_both)
        def _():
            head, deriv = target_ref[place], target_ref[place + 1][0:6]
            forces = force_ref[index][0:6]
            moved = correct(head[0:6], deriv, forces, head[6:7])
            ahead = predict(moved[:3], moved[3:], forces[:3], forces[3:], step_length)
            next_ref[index] = jnp.concatenate([ahead, head[6:8]], axis=0)

        @pl.when(jnp.logical_not(is_both))
        def _():
            next_ref[index] = target_ref[place]

        return carry

    lax.fori_loop(0, table_ref[2, 8], one, 0)


def place_forces(step, table_ref, force_ref, placed_ref):
    for number in range(placed_ref.shape[1] // BLOCK):
        code = table_ref[step, number]
        tile = force_ref[jnp.maximum(code, 0)]
        tile = tile * jnp.where(code >= 0, 1.0, 0.0)
        placed_ref[:, pl.ds(number * BLOCK, BLOCK)] = tile


def moved_part(step, where, placed_ref, kin_ref, der_ref, last_ref):
    time_now = step * step_length
    placed = placed_ref[:, where]
    forces, moved = placed[0:6], placed[6:7] > 0.5
    kin, der, last = kin_ref[:, where], der_ref[:, where], last_ref[:, where]
    interval = time_now - last
    predicted = predict(kin[:3], kin[3:], der[:3], der[3:], interval)
    corrected = correct(predicted, der, forces, interval)
    return (
        jnp.where(moved, corrected, kin),
        jnp.where(moved, forces, der),
        jnp.where(moved, time_now, last),
    )


def second_forces_kernel(
    n_blk, table_ref, force_ref, target_ref, kin_ref, der_ref, last_ref, mass_ref,
    out_ref, new_kin_ref, new_der_ref, new_last_ref, placed_ref, pred_ref, piece_ref, moment_ref,
):
    width = kin_ref.shape[1]
    place_forces(0, table_ref, force_ref, placed_ref)
    for part in range(width // prep_width):
        where = pl.ds(part * prep_width, prep_width)
        kin, der, last = moved_part(0, where, placed_ref, kin_ref, der_ref, last_ref)
        new_kin_ref[:, where] = kin
        new_der_ref[:, where] = der
        new_last_ref[:, where] = last
    centre = write_pieces(
        n_blk, width, new_kin_ref, new_der_ref, new_last_ref, mass_ref, step_length,
        pred_ref, piece_ref, moment_ref,
    )
    out_ref[...] = jnp.zeros_like(out_ref)

    def stars_of(index):
        return target_ref[index][0:6] - centre

    def store(index, result):
        place = table_ref[4, index]
        out_ref[(place // 4) * 2 + place % 2] = result

    all_forces(table_ref[2, 8], stars_of, store, piece_ref, moment_ref)


def last_kernel(
    table_ref, force_ref, kin_ref, der_ref, last_ref, new_kin_ref, new_der_ref, placed_ref
):
    place_forces(1, table_ref, force_ref, placed_ref)
    for part in range(kin_ref.shape[1] // prep_width):
        where = pl.ds(part * prep_width, prep_width)
        kin, der, last = moved_part(1, where, placed_ref, kin_ref, der_ref, last_ref)
        new_kin_ref[:, where] = kin
        new_der_ref[:, where] = der


def shape_of(*sizes):
    return jax.ShapeDtypeStruct(sizes, F32)


def run_kernel(body, scalars, arrays, out_shape, scratch=(), cost=None):
    return pl.pallas_call(
        body,
        out_shape=out_shape,
        in_specs=[pl.BlockSpec(memory_space=pltpu.SMEM)] * len(scalars)
        + [pl.BlockSpec(memory_space=pltpu.VMEM)] * len(arrays),
        out_specs=jax.tree.map(lambda leaf: pl.BlockSpec(memory_space=pltpu.VMEM), out_shape),
        scratch_shapes=list(scratch),
        cost_estimate=cost,
        compiler_params=pltpu.CompilerParams(vmem_limit_bytes=32 * 2**20),
    )(*scalars, *arrays)


def plain_steps(kinematics, derivatives, mass, last, block_list, block_count):
    width = kinematics.shape[1]
    n_blk = lax.axis_size("blk")
    n_rep = lax.axis_size("rep")
    flat_list = block_list.reshape(-1)
    flat_count = block_count.reshape(-1)
    targets = run_kernel(
        functools.partial(targets_kernel, 0, n_blk, n_rep),
        [flat_list],
        [kinematics, derivatives, last],
        shape_of(n_blk, CAP * ROWS, BLOCK),
    )
    for step in range(STEPS):
        gathered = lax.all_to_all(targets, "blk", 0, 0, tiled=True)
        partial_forces = run_kernel(
            functools.partial(forces_kernel, step, n_blk, n_rep),
            [flat_count],
            [gathered.reshape(n_blk * CAP, ROWS, BLOCK), kinematics, derivatives, last, mass],
            shape_of(n_blk * CAP, ROWS, BLOCK),
            [
                pltpu.VMEM((6, width), F32),
                pltpu.VMEM((width, piece_rows), BF16),
                pltpu.VMEM((32, width), BF16),
            ],
        )
        partial_forces = partial_forces.reshape(n_blk, CAP * ROWS, BLOCK)
        spread = lax.all_to_all(partial_forces, "blk", 0, 0, tiled=True)
        mine = run_kernel(
            functools.partial(total_kernel, n_blk, n_rep),
            [],
            [spread],
            shape_of(n_rep, CAP * ROWS, BLOCK),
        )
        forces = lax.all_to_all(mine, "rep", 0, 0, tiled=True)
        out_shape = [shape_of(6, width), shape_of(6, width), shape_of(1, width)]
        if step + 1 < STEPS:
            out_shape.append(shape_of(n_blk, CAP * ROWS, BLOCK))
        kinematics, derivatives, last, *rest = run_kernel(
            functools.partial(update_kernel, step, n_blk, n_rep),
            [flat_list, flat_count],
            [forces.reshape(n_rep * CAP, ROWS, BLOCK), kinematics, derivatives, last],
            out_shape,
        )
        if rest:
            targets = rest[0]
    return (kinematics, derivatives)


def add_over_blk(value):
    n_blk = lax.axis_size("blk")

    def from_partner(distance):
        return lax.ppermute(value, "blk", [(i, i ^ distance) for i in range(n_blk)])

    value = value + from_partner(1)
    value = value + from_partner(2)
    return [value, from_partner(4), from_partner(12), from_partner(8)]


def shared_steps(kinematics, derivatives, mass, last, table, gathered, pieces, moments, centre):
    width = kinematics.shape[1]
    n_blk = lax.axis_size("blk")
    n_rep = lax.axis_size("rep")
    piece_scratch = [pltpu.VMEM((width, piece_rows), BF16), pltpu.VMEM((32, width), BF16)]
    stars_scratch = pltpu.VMEM((6, width), F32)
    partial_forces = run_kernel(
        first_forces_kernel,
        [table],
        [gathered, pieces, moments, centre],
        shape_of(first_slots, ROWS, BLOCK),
    )
    terms = add_over_blk(partial_forces.reshape(first_slots * ROWS, BLOCK))
    terms = [term.reshape(first_slots, ROWS, BLOCK) for term in terms]
    shares, targets = run_kernel(
        functools.partial(middle_kernel, n_rep),
        [table],
        [*terms, gathered],
        [shape_of(n_rep, 2 * ROWS, BLOCK), shape_of(n_rep, ROWS, BLOCK)],
        [pltpu.VMEM((first_slots, ROWS, BLOCK), F32)],
    )
    shares = lax.all_to_all(shares, "rep", 0, 0, tiled=True)
    partial_forces, kinematics, derivatives, last = run_kernel(
        functools.partial(second_forces_kernel, n_blk),
        [table],
        [shares.reshape(n_rep * 2, ROWS, BLOCK), targets, kinematics, derivatives, last, mass],
        [shape_of(n_blk * 2, ROWS, BLOCK), shape_of(6, width), shape_of(6, width), shape_of(1, width)],
        [pltpu.VMEM((ROWS, width), F32), stars_scratch] + piece_scratch,
    )
    spread = lax.all_to_all(
        partial_forces.reshape(n_blk, 2 * ROWS, BLOCK), "blk", 0, 0, tiled=True
    )
    mine = run_kernel(
        functools.partial(flagged_total_kernel, n_blk, n_rep),
        [],
        [spread],
        shape_of(n_rep, 2 * ROWS, BLOCK),
    )
    shares = lax.all_to_all(mine, "rep", 0, 0, tiled=True)
    return run_kernel(
        last_kernel,
        [table],
        [shares.reshape(n_rep * 2, ROWS, BLOCK), kinematics, derivatives, last],
        [shape_of(6, width), shape_of(6, width)],
        [pltpu.VMEM((ROWS, width), F32)],
    )


def per_device(kinematics, derivatives, masses, last_time, block_list, block_count):
    width = kinematics.shape[1]
    n_blk = lax.axis_size("blk")
    n_rep = lax.axis_size("rep")
    mass = masses.reshape(1, width)
    last = last_time.reshape(1, width)
    table, targets = run_kernel(
        functools.partial(share_kernel, n_blk, n_rep),
        [],
        [block_list.transpose(0, 1, 3, 2), block_count, kinematics, derivatives, last],
        [jax.ShapeDtypeStruct((8, BLOCK), jnp.int32), shape_of(n_blk, 4 * ROWS, BLOCK)],
    )
    gathered = lax.all_to_all(targets, "blk", 0, 0, tiled=True)
    gathered = gathered.reshape(n_blk * 4, ROWS, BLOCK)
    pieces, moments, centre = run_kernel(
        functools.partial(pieces_kernel, n_blk),
        [],
        [kinematics, derivatives, last, mass],
        [
            jax.ShapeDtypeStruct((width, piece_rows), BF16),
            jax.ShapeDtypeStruct((32, width), BF16),
            shape_of(6, BLOCK),
        ],
        [pltpu.VMEM((6, width), F32)],
    )
    return tuple(
        lax.cond(
            table[2, 0] > 0,
            lambda: tuple(
                shared_steps(
                    kinematics, derivatives, mass, last, table, gathered, pieces, moments, centre
                )
            ),
            lambda: tuple(
                plain_steps(kinematics, derivatives, mass, last, block_list, block_count)
            ),
        )
    )


def solution(mesh):
    return jax.shard_map(
        per_device,
        mesh=mesh,
        in_specs=(P(None, "blk"), P(None, "blk"), P("blk"), P("blk"), P(), P()),
        out_specs=(P(None, "blk"), P(None, "blk")),
        check_vma=False,
    )
```

```python
import functools

import jax
import jax.numpy as jnp
from jax import lax
from jax.experimental import pallas as pl
from jax.experimental.pallas import tpu as pltpu
from jax.sharding import PartitionSpec as P

BLOCK = 128
CAP = 2
STEPS = 2
ROWS = 8
F32 = jnp.float32
BF16 = jnp.bfloat16

step_length = 0.125
softening = 0.0025
grid_shift = 1.5 * 2.0**16
piece_rows = 128
chunk = 256
ahead_chunk = 1024
early_chunks = 2
early_pair = 2
prep_width = 512
first_slots = 12


def predict(position, velocity, acceleration, jerk_old, interval):
    new_position = position + interval * (
        velocity + interval * (acceleration * 0.5 + interval * jerk_old / 6.0)
    )
    new_velocity = velocity + interval * (acceleration + interval * jerk_old * 0.5)
    return jnp.concatenate([new_position, new_velocity], axis=0)


def correct(predicted, old_deriv, forces, interval):
    change = old_deriv[:3] - forces[:3]
    second_term = -6.0 * change - interval * (4.0 * old_deriv[3:] + 2.0 * forces[3:])
    third_term = 12.0 * change + 6.0 * interval * (old_deriv[3:] + forces[3:])
    new_position = predicted[:3] + interval * interval * (second_term / 24.0 + third_term / 120.0)
    new_velocity = predicted[3:] + interval * (second_term / 6.0 + third_term / 24.0)
    return jnp.concatenate([new_position, new_velocity], axis=0)


def round_short(value):
    return value.astype(BF16).astype(F32)


def split_three(value):
    high = round_short(value)
    rest = value - high
    middle = round_short(rest)
    return high, middle, rest - middle


def stack_three(value):
    return jnp.concatenate(split_three(value), axis=0)


def star_pieces(stars):
    position, velocity = stars[0:3], stars[3:6]
    coarse = (position + grid_shift) - grid_shift
    coarse_a = round_short(coarse)
    coarse_b = coarse - coarse_a
    fine = position - coarse
    fine_a = round_short(fine)
    fine_b = round_short(fine - fine_a)
    fine = fine_a + fine_b
    square = jnp.sum(coarse * coarse, axis=0, keepdims=True)
    cross = jnp.sum(2.0 * coarse * fine + fine * fine, axis=0, keepdims=True)
    mixed = jnp.sum(position * velocity, axis=0, keepdims=True)
    return coarse_a, coarse_b, fine_a, fine_b, square, cross, mixed


def source_pieces(stars):
    ca, cb, fa, fb, square, cross, mixed = star_pieces(stars)
    va, vb, vc = split_three(stars[3:6])
    width = stars.shape[1]
    one = jnp.ones((3, width), F32)
    rows = [ca, ca, cb, cb, stack_three(square), one, jnp.zeros((6, width), F32)]
    rows += [ca, ca, cb, cb, fa, fa, fb, fb, fa, fa, stack_three(cross), one]
    rows += [va, va, va, vb, vb, vc, stack_three(mixed), one]
    rows += [jnp.zeros((piece_rows - 84, width), F32)]
    return jnp.concatenate(rows, axis=0)


def target_pieces(stars):
    ca, cb, fa, fb, square, cross, mixed = star_pieces(stars)
    va, vb, vc = split_three(stars[3:6])
    xa, xb, xc = split_three(stars[0:3])
    width = stars.shape[1]
    one = jnp.ones((3, width), F32)
    zero = jnp.zeros((3, width), F32)
    da, db = -2.0 * ca, -2.0 * cb
    ea, eb = -2.0 * fa, -2.0 * fb
    tail = jnp.zeros((piece_rows - 84, width), F32)
    radius = [da, db, da, db, one, stack_three(square), zero, zero]
    radius += [ea, eb, ea, eb, da, db, da, db, ea, eb, one, stack_three(cross + softening)]
    radius += [zero] * 8 + [tail]
    moving = [-va, -vb, -va, -vb, zero, zero, zero, zero]
    moving += [-vc, zero, zero, zero, -va, -vb, -va, zero, zero, zero, zero, zero]
    moving += [-xa, -xb, -xc, -xa, -xb, -xa, one, stack_three(mixed), tail]
    both = [jnp.concatenate(radius, axis=0), jnp.concatenate(moving, axis=0)]
    return jnp.concatenate(both, axis=1).astype(BF16)


def block_at(number):
    return pl.ds(pl.multiple_of(number * BLOCK, BLOCK), BLOCK)


def predicted_block(kin_ref, der_ref, last_ref, where, time_now):
    kin, der = kin_ref[:, where], der_ref[:, where]
    return predict(kin[:3], kin[3:], der[:3], der[3:], time_now - last_ref[:, where])


def list_place(step, blk, rep, slot, n_blk, n_rep):
    return ((step * n_blk + blk) * n_rep + rep) * CAP + slot


def write_targets(step, n_blk, n_rep, list_ref, kin_ref, der_ref, last_ref, out_ref):
    blk, rep = lax.axis_index("blk"), lax.axis_index("rep")
    rows = []
    for slot in range(CAP):
        number = list_ref[list_place(step, blk, rep, slot, n_blk, n_rep)]
        rows.append(predicted_block(kin_ref, der_ref, last_ref, block_at(number), step * step_length))
        rows.append(jnp.zeros((ROWS - 6, BLOCK), F32))
    mine = jnp.concatenate(rows, axis=0)
    for other in range(n_blk):
        out_ref[other] = mine


def targets_kernel(step, n_blk, n_rep, list_ref, kin_ref, der_ref, last_ref, out_ref):
    write_targets(step, n_blk, n_rep, list_ref, kin_ref, der_ref, last_ref, out_ref)


def forces_kernel(
    step, n_blk, n_rep, count_ref, target_ref, kin_ref, der_ref, last_ref, mass_ref,
    out_ref, pred_ref, piece_ref, moment_ref,
):
    rep = lax.axis_index("rep")
    width = kin_ref.shape[1]
    total = jnp.zeros((6, prep_width), F32)
    for part in range(width // prep_width):
        where = pl.ds(part * prep_width, prep_width)
        stars = predicted_block(kin_ref, der_ref, last_ref, where, step * step_length)
        pred_ref[:, where] = stars
        total = total + stars
    centre = jnp.sum(total, axis=1, keepdims=True) / width
    for part in range(width // prep_width):
        where = pl.ds(part * prep_width, prep_width)
        stars = pred_ref[:, where] - centre
        piece_ref[where, :] = source_pieces(stars).T.astype(BF16)
        scaled = mass_ref[:, where] / (width * n_blk)
        ones = jnp.ones((1, prep_width), F32)
        moments = jnp.concatenate([stars, ones, jnp.zeros_like(ones)], axis=0) * scaled
        moments = jnp.concatenate([stack_three(moments), jnp.zeros((8, prep_width), F32)], axis=0)
        moment_ref[:, where] = moments.astype(BF16)

    def one_slot(place, carry):
        blk = place // CAP
        slot = place % CAP
        active = slot < count_ref[(step * n_blk + blk) * n_rep + rep]

        @pl.when(active)
        def _():
            stars = target_ref[place][0:6] - centre
            against = target_pieces(stars)
            acc = jnp.zeros((32, 2 * BLOCK), F32)
            for part in range(width // chunk):
                where = pl.ds(part * chunk, chunk)
                both = jnp.dot(piece_ref[where, :], against, preferred_element_type=F32)
                inverse = lax.rsqrt(both[:, :BLOCK])
                inverse_sq = inverse * inverse
                weight = inverse * inverse_sq
                radial = weight * (inverse_sq * both[:, BLOCK:])
                pair = jnp.concatenate([weight, radial], axis=1)
                high = pair.astype(BF16)
                low = (pair - high.astype(F32)).astype(BF16)
                moments = moment_ref[:, where]
                acc = acc + jnp.dot(moments, high, preferred_element_type=F32)
                acc = acc + jnp.dot(moments, low, preferred_element_type=F32)
            acc = acc[0:8] + acc[8:16] + acc[16:24]
            by_weight, by_radial = acc[:, :BLOCK], acc[:, BLOCK:]
            sums = by_weight[0:6] - stars * by_weight[6:7]
            pull = by_radial[0:3] - stars[0:3] * by_radial[6:7]
            out_ref[place] = jnp.concatenate(
                [sums[0:3], sums[3:6] - 3.0 * pull, jnp.zeros((ROWS - 6, BLOCK), F32)], axis=0
            )

        @pl.when(jnp.logical_not(active))
        def _():
            out_ref[place] = jnp.zeros((ROWS, BLOCK), F32)

        return carry

    lax.fori_loop(0, n_blk * CAP, one_slot, 0)


def total_kernel(n_blk, n_rep, part_ref, out_ref):
    total = part_ref[0]
    for other in range(1, n_blk):
        total = total + part_ref[other]
    for other in range(n_rep):
        out_ref[other] = total


def update_kernel(
    step, n_blk, n_rep, list_ref, count_ref, force_ref, kin_ref, der_ref, last_ref,
    new_kin_ref, new_der_ref, new_last_ref, *next_refs,
):
    blk = lax.axis_index("blk")
    time_now = step * step_length
    new_kin_ref[...] = kin_ref[...]
    new_der_ref[...] = der_ref[...]
    new_last_ref[...] = last_ref[...]

    def one_slot(place, carry):
        rep = place // CAP
        slot = place % CAP

        @pl.when(slot < count_ref[(step * n_blk + blk) * n_rep + rep])
        def _():
            number = list_ref[list_place(step, blk, rep, slot, n_blk, n_rep)]
            where = block_at(number)
            predicted = predicted_block(kin_ref, der_ref, last_ref, where, time_now)
            forces = force_ref[place][0:6]
            interval = time_now - last_ref[:, where]
            new_kin_ref[:, where] = correct(predicted, der_ref[:, where], forces, interval)
            new_der_ref[:, where] = forces
            new_last_ref[:, where] = jnp.full((1, BLOCK), time_now, F32)

        return carry

    lax.fori_loop(0, n_rep * CAP, one_slot, 0)
    if next_refs:
        write_targets(
            step + 1, n_blk, n_rep, list_ref, new_kin_ref, new_der_ref, new_last_ref, next_refs[0]
        )


def lane_iota(rows):
    return lax.broadcasted_iota(jnp.int32, (rows, BLOCK), 1)


def active_rows(n_blk, n_rep, list_ref, count_ref):
    per_row = BLOCK // n_rep
    parts = BLOCK * n_rep // BLOCK // 4
    lanes = lane_iota(n_blk)
    steps = []
    for step in range(STEPS):
        counted = count_ref[step]
        tiled = []
        for slot in range(CAP):
            listed = jnp.where(counted > slot, list_ref[step, :, slot, :], -1)
            tiled.append(jnp.concatenate([listed] * per_row, axis=1))
        hits = []
        for part in range(parts):
            number = lanes // n_rep + part * per_row
            hit = (tiled[0] == number) | (tiled[1] == number)
            hits.append(jnp.where(hit, 1.0, 0.0))
        steps.append(jnp.concatenate(hits, axis=1))
    hits = jnp.concatenate(steps, axis=0).astype(BF16)
    width = parts * BLOCK
    rows = lax.broadcasted_iota(jnp.int32, (width, BLOCK), 0) // n_rep
    spread = jnp.where(rows == lax.broadcasted_iota(jnp.int32, (width, BLOCK), 1), 1.0, 0.0)
    return jnp.dot(hits, spread.astype(BF16), preferred_element_type=F32)


def share_blocks(n_blk, n_rep, list_ref, count_ref, table_ref):
    blk, rep = lax.axis_index("blk"), lax.axis_index("rep")
    flags = active_rows(n_blk, n_rep, list_ref, count_ref)
    first, second = flags[:n_blk], flags[n_blk:]
    in_both = first * second
    kinds = [in_both, first - in_both, second - in_both]
    earlier = lax.broadcasted_iota(jnp.int32, (BLOCK, BLOCK), 0) < lax.broadcasted_iota(
        jnp.int32, (BLOCK, BLOCK), 1
    )
    earlier = jnp.where(earlier, 1.0, 0.0).astype(BF16)
    above = lax.broadcasted_iota(jnp.int32, (n_blk, n_blk), 0) > lax.broadcasted_iota(
        jnp.int32, (n_blk, n_blk), 1
    )
    above = jnp.where(above, 1.0, 0.0).astype(BF16)
    own_row = lax.broadcasted_iota(jnp.int32, (n_blk, BLOCK), 0) == blk
    lanes = lane_iota(1)
    order = lanes * n_rep + rep
    start = jnp.zeros((1, 1), F32)
    fits = jnp.ones((1, 1), jnp.bool_)
    own_kind, own_place, own_rank, finish, owner = [], [], [], [], []
    for kind in kinds:
        short = kind.astype(BF16)
        rank = jnp.dot(short, earlier, preferred_element_type=F32)
        before = jnp.dot(above, short, preferred_element_type=F32)
        before = jnp.sum(before, axis=1, keepdims=True) + start
        amount = jnp.sum(kind, axis=1, keepdims=True)
        fits = fits & (jnp.max(amount, axis=0, keepdims=True) <= n_rep)
        ends = (before + amount).astype(jnp.int32)
        owner.append(jnp.sum(jnp.where(ends <= order, 1, 0), axis=0, keepdims=True))
        place = jnp.sum(jnp.where(own_row, before + rank, 0.0), axis=0, keepdims=True)
        own_place.append(place.astype(jnp.int32))
        own_rank.append(jnp.sum(jnp.where(own_row, rank, 0.0), axis=0, keepdims=True))
        own_kind.append(jnp.sum(jnp.where(own_row, kind, 0.0), axis=0, keepdims=True) > 0.5)
        finish.append((jnp.max(before + amount, axis=0, keepdims=True)).astype(jnp.int32))
        if len(finish) == 1:
            start = jnp.sum(amount, axis=0, keepdims=True)
    both_end = finish[0]
    total = [jnp.maximum(finish[0], finish[1]), jnp.maximum(finish[0], finish[2])]
    fits = fits & (total[0] <= n_rep * first_slots) & (total[1] <= n_rep * n_rep)
    handler = [jnp.bitwise_and(place, n_rep - 1) for place in own_place]
    home = []
    for step in range(STEPS):
        code = jnp.where(own_kind[0], handler[0] * 2, -1)
        home.append(jnp.where(own_kind[1 + step], handler[1 + step] * 2 + 1, code))
    places = []
    for step in range(STEPS):
        is_both = order < both_end
        places.append(jnp.where(is_both, owner[0] * 4, owner[1 + step] * 4 + 2 + step))
    scalars = jnp.where(lanes == 0, jnp.where(fits, 1, 0), 0)
    numbers = []
    for index in range(3):
        mine = own_kind[index] & (handler[index] == rep)
        numbers.append(jnp.sum(jnp.where(mine, lanes.astype(F32), 0.0)).astype(jnp.int32))
        spot = jnp.max(jnp.where(mine, own_place[index] // n_rep, 0), axis=1, keepdims=True)
        scalars = jnp.where(lanes == 4 + index, spot, scalars)
    for step in range(STEPS):
        amount = (total[step] - rep + n_rep - 1) // n_rep
        scalars = jnp.where(lanes == 7 + step, amount, scalars)
    amount = (both_end - rep + n_rep - 1) // n_rep
    scalars = jnp.where(lanes == 9, amount, scalars)
    moved = own_kind[0] | own_kind[1]
    moved_amount = jnp.sum(jnp.where(moved, 1, 0), axis=1, keepdims=True)
    scalars = jnp.where(lanes == 10, moved_amount, scalars)
    moved_rank = (own_rank[0] + own_rank[1]).astype(jnp.int32)
    spots = jnp.where(moved, moved_rank, moved_amount + lanes - moved_rank)
    listed = (prep_width // BLOCK) * 8
    numbers_down = lax.broadcasted_iota(jnp.int32, (listed, BLOCK), 0)
    spots_down = jnp.sum(jnp.where(numbers_down == lanes, spots, 0), axis=1, keepdims=True)
    members = jnp.sum(jnp.where(spots_down == lanes, numbers_down, 0), axis=0, keepdims=True)
    gap = jnp.zeros((1, BLOCK), jnp.int32)
    rows = [home[0], home[1], scalars, places[0], places[1], spots, members, gap]
    table_ref[...] = jnp.concatenate(rows, axis=0)
    return numbers


def share_kernel(n_blk, n_rep, list_ref, count_ref, kin_ref, der_ref, last_ref, table_ref, out_ref):
    numbers = share_blocks(n_blk, n_rep, list_ref, count_ref, table_ref)
    where = [block_at(number) for number in numbers]
    gap = jnp.zeros((2, BLOCK), F32)
    rows = [
        predicted_block(kin_ref, der_ref, last_ref, where[0], 0.0),
        0.0 - last_ref[:, where[0]],
        gap[0:1],
        der_ref[:, where[0]],
        gap,
        predicted_block(kin_ref, der_ref, last_ref, where[1], 0.0),
        gap,
        predicted_block(kin_ref, der_ref, last_ref, where[2], step_length),
        gap,
    ]
    mine = jnp.concatenate(rows, axis=0)
    for other in range(n_blk):
        out_ref[other] = mine


def write_part(n_blk, width, stars, mass, where, piece_ref, moment_ref):
    piece_ref[where, :] = source_pieces(stars).T.astype(BF16)
    ones = jnp.ones((1, prep_width), F32)
    moments = jnp.concatenate([stars, ones, jnp.zeros_like(ones)], axis=0) * (mass / (width * n_blk))
    moments = jnp.concatenate([stack_three(moments), jnp.zeros((8, prep_width), F32)], axis=0)
    moment_ref[:, where] = moments.astype(BF16)


def write_pieces(n_blk, kin_ref, der_ref, last_ref, mass_ref, pred_ref, piece_ref, moment_ref):
    width = kin_ref.shape[1]
    total = jnp.zeros((6, prep_width), F32)
    for part in range(width // prep_width):
        where = pl.ds(part * prep_width, prep_width)
        stars = predicted_block(kin_ref, der_ref, last_ref, where, 0.0)
        pred_ref[:, where] = stars
        total = total + stars
    centre = jnp.sum(total, axis=1, keepdims=True) / width
    for part in range(width // prep_width):
        where = pl.ds(part * prep_width, prep_width)
        stars = pred_ref[:, where] - centre
        write_part(n_blk, width, stars, mass_ref[:, where], where, piece_ref, moment_ref)
    return centre


def write_listed(
    n_blk, parts, table_ref, centre, kin_ref, der_ref, last_ref, mass_ref, piece_ref, moment_ref
):
    blocks = prep_width // BLOCK
    for part in parts:
        places = [block_at(table_ref[6, part * blocks + index]) for index in range(blocks)]
        stars = [predicted_block(kin_ref, der_ref, last_ref, one, step_length) for one in places]
        stars = jnp.concatenate([one - centre for one in stars], axis=1)
        mass = jnp.concatenate([mass_ref[:, one] for one in places], axis=1)
        where = pl.ds(part * prep_width, prep_width)
        write_part(n_blk, kin_ref.shape[1], stars, mass, where, piece_ref, moment_ref)


def block_forces(blocks, parts, piece_ref, moment_ref):
    against = [target_pieces(stars) for stars in blocks]
    order = [(index, part) for index in range(len(blocks)) for part in parts]
    by_weight = [jnp.zeros((32, 2 * BLOCK), F32) for stars in blocks]
    by_radial = [jnp.zeros((32, 2 * BLOCK), F32) for stars in blocks]

    def meet(index, part):
        where = pl.ds(part * ahead_chunk, ahead_chunk)
        return jnp.dot(piece_ref[where, :], against[index], preferred_element_type=F32)

    def halves(value):
        high = value.astype(BF16)
        low = (value - high.astype(F32)).astype(BF16)
        return jnp.concatenate([high, low], axis=1)

    both = meet(*order[0])
    for turn, (index, part) in enumerate(order):
        ahead = meet(*order[turn + 1]) if turn + 1 < len(order) else None
        inverse = lax.rsqrt(both[:, :BLOCK])
        inverse_sq = inverse * inverse
        weight = inverse * inverse_sq
        radial = weight * (inverse_sq * both[:, BLOCK:])
        moments = moment_ref[:, pl.ds(part * ahead_chunk, ahead_chunk)]
        by_weight[index] += jnp.dot(moments, halves(weight), preferred_element_type=F32)
        by_radial[index] += jnp.dot(moments, halves(radial), preferred_element_type=F32)
        both = ahead

    def gather_up(value):
        value = value[0:8] + value[8:16] + value[16:24]
        return value[:, :BLOCK] + value[:, BLOCK:]

    results = []
    for index, stars in enumerate(blocks):
        on_weight, on_radial = gather_up(by_weight[index]), gather_up(by_radial[index])
        sums = on_weight[0:6] - stars * on_weight[6:7]
        pull = on_radial[0:3] - stars[0:3] * on_radial[6:7]
        gap = jnp.zeros((ROWS - 6, BLOCK), F32)
        results.append(jnp.concatenate([sums[0:3], sums[3:6] - 3.0 * pull, gap], axis=0))
    return results


def all_forces(begin, end, parts, stars_of, store, piece_ref, moment_ref):
    def some(first, size):
        blocks = [stars_of(first + index) for index in range(size)]
        results = block_forces(blocks, parts, piece_ref, moment_ref)
        for index, result in enumerate(results):
            store(first + index, result)

    pairs = (end - begin) // 2

    def two(pair, carry):
        some(begin + pair * 2, 2)
        return carry

    lax.fori_loop(0, pairs, two, 0)

    @pl.when(end > begin + pairs * 2)
    def _():
        some(begin + pairs * 2, 1)


def every_part(piece_ref):
    return list(range(piece_ref.shape[0] // ahead_chunk))


def pieces_kernel(
    n_blk, kin_ref, der_ref, last_ref, mass_ref, piece_ref, moment_ref, centre_ref, pred_ref
):
    centre = write_pieces(
        n_blk, kin_ref, der_ref, last_ref, mass_ref, pred_ref, piece_ref, moment_ref
    )
    centre_ref[...] = jnp.broadcast_to(centre, (6, BLOCK))


def early_parts():
    return early_chunks * ahead_chunk // prep_width


def early_pieces_kernel(
    n_blk, table_ref, kin_ref, der_ref, last_ref, mass_ref, centre_ref, piece_ref, moment_ref
):
    centre = centre_ref[...]
    parts = range(early_parts(), kin_ref.shape[1] // prep_width)
    piece_ref[pl.ds(0, early_chunks * ahead_chunk), :] = jnp.zeros(
        (early_chunks * ahead_chunk, piece_rows), BF16
    )
    moment_ref[:, pl.ds(0, early_chunks * ahead_chunk)] = jnp.zeros(
        (32, early_chunks * ahead_chunk), BF16
    )
    write_listed(
        n_blk, parts, table_ref, centre, kin_ref, der_ref, last_ref, mass_ref, piece_ref, moment_ref
    )


def few_moved(table_ref):
    return table_ref[2, 10] <= early_chunks * ahead_chunk // BLOCK


def early_forces_kernel(
    turn, table_ref, after_ref, target_ref, piece_ref, moment_ref, centre_ref, out_ref, *zero_refs
):
    out_ref[...] = jnp.zeros_like(out_ref)
    for zero_ref in zero_refs:
        zero_ref[...] = jnp.zeros_like(zero_ref)
    moved_end, end = table_ref[2, 9], table_ref[2, 8]
    begin = jnp.minimum(moved_end + turn * early_pair, end)
    last = turn == 2

    def number(index):
        if not last:
            return begin + index
        return jnp.where(index < end - begin, begin + index, index - (end - begin))

    def stars_of(index):
        place = number(index) if last else table_ref[4, number(index)]
        return target_ref[place][0:6] - centre_ref[...]

    def store(index, result):
        out_ref[number(index)] = result

    amount = end - begin + moved_end if last else jnp.minimum(early_pair, end - begin)

    @pl.when(few_moved(table_ref))
    def _():
        parts = every_part(piece_ref)[early_chunks:]
        all_forces(0, amount, parts, stars_of, store, piece_ref, moment_ref)


def first_forces_kernel(table_ref, target_ref, piece_ref, moment_ref, centre_ref, out_ref):
    out_ref[...] = jnp.zeros_like(out_ref)

    def stars_of(index):
        return target_ref[table_ref[3, index]][0:6] - centre_ref[...]

    def store(index, result):
        out_ref[index] = result

    all_forces(0, table_ref[2, 7], every_part(piece_ref), stars_of, store, piece_ref, moment_ref)


def flag_rows():
    rows = lax.broadcasted_iota(jnp.int32, (CAP * ROWS, BLOCK), 0)
    return jnp.bitwise_and(rows, ROWS - 1) == 6


def flagged_total_kernel(n_blk, n_rep, part_ref, out_ref):
    total = part_ref[0]
    for other in range(1, n_blk):
        total = total + part_ref[other]
    total = jnp.where(flag_rows(), 1.0, total)
    for other in range(n_rep):
        out_ref[other] = total


def middle_kernel(
    n_rep, table_ref, term_a, term_b, term_c, term_d, early_ref, target_ref,
    share_ref, next_ref, force_ref,
):
    force_ref[...] = term_a[...] + ((term_b[...] + term_c[...]) + term_d[...])
    own = jnp.concatenate([force_ref[table_ref[2, 4]], force_ref[table_ref[2, 5]]], axis=0)
    own = jnp.where(flag_rows(), 1.0, own)
    for other in range(n_rep):
        share_ref[other] = own

    def one(index, carry):
        place = table_ref[4, index]
        is_both = index < table_ref[2, 9]

        @pl.when(is_both)
        def _():
            head, deriv = target_ref[place], target_ref[place + 1][0:6]
            forces = force_ref[index][0:6]
            moved = correct(head[0:6], deriv, forces, head[6:7])
            ahead = predict(moved[:3], moved[3:], forces[:3], forces[3:], step_length)
            next_ref[index] = jnp.concatenate([ahead, head[6:8]], axis=0)

        @pl.when(jnp.logical_not(is_both))
        def _():
            next_ref[index] = target_ref[place]

        return carry

    lax.fori_loop(0, table_ref[2, 8], one, 0)


def place_forces(step, table_ref, force_ref, placed_ref):
    for number in range(placed_ref.shape[1] // BLOCK):
        code = table_ref[step, number]
        tile = force_ref[jnp.maximum(code, 0)]
        tile = tile * jnp.where(code >= 0, 1.0, 0.0)
        placed_ref[:, pl.ds(number * BLOCK, BLOCK)] = tile


def moved_part(step, where, placed_ref, kin_ref, der_ref, last_ref):
    time_now = step * step_length
    placed = placed_ref[:, where]
    forces, moved = placed[0:6], placed[6:7] > 0.5
    kin, der, last = kin_ref[:, where], der_ref[:, where], last_ref[:, where]
    interval = time_now - last
    predicted = predict(kin[:3], kin[3:], der[:3], der[3:], interval)
    corrected = correct(predicted, der, forces, interval)
    return (
        jnp.where(moved, corrected, kin),
        jnp.where(moved, forces, der),
        jnp.where(moved, time_now, last),
    )


def second_forces_kernel(
    n_blk, table_ref, force_ref, target_ref, early_a, early_b, early_c, centre_ref,
    kin_ref, der_ref, last_ref, mass_ref,
    out_ref, new_kin_ref, new_der_ref, new_last_ref, placed_ref, piece_ref, moment_ref,
):
    width = kin_ref.shape[1]
    place_forces(0, table_ref, force_ref, placed_ref)
    for part in range(width // prep_width):
        where = pl.ds(part * prep_width, prep_width)
        kin, der, last = moved_part(0, where, placed_ref, kin_ref, der_ref, last_ref)
        new_kin_ref[:, where] = kin
        new_der_ref[:, where] = der
        new_last_ref[:, where] = last
    centre = centre_ref[...]
    few = few_moved(table_ref)

    def listed(parts):
        write_listed(
            n_blk, parts, table_ref, centre, new_kin_ref, new_der_ref, new_last_ref, mass_ref,
            piece_ref, moment_ref,
        )

    listed(range(early_parts()))

    @pl.when(jnp.logical_not(few))
    def _():
        listed(range(early_parts(), width // prep_width))

    out_ref[...] = jnp.zeros_like(out_ref)

    def stars_of(index):
        return target_ref[index][0:6] - centre

    def store(index, result):
        place = table_ref[4, index]
        out_ref[(place // 4) * 2 + place % 2] = result

    def store_with_early(index, result):
        store(index, result + ((early_a[index] + early_b[index]) + early_c[index]))

    parts = every_part(piece_ref)

    @pl.when(few)
    def _():
        all_forces(
            0, table_ref[2, 8], parts[:early_chunks], stars_of, store_with_early, piece_ref, moment_ref
        )

    @pl.when(jnp.logical_not(few))
    def _():
        all_forces(0, table_ref[2, 8], parts, stars_of, store, piece_ref, moment_ref)


def last_kernel(
    table_ref, force_ref, kin_ref, der_ref, last_ref, new_kin_ref, new_der_ref, placed_ref
):
    place_forces(1, table_ref, force_ref, placed_ref)
    for part in range(kin_ref.shape[1] // prep_width):
        where = pl.ds(part * prep_width, prep_width)
        kin, der, last = moved_part(1, where, placed_ref, kin_ref, der_ref, last_ref)
        new_kin_ref[:, where] = kin
        new_der_ref[:, where] = der


def shape_of(*sizes):
    return jax.ShapeDtypeStruct(sizes, F32)


def run_kernel(body, scalars, arrays, out_shape, scratch=(), after=None):
    scalar_specs = [pl.BlockSpec(memory_space=pltpu.SMEM)] * len(scalars)
    if after is not None:
        arrays = [after, *arrays]
    return pl.pallas_call(
        body,
        out_shape=out_shape,
        in_specs=scalar_specs
        + [pl.BlockSpec(memory_space=pltpu.VMEM)] * len(arrays),
        out_specs=jax.tree.map(lambda leaf: pl.BlockSpec(memory_space=pltpu.VMEM), out_shape),
        scratch_shapes=list(scratch),
        compiler_params=pltpu.CompilerParams(vmem_limit_bytes=32 * 2**20),
    )(*scalars, *arrays)


def plain_steps(kinematics, derivatives, mass, last, block_list, block_count):
    width = kinematics.shape[1]
    n_blk = lax.axis_size("blk")
    n_rep = lax.axis_size("rep")
    flat_list = block_list.reshape(-1)
    flat_count = block_count.reshape(-1)
    targets = run_kernel(
        functools.partial(targets_kernel, 0, n_blk, n_rep),
        [flat_list],
        [kinematics, derivatives, last],
        shape_of(n_blk, CAP * ROWS, BLOCK),
    )
    for step in range(STEPS):
        gathered = lax.all_to_all(targets, "blk", 0, 0, tiled=True)
        partial_forces = run_kernel(
            functools.partial(forces_kernel, step, n_blk, n_rep),
            [flat_count],
            [gathered.reshape(n_blk * CAP, ROWS, BLOCK), kinematics, derivatives, last, mass],
            shape_of(n_blk * CAP, ROWS, BLOCK),
            [
                pltpu.VMEM((6, width), F32),
                pltpu.VMEM((width, piece_rows), BF16),
                pltpu.VMEM((32, width), BF16),
            ],
        )
        partial_forces = partial_forces.reshape(n_blk, CAP * ROWS, BLOCK)
        spread = lax.all_to_all(partial_forces, "blk", 0, 0, tiled=True)
        mine = run_kernel(
            functools.partial(total_kernel, n_blk, n_rep),
            [],
            [spread],
            shape_of(n_rep, CAP * ROWS, BLOCK),
        )
        forces = lax.all_to_all(mine, "rep", 0, 0, tiled=True)
        out_shape = [shape_of(6, width), shape_of(6, width), shape_of(1, width)]
        if step + 1 < STEPS:
            out_shape.append(shape_of(n_blk, CAP * ROWS, BLOCK))
        kinematics, derivatives, last, *rest = run_kernel(
            functools.partial(update_kernel, step, n_blk, n_rep),
            [flat_list, flat_count],
            [forces.reshape(n_rep * CAP, ROWS, BLOCK), kinematics, derivatives, last],
            out_shape,
        )
        if rest:
            targets = rest[0]
    return (kinematics, derivatives)


def from_partner(value, distance):
    n_blk = lax.axis_size("blk")
    return lax.ppermute(value, "blk", [(i, i ^ distance) for i in range(n_blk)])


def shared_steps(kinematics, derivatives, mass, last, table, gathered, pieces, early_pieces):
    width = kinematics.shape[1]
    n_blk = lax.axis_size("blk")
    n_rep = lax.axis_size("rep")
    piece_scratch = [pltpu.VMEM((width, piece_rows), BF16), pltpu.VMEM((32, width), BF16)]
    partial_forces = run_kernel(
        first_forces_kernel,
        [table],
        [gathered, *pieces],
        shape_of(first_slots, ROWS, BLOCK),
    )
    value = partial_forces.reshape(first_slots * ROWS, BLOCK)
    value = value + from_partner(value, 1)

    def early_forces(turn, after, target, *zeros):
        return run_kernel(
            functools.partial(early_forces_kernel, turn),
            [table],
            [target, *early_pieces, pieces[2]],
            [shape_of(n_rep, ROWS, BLOCK), *zeros],
            after=after,
        )

    first_early, zero = early_forces(0, value, gathered, shape_of(first_slots * ROWS, BLOCK))
    value = (value + from_partner(value, 2)) + zero
    early = [first_early, *early_forces(1, value, gathered)]
    terms = [value] + [from_partner(value, distance) for distance in (4, 12, 8)]
    terms = [term.reshape(first_slots, ROWS, BLOCK) for term in terms]
    shares, targets = run_kernel(
        functools.partial(middle_kernel, n_rep),
        [table],
        [*terms, early[1], gathered],
        [shape_of(n_rep, 2 * ROWS, BLOCK), shape_of(n_rep, ROWS, BLOCK)],
        [pltpu.VMEM((first_slots, ROWS, BLOCK), F32)],
    )
    early += early_forces(2, targets, targets)
    shares = lax.all_to_all(shares, "rep", 0, 0, tiled=True)
    shard = [kinematics, derivatives, last, mass]
    partial_forces, kinematics, derivatives, last = run_kernel(
        functools.partial(second_forces_kernel, n_blk),
        [table],
        [shares.reshape(n_rep * 2, ROWS, BLOCK), targets, *early, pieces[2], *shard],
        [shape_of(n_blk * 2, ROWS, BLOCK), shape_of(6, width), shape_of(6, width), shape_of(1, width)],
        [pltpu.VMEM((ROWS, width), F32)] + piece_scratch,
    )
    spread = lax.all_to_all(
        partial_forces.reshape(n_blk, 2 * ROWS, BLOCK), "blk", 0, 0, tiled=True
    )
    mine = run_kernel(
        functools.partial(flagged_total_kernel, n_blk, n_rep),
        [],
        [spread],
        shape_of(n_rep, 2 * ROWS, BLOCK),
    )
    shares = lax.all_to_all(mine, "rep", 0, 0, tiled=True)
    return run_kernel(
        last_kernel,
        [table],
        [shares.reshape(n_rep * 2, ROWS, BLOCK), kinematics, derivatives, last],
        [shape_of(6, width), shape_of(6, width)],
        [pltpu.VMEM((ROWS, width), F32)],
    )


def per_device(kinematics, derivatives, masses, last_time, block_list, block_count):
    width = kinematics.shape[1]
    n_blk = lax.axis_size("blk")
    n_rep = lax.axis_size("rep")
    mass = masses.reshape(1, width)
    last = last_time.reshape(1, width)
    table, targets = run_kernel(
        functools.partial(share_kernel, n_blk, n_rep),
        [],
        [block_list.transpose(0, 1, 3, 2), block_count, kinematics, derivatives, last],
        [jax.ShapeDtypeStruct((8, BLOCK), jnp.int32), shape_of(n_blk, 4 * ROWS, BLOCK)],
    )
    gathered = lax.all_to_all(targets, "blk", 0, 0, tiled=True)
    gathered = gathered.reshape(n_blk * 4, ROWS, BLOCK)
    piece_shapes = [
        jax.ShapeDtypeStruct((width, piece_rows), BF16),
        jax.ShapeDtypeStruct((32, width), BF16),
        shape_of(6, BLOCK),
    ]
    shard = [kinematics, derivatives, last, mass]
    pieces = run_kernel(
        functools.partial(pieces_kernel, n_blk),
        [],
        shard,
        piece_shapes,
        [pltpu.VMEM((6, width), F32)],
    )
    early_pieces = run_kernel(
        functools.partial(early_pieces_kernel, n_blk),
        [table],
        [*shard, pieces[2]],
        piece_shapes[:2],
    )
    return tuple(
        lax.cond(
            table[2, 0] > 0,
            lambda: tuple(
                shared_steps(
                    kinematics, derivatives, mass, last, table, gathered, pieces, early_pieces
                )
            ),
            lambda: tuple(
                plain_steps(kinematics, derivatives, mass, last, block_list, block_count)
            ),
        )
    )


def solution(mesh):
    return jax.shard_map(
        per_device,
        mesh=mesh,
        in_specs=(P(None, "blk"), P(None, "blk"), P("blk"), P("blk"), P(), P()),
        out_specs=(P(None, "blk"), P(None, "blk")),
        check_vma=False,
    )
```

```python
import functools

import jax
import jax.numpy as jnp
from jax import lax
from jax.experimental import pallas as pl
from jax.experimental.pallas import tpu as pltpu
from jax.sharding import PartitionSpec as P

BLOCK = 128
CAP = 2
STEPS = 2
ROWS = 8
F32 = jnp.float32
BF16 = jnp.bfloat16

step_length = 0.125
softening = 0.0025
grid_shift = 1.5 * 2.0**16
piece_rows = 128
chunk = 256
ahead_chunk = 1024
early_chunks = 2
early_pair = 2
prep_width = 512
first_slots = 12


def predict(position, velocity, acceleration, jerk_old, interval):
    new_position = position + interval * (
        velocity + interval * (acceleration * 0.5 + interval * jerk_old / 6.0)
    )
    new_velocity = velocity + interval * (acceleration + interval * jerk_old * 0.5)
    return jnp.concatenate([new_position, new_velocity], axis=0)


def correct(predicted, old_deriv, forces, interval):
    change = old_deriv[:3] - forces[:3]
    second_term = -6.0 * change - interval * (4.0 * old_deriv[3:] + 2.0 * forces[3:])
    third_term = 12.0 * change + 6.0 * interval * (old_deriv[3:] + forces[3:])
    new_position = predicted[:3] + interval * interval * (second_term / 24.0 + third_term / 120.0)
    new_velocity = predicted[3:] + interval * (second_term / 6.0 + third_term / 24.0)
    return jnp.concatenate([new_position, new_velocity], axis=0)


def round_short(value):
    return value.astype(BF16).astype(F32)


def split_three(value):
    high = round_short(value)
    rest = value - high
    middle = round_short(rest)
    return high, middle, rest - middle


def stack_three(value):
    return jnp.concatenate(split_three(value), axis=0)


def star_pieces(stars):
    position, velocity = stars[0:3], stars[3:6]
    coarse = (position + grid_shift) - grid_shift
    coarse_a = round_short(coarse)
    coarse_b = coarse - coarse_a
    fine = position - coarse
    fine_a = round_short(fine)
    fine_b = round_short(fine - fine_a)
    fine = fine_a + fine_b
    square = jnp.sum(coarse * coarse, axis=0, keepdims=True)
    cross = jnp.sum(2.0 * coarse * fine + fine * fine, axis=0, keepdims=True)
    mixed = jnp.sum(position * velocity, axis=0, keepdims=True)
    return coarse_a, coarse_b, fine_a, fine_b, square, cross, mixed


def source_pieces(stars):
    ca, cb, fa, fb, square, cross, mixed = star_pieces(stars)
    va, vb, vc = split_three(stars[3:6])
    width = stars.shape[1]
    one = jnp.ones((3, width), F32)
    rows = [ca, ca, cb, cb, stack_three(square), one, jnp.zeros((6, width), F32)]
    rows += [ca, ca, cb, cb, fa, fa, fb, fb, fa, fa, stack_three(cross), one]
    rows += [va, va, va, vb, vb, vc, stack_three(mixed), one]
    rows += [jnp.zeros((piece_rows - 84, width), F32)]
    return jnp.concatenate(rows, axis=0)


def target_pieces(stars):
    ca, cb, fa, fb, square, cross, mixed = star_pieces(stars)
    va, vb, vc = split_three(stars[3:6])
    xa, xb, xc = split_three(stars[0:3])
    width = stars.shape[1]
    one = jnp.ones((3, width), F32)
    zero = jnp.zeros((3, width), F32)
    da, db = -2.0 * ca, -2.0 * cb
    ea, eb = -2.0 * fa, -2.0 * fb
    tail = jnp.zeros((piece_rows - 84, width), F32)
    radius = [da, db, da, db, one, stack_three(square), zero, zero]
    radius += [ea, eb, ea, eb, da, db, da, db, ea, eb, one, stack_three(cross + softening)]
    radius += [zero] * 8 + [tail]
    moving = [-va, -vb, -va, -vb, zero, zero, zero, zero]
    moving += [-vc, zero, zero, zero, -va, -vb, -va, zero, zero, zero, zero, zero]
    moving += [-xa, -xb, -xc, -xa, -xb, -xa, one, stack_three(mixed), tail]
    both = [jnp.concatenate(radius, axis=0), jnp.concatenate(moving, axis=0)]
    return jnp.concatenate(both, axis=1).astype(BF16)


def block_at(number):
    return pl.ds(pl.multiple_of(number * BLOCK, BLOCK), BLOCK)


def predicted_block(kin_ref, der_ref, last_ref, where, time_now):
    kin, der = kin_ref[:, where], der_ref[:, where]
    return predict(kin[:3], kin[3:], der[:3], der[3:], time_now - last_ref[:, where])


def list_place(step, blk, rep, slot, n_blk, n_rep):
    return ((step * n_blk + blk) * n_rep + rep) * CAP + slot


def write_targets(step, n_blk, n_rep, list_ref, kin_ref, der_ref, last_ref, out_ref):
    blk, rep = lax.axis_index("blk"), lax.axis_index("rep")
    rows = []
    for slot in range(CAP):
        number = list_ref[list_place(step, blk, rep, slot, n_blk, n_rep)]
        rows.append(predicted_block(kin_ref, der_ref, last_ref, block_at(number), step * step_length))
        rows.append(jnp.zeros((ROWS - 6, BLOCK), F32))
    mine = jnp.concatenate(rows, axis=0)
    for other in range(n_blk):
        out_ref[other] = mine


def targets_kernel(step, n_blk, n_rep, list_ref, kin_ref, der_ref, last_ref, out_ref):
    write_targets(step, n_blk, n_rep, list_ref, kin_ref, der_ref, last_ref, out_ref)


def forces_kernel(
    step, n_blk, n_rep, count_ref, target_ref, kin_ref, der_ref, last_ref, mass_ref,
    out_ref, pred_ref, piece_ref, moment_ref,
):
    rep = lax.axis_index("rep")
    width = kin_ref.shape[1]
    total = jnp.zeros((6, prep_width), F32)
    for part in range(width // prep_width):
        where = pl.ds(part * prep_width, prep_width)
        stars = predicted_block(kin_ref, der_ref, last_ref, where, step * step_length)
        pred_ref[:, where] = stars
        total = total + stars
    centre = jnp.sum(total, axis=1, keepdims=True) / width
    for part in range(width // prep_width):
        where = pl.ds(part * prep_width, prep_width)
        stars = pred_ref[:, where] - centre
        piece_ref[where, :] = source_pieces(stars).T.astype(BF16)
        scaled = mass_ref[:, where] / (width * n_blk)
        ones = jnp.ones((1, prep_width), F32)
        moments = jnp.concatenate([stars, ones, jnp.zeros_like(ones)], axis=0) * scaled
        moments = jnp.concatenate([stack_three(moments), jnp.zeros((8, prep_width), F32)], axis=0)
        moment_ref[:, where] = moments.astype(BF16)

    def one_slot(place, carry):
        blk = place // CAP
        slot = place % CAP
        active = slot < count_ref[(step * n_blk + blk) * n_rep + rep]

        @pl.when(active)
        def _():
            stars = target_ref[place][0:6] - centre
            against = target_pieces(stars)
            acc = jnp.zeros((32, 2 * BLOCK), F32)
            for part in range(width // chunk):
                where = pl.ds(part * chunk, chunk)
                both = jnp.dot(piece_ref[where, :], against, preferred_element_type=F32)
                inverse = lax.rsqrt(both[:, :BLOCK])
                inverse_sq = inverse * inverse
                weight = inverse * inverse_sq
                radial = weight * (inverse_sq * both[:, BLOCK:])
                pair = jnp.concatenate([weight, radial], axis=1)
                high = pair.astype(BF16)
                low = (pair - high.astype(F32)).astype(BF16)
                moments = moment_ref[:, where]
                acc = acc + jnp.dot(moments, high, preferred_element_type=F32)
                acc = acc + jnp.dot(moments, low, preferred_element_type=F32)
            acc = acc[0:8] + acc[8:16] + acc[16:24]
            by_weight, by_radial = acc[:, :BLOCK], acc[:, BLOCK:]
            sums = by_weight[0:6] - stars * by_weight[6:7]
            pull = by_radial[0:3] - stars[0:3] * by_radial[6:7]
            out_ref[place] = jnp.concatenate(
                [sums[0:3], sums[3:6] - 3.0 * pull, jnp.zeros((ROWS - 6, BLOCK), F32)], axis=0
            )

        @pl.when(jnp.logical_not(active))
        def _():
            out_ref[place] = jnp.zeros((ROWS, BLOCK), F32)

        return carry

    lax.fori_loop(0, n_blk * CAP, one_slot, 0)


def total_kernel(n_blk, n_rep, part_ref, out_ref):
    total = part_ref[0]
    for other in range(1, n_blk):
        total = total + part_ref[other]
    for other in range(n_rep):
        out_ref[other] = total


def update_kernel(
    step, n_blk, n_rep, list_ref, count_ref, force_ref, kin_ref, der_ref, last_ref,
    new_kin_ref, new_der_ref, new_last_ref, *next_refs,
):
    blk = lax.axis_index("blk")
    time_now = step * step_length
    new_kin_ref[...] = kin_ref[...]
    new_der_ref[...] = der_ref[...]
    new_last_ref[...] = last_ref[...]

    def one_slot(place, carry):
        rep = place // CAP
        slot = place % CAP

        @pl.when(slot < count_ref[(step * n_blk + blk) * n_rep + rep])
        def _():
            number = list_ref[list_place(step, blk, rep, slot, n_blk, n_rep)]
            where = block_at(number)
            predicted = predicted_block(kin_ref, der_ref, last_ref, where, time_now)
            forces = force_ref[place][0:6]
            interval = time_now - last_ref[:, where]
            new_kin_ref[:, where] = correct(predicted, der_ref[:, where], forces, interval)
            new_der_ref[:, where] = forces
            new_last_ref[:, where] = jnp.full((1, BLOCK), time_now, F32)

        return carry

    lax.fori_loop(0, n_rep * CAP, one_slot, 0)
    if next_refs:
        write_targets(
            step + 1, n_blk, n_rep, list_ref, new_kin_ref, new_der_ref, new_last_ref, next_refs[0]
        )


def lane_iota(rows):
    return lax.broadcasted_iota(jnp.int32, (rows, BLOCK), 1)


def active_rows(n_blk, n_rep, list_ref, count_ref):
    per_row = BLOCK // n_rep
    parts = BLOCK * n_rep // BLOCK // 4
    lanes = lane_iota(n_blk)
    steps = []
    for step in range(STEPS):
        counted = count_ref[step]
        tiled = []
        for slot in range(CAP):
            listed = jnp.where(counted > slot, list_ref[step, :, slot, :], -1)
            tiled.append(jnp.concatenate([listed] * per_row, axis=1))
        hits = []
        for part in range(parts):
            number = lanes // n_rep + part * per_row
            hit = (tiled[0] == number) | (tiled[1] == number)
            hits.append(jnp.where(hit, 1.0, 0.0))
        steps.append(jnp.concatenate(hits, axis=1))
    hits = jnp.concatenate(steps, axis=0).astype(BF16)
    width = parts * BLOCK
    rows = lax.broadcasted_iota(jnp.int32, (width, BLOCK), 0) // n_rep
    spread = jnp.where(rows == lax.broadcasted_iota(jnp.int32, (width, BLOCK), 1), 1.0, 0.0)
    return jnp.dot(hits, spread.astype(BF16), preferred_element_type=F32)


def share_blocks(n_blk, n_rep, list_ref, count_ref, table_ref):
    blk, rep = lax.axis_index("blk"), lax.axis_index("rep")
    flags = active_rows(n_blk, n_rep, list_ref, count_ref)
    first, second = flags[:n_blk], flags[n_blk:]
    in_both = first * second
    kinds = [in_both, first - in_both, second - in_both]
    earlier = lax.broadcasted_iota(jnp.int32, (BLOCK, BLOCK), 0) < lax.broadcasted_iota(
        jnp.int32, (BLOCK, BLOCK), 1
    )
    earlier = jnp.where(earlier, 1.0, 0.0).astype(BF16)
    above = lax.broadcasted_iota(jnp.int32, (n_blk, n_blk), 0) > lax.broadcasted_iota(
        jnp.int32, (n_blk, n_blk), 1
    )
    above = jnp.where(above, 1.0, 0.0).astype(BF16)
    own_row = lax.broadcasted_iota(jnp.int32, (n_blk, BLOCK), 0) == blk
    lanes = lane_iota(1)
    order = lanes * n_rep + rep
    start = jnp.zeros((1, 1), F32)
    fits = jnp.ones((1, 1), jnp.bool_)
    own_kind, own_place, own_rank, finish, owner = [], [], [], [], []
    for kind in kinds:
        short = kind.astype(BF16)
        rank = jnp.dot(short, earlier, preferred_element_type=F32)
        before = jnp.dot(above, short, preferred_element_type=F32)
        before = jnp.sum(before, axis=1, keepdims=True) + start
        amount = jnp.sum(kind, axis=1, keepdims=True)
        fits = fits & (jnp.max(amount, axis=0, keepdims=True) <= n_rep)
        ends = (before + amount).astype(jnp.int32)
        owner.append(jnp.sum(jnp.where(ends <= order, 1, 0), axis=0, keepdims=True))
        place = jnp.sum(jnp.where(own_row, before + rank, 0.0), axis=0, keepdims=True)
        own_place.append(place.astype(jnp.int32))
        own_rank.append(jnp.sum(jnp.where(own_row, rank, 0.0), axis=0, keepdims=True))
        own_kind.append(jnp.sum(jnp.where(own_row, kind, 0.0), axis=0, keepdims=True) > 0.5)
        finish.append((jnp.max(before + amount, axis=0, keepdims=True)).astype(jnp.int32))
        if len(finish) == 1:
            start = jnp.sum(amount, axis=0, keepdims=True)
    both_end = finish[0]
    total = [jnp.maximum(finish[0], finish[1]), jnp.maximum(finish[0], finish[2])]
    fits = fits & (total[0] <= n_rep * first_slots) & (total[1] <= n_rep * n_rep)
    handler = [jnp.bitwise_and(place, n_rep - 1) for place in own_place]
    home = []
    for step in range(STEPS):
        code = jnp.where(own_kind[0], handler[0] * 2, -1)
        home.append(jnp.where(own_kind[1 + step], handler[1 + step] * 2 + 1, code))
    places = []
    for step in range(STEPS):
        is_both = order < both_end
        places.append(jnp.where(is_both, owner[0] * 4, owner[1 + step] * 4 + 2 + step))
    scalars = jnp.where(lanes == 0, jnp.where(fits, 1, 0), 0)
    numbers = []
    for index in range(3):
        mine = own_kind[index] & (handler[index] == rep)
        numbers.append(jnp.sum(jnp.where(mine, lanes.astype(F32), 0.0)).astype(jnp.int32))
        spot = jnp.max(jnp.where(mine, own_place[index] // n_rep, 0), axis=1, keepdims=True)
        scalars = jnp.where(lanes == 4 + index, spot, scalars)
    for step in range(STEPS):
        amount = (total[step] - rep + n_rep - 1) // n_rep
        scalars = jnp.where(lanes == 7 + step, amount, scalars)
    amount = (both_end - rep + n_rep - 1) // n_rep
    scalars = jnp.where(lanes == 9, amount, scalars)
    moved = own_kind[0] | own_kind[1]
    moved_amount = jnp.sum(jnp.where(moved, 1, 0), axis=1, keepdims=True)
    scalars = jnp.where(lanes == 10, moved_amount, scalars)
    moved_rank = (own_rank[0] + own_rank[1]).astype(jnp.int32)
    spots = jnp.where(moved, moved_rank, moved_amount + lanes - moved_rank)
    listed = (prep_width // BLOCK) * 8
    numbers_down = lax.broadcasted_iota(jnp.int32, (listed, BLOCK), 0)
    spots_down = jnp.sum(jnp.where(numbers_down == lanes, spots, 0), axis=1, keepdims=True)
    members = jnp.sum(jnp.where(spots_down == lanes, numbers_down, 0), axis=0, keepdims=True)
    gap = jnp.zeros((1, BLOCK), jnp.int32)
    rows = [home[0], home[1], scalars, places[0], places[1], spots, members, gap]
    table_ref[...] = jnp.concatenate(rows, axis=0)
    return numbers


def share_kernel(n_blk, n_rep, list_ref, count_ref, kin_ref, der_ref, last_ref, table_ref, out_ref):
    numbers = share_blocks(n_blk, n_rep, list_ref, count_ref, table_ref)
    where = [block_at(number) for number in numbers]
    gap = jnp.zeros((2, BLOCK), F32)
    rows = [
        predicted_block(kin_ref, der_ref, last_ref, where[0], 0.0),
        0.0 - last_ref[:, where[0]],
        gap[0:1],
        der_ref[:, where[0]],
        gap,
        predicted_block(kin_ref, der_ref, last_ref, where[1], 0.0),
        gap,
        predicted_block(kin_ref, der_ref, last_ref, where[2], step_length),
        gap,
    ]
    mine = jnp.concatenate(rows, axis=0)
    for other in range(n_blk):
        out_ref[other] = mine


def write_part(n_blk, width, stars, mass, where, piece_ref, moment_ref):
    piece_ref[where, :] = source_pieces(stars).T.astype(BF16)
    ones = jnp.ones((1, prep_width), F32)
    moments = jnp.concatenate([stars, ones, jnp.zeros_like(ones)], axis=0) * (mass / (width * n_blk))
    moments = jnp.concatenate([stack_three(moments), jnp.zeros((8, prep_width), F32)], axis=0)
    moment_ref[:, where] = moments.astype(BF16)


def write_pieces(n_blk, kin_ref, der_ref, last_ref, mass_ref, pred_ref, piece_ref, moment_ref):
    width = kin_ref.shape[1]
    total = jnp.zeros((6, prep_width), F32)
    for part in range(width // prep_width):
        where = pl.ds(part * prep_width, prep_width)
        stars = predicted_block(kin_ref, der_ref, last_ref, where, 0.0)
        pred_ref[:, where] = stars
        total = total + stars
    centre = jnp.sum(total, axis=1, keepdims=True) / width
    for part in range(width // prep_width):
        where = pl.ds(part * prep_width, prep_width)
        stars = pred_ref[:, where] - centre
        write_part(n_blk, width, stars, mass_ref[:, where], where, piece_ref, moment_ref)
    return centre


def write_listed(
    n_blk, parts, table_ref, centre, kin_ref, der_ref, last_ref, mass_ref, piece_ref, moment_ref
):
    blocks = prep_width // BLOCK
    for part in parts:
        places = [block_at(table_ref[6, part * blocks + index]) for index in range(blocks)]
        stars = [predicted_block(kin_ref, der_ref, last_ref, one, step_length) for one in places]
        stars = jnp.concatenate([one - centre for one in stars], axis=1)
        mass = jnp.concatenate([mass_ref[:, one] for one in places], axis=1)
        where = pl.ds(part * prep_width, prep_width)
        write_part(n_blk, kin_ref.shape[1], stars, mass, where, piece_ref, moment_ref)


def block_forces(blocks, parts, piece_ref, moment_ref):
    against = [target_pieces(stars) for stars in blocks]
    order = [(index, part) for index in range(len(blocks)) for part in parts]
    by_weight = [jnp.zeros((32, 2 * BLOCK), F32) for stars in blocks]
    by_radial = [jnp.zeros((32, 2 * BLOCK), F32) for stars in blocks]

    def meet(index, part):
        where = pl.ds(part * ahead_chunk, ahead_chunk)
        return jnp.dot(piece_ref[where, :], against[index], preferred_element_type=F32)

    def halves(value):
        high = value.astype(BF16)
        low = (value - high.astype(F32)).astype(BF16)
        return jnp.concatenate([high, low], axis=1)

    both = meet(*order[0])
    for turn, (index, part) in enumerate(order):
        ahead = meet(*order[turn + 1]) if turn + 1 < len(order) else None
        inverse = lax.rsqrt(both[:, :BLOCK])
        inverse_sq = inverse * inverse
        weight = inverse * inverse_sq
        radial = weight * (inverse_sq * both[:, BLOCK:])
        moments = moment_ref[:, pl.ds(part * ahead_chunk, ahead_chunk)]
        by_weight[index] += jnp.dot(moments, halves(weight), preferred_element_type=F32)
        by_radial[index] += jnp.dot(moments, halves(radial), preferred_element_type=F32)
        both = ahead

    def gather_up(value):
        value = value[0:8] + value[8:16] + value[16:24]
        return value[:, :BLOCK] + value[:, BLOCK:]

    results = []
    for index, stars in enumerate(blocks):
        on_weight, on_radial = gather_up(by_weight[index]), gather_up(by_radial[index])
        sums = on_weight[0:6] - stars * on_weight[6:7]
        pull = on_radial[0:3] - stars[0:3] * on_radial[6:7]
        gap = jnp.zeros((ROWS - 6, BLOCK), F32)
        results.append(jnp.concatenate([sums[0:3], sums[3:6] - 3.0 * pull, gap], axis=0))
    return results


def all_forces(begin, end, parts, stars_of, store, piece_ref, moment_ref):
    def some(first, size):
        blocks = [stars_of(first + index) for index in range(size)]
        results = block_forces(blocks, parts, piece_ref, moment_ref)
        for index, result in enumerate(results):
            store(first + index, result)

    pairs = (end - begin) // 2

    def two(pair, carry):
        some(begin + pair * 2, 2)
        return carry

    lax.fori_loop(0, pairs, two, 0)

    @pl.when(end > begin + pairs * 2)
    def _():
        some(begin + pairs * 2, 1)


def every_part(piece_ref):
    return list(range(piece_ref.shape[0] // ahead_chunk))


def pieces_kernel(
    n_blk, kin_ref, der_ref, last_ref, mass_ref, piece_ref, moment_ref, centre_ref, pred_ref
):
    centre = write_pieces(
        n_blk, kin_ref, der_ref, last_ref, mass_ref, pred_ref, piece_ref, moment_ref
    )
    centre_ref[...] = jnp.broadcast_to(centre, (6, BLOCK))


def early_parts():
    return early_chunks * ahead_chunk // prep_width


def early_pieces_kernel(
    n_blk, table_ref, kin_ref, der_ref, last_ref, mass_ref, centre_ref, piece_ref, moment_ref
):
    centre = centre_ref[...]
    parts = range(early_parts(), kin_ref.shape[1] // prep_width)
    piece_ref[pl.ds(0, early_chunks * ahead_chunk), :] = jnp.zeros(
        (early_chunks * ahead_chunk, piece_rows), BF16
    )
    moment_ref[:, pl.ds(0, early_chunks * ahead_chunk)] = jnp.zeros(
        (32, early_chunks * ahead_chunk), BF16
    )
    write_listed(
        n_blk, parts, table_ref, centre, kin_ref, der_ref, last_ref, mass_ref, piece_ref, moment_ref
    )


def late_chunks(table_ref, chunks):
    needed = (table_ref[2, 10] * BLOCK + ahead_chunk - 1) // ahead_chunk
    return jnp.minimum(jnp.maximum(needed, early_chunks), chunks)


def early_forces_kernel(
    turn, table_ref, after_ref, target_ref, piece_ref, moment_ref, centre_ref, out_ref, *more_refs
):
    out_ref[...] = jnp.zeros_like(out_ref)
    last = turn == 2
    if last:
        write_next_targets(table_ref, after_ref, target_ref, more_refs[0])
        target_ref = more_refs[0]
    else:
        for zero_ref in more_refs:
            zero_ref[...] = jnp.zeros_like(zero_ref)
    moved_end, end = table_ref[2, 9], table_ref[2, 8]
    begin = jnp.minimum(moved_end + turn * early_pair, end)

    def number(index):
        if not last:
            return begin + index
        return jnp.where(index < end - begin, begin + index, index - (end - begin))

    def stars_of(index):
        place = number(index) if last else table_ref[4, number(index)]
        return target_ref[place][0:6] - centre_ref[...]

    def store(index, result):
        out_ref[number(index)] = result

    amount = end - begin + moved_end if last else jnp.minimum(early_pair, end - begin)

    parts = every_part(piece_ref)
    late = late_chunks(table_ref, len(parts))

    for split in range(early_chunks, len(parts)):

        @pl.when(late == split)
        def _(split=split):
            all_forces(0, amount, parts[split:], stars_of, store, piece_ref, moment_ref)


def first_forces_kernel(table_ref, target_ref, piece_ref, moment_ref, centre_ref, out_ref):
    out_ref[...] = jnp.zeros_like(out_ref)

    def stars_of(index):
        return target_ref[table_ref[3, index]][0:6] - centre_ref[...]

    def store(index, result):
        out_ref[index] = result

    all_forces(0, table_ref[2, 7], every_part(piece_ref), stars_of, store, piece_ref, moment_ref)


def flag_rows():
    rows = lax.broadcasted_iota(jnp.int32, (CAP * ROWS, BLOCK), 0)
    return jnp.bitwise_and(rows, ROWS - 1) == 6


def flagged_total_kernel(n_blk, n_rep, part_ref, out_ref):
    total = part_ref[0]
    for other in range(1, n_blk):
        total = total + part_ref[other]
    total = jnp.where(flag_rows(), 1.0, total)
    for other in range(n_rep):
        out_ref[other] = total


def middle_kernel(
    n_rep, table_ref, term_a, term_b, term_c, term_d, early_ref, share_ref, force_ref
):
    force_ref[...] = term_a[...] + ((term_b[...] + term_c[...]) + term_d[...])
    own = jnp.concatenate([force_ref[table_ref[2, 4]], force_ref[table_ref[2, 5]]], axis=0)
    own = jnp.where(flag_rows(), 1.0, own)
    for other in range(n_rep):
        share_ref[other] = own


def write_next_targets(table_ref, force_ref, target_ref, next_ref):
    def one(index, carry):
        place = table_ref[4, index]
        is_both = index < table_ref[2, 9]

        @pl.when(is_both)
        def _():
            head, deriv = target_ref[place], target_ref[place + 1][0:6]
            forces = force_ref[index][0:6]
            moved = correct(head[0:6], deriv, forces, head[6:7])
            ahead = predict(moved[:3], moved[3:], forces[:3], forces[3:], step_length)
            next_ref[index] = jnp.concatenate([ahead, head[6:8]], axis=0)

        @pl.when(jnp.logical_not(is_both))
        def _():
            next_ref[index] = target_ref[place]

        return carry

    lax.fori_loop(0, table_ref[2, 8], one, 0)


def place_forces(step, table_ref, force_ref, placed_ref):
    for number in range(placed_ref.shape[1] // BLOCK):
        code = table_ref[step, number]
        tile = force_ref[jnp.maximum(code, 0)]
        tile = tile * jnp.where(code >= 0, 1.0, 0.0)
        placed_ref[:, pl.ds(number * BLOCK, BLOCK)] = tile


def moved_part(step, where, placed_ref, kin_ref, der_ref, last_ref):
    time_now = step * step_length
    placed = placed_ref[:, where]
    forces, moved = placed[0:6], placed[6:7] > 0.5
    kin, der, last = kin_ref[:, where], der_ref[:, where], last_ref[:, where]
    interval = time_now - last
    predicted = predict(kin[:3], kin[3:], der[:3], der[3:], interval)
    corrected = correct(predicted, der, forces, interval)
    return (
        jnp.where(moved, corrected, kin),
        jnp.where(moved, forces, der),
        jnp.where(moved, time_now, last),
    )


def second_forces_kernel(
    n_blk, table_ref, force_ref, target_ref, early_a, early_b, early_c, centre_ref,
    kin_ref, der_ref, last_ref, mass_ref,
    out_ref, new_kin_ref, new_der_ref, new_last_ref, placed_ref, piece_ref, moment_ref,
):
    width = kin_ref.shape[1]
    place_forces(0, table_ref, force_ref, placed_ref)
    for part in range(width // prep_width):
        where = pl.ds(part * prep_width, prep_width)
        kin, der, last = moved_part(0, where, placed_ref, kin_ref, der_ref, last_ref)
        new_kin_ref[:, where] = kin
        new_der_ref[:, where] = der
        new_last_ref[:, where] = last
    centre = centre_ref[...]
    parts = every_part(piece_ref)
    late = late_chunks(table_ref, len(parts))
    steps = ahead_chunk // prep_width

    def listed(parts):
        write_listed(
            n_blk, parts, table_ref, centre, new_kin_ref, new_der_ref, new_last_ref, mass_ref,
            piece_ref, moment_ref,
        )

    listed(range(early_parts()))

    for more in range(early_chunks, len(parts)):

        @pl.when(late > more)
        def _(more=more):
            listed(range(more * steps, (more + 1) * steps))

    out_ref[...] = jnp.zeros_like(out_ref)

    def stars_of(index):
        return target_ref[index][0:6] - centre

    def store(index, result):
        place = table_ref[4, index]
        early = (early_a[index] + early_b[index]) + early_c[index]
        out_ref[(place // 4) * 2 + place % 2] = result + early

    for split in range(early_chunks, len(parts) + 1):

        @pl.when(late == split)
        def _(split=split):
            all_forces(0, table_ref[2, 8], parts[:split], stars_of, store, piece_ref, moment_ref)


def last_kernel(
    table_ref, force_ref, kin_ref, der_ref, last_ref, new_kin_ref, new_der_ref, placed_ref
):
    place_forces(1, table_ref, force_ref, placed_ref)
    for part in range(kin_ref.shape[1] // prep_width):
        where = pl.ds(part * prep_width, prep_width)
        kin, der, last = moved_part(1, where, placed_ref, kin_ref, der_ref, last_ref)
        new_kin_ref[:, where] = kin
        new_der_ref[:, where] = der


def shape_of(*sizes):
    return jax.ShapeDtypeStruct(sizes, F32)


def run_kernel(body, scalars, arrays, out_shape, scratch=(), after=None):
    scalar_specs = [pl.BlockSpec(memory_space=pltpu.SMEM)] * len(scalars)
    if after is not None:
        arrays = [after, *arrays]
    return pl.pallas_call(
        body,
        out_shape=out_shape,
        in_specs=scalar_specs
        + [pl.BlockSpec(memory_space=pltpu.VMEM)] * len(arrays),
        out_specs=jax.tree.map(lambda leaf: pl.BlockSpec(memory_space=pltpu.VMEM), out_shape),
        scratch_shapes=list(scratch),
        compiler_params=pltpu.CompilerParams(vmem_limit_bytes=32 * 2**20),
    )(*scalars, *arrays)


def plain_steps(kinematics, derivatives, mass, last, block_list, block_count):
    width = kinematics.shape[1]
    n_blk = lax.axis_size("blk")
    n_rep = lax.axis_size("rep")
    flat_list = block_list.reshape(-1)
    flat_count = block_count.reshape(-1)
    targets = run_kernel(
        functools.partial(targets_kernel, 0, n_blk, n_rep),
        [flat_list],
        [kinematics, derivatives, last],
        shape_of(n_blk, CAP * ROWS, BLOCK),
    )
    for step in range(STEPS):
        gathered = lax.all_to_all(targets, "blk", 0, 0, tiled=True)
        partial_forces = run_kernel(
            functools.partial(forces_kernel, step, n_blk, n_rep),
            [flat_count],
            [gathered.reshape(n_blk * CAP, ROWS, BLOCK), kinematics, derivatives, last, mass],
            shape_of(n_blk * CAP, ROWS, BLOCK),
            [
                pltpu.VMEM((6, width), F32),
                pltpu.VMEM((width, piece_rows), BF16),
                pltpu.VMEM((32, width), BF16),
            ],
        )
        partial_forces = partial_forces.reshape(n_blk, CAP * ROWS, BLOCK)
        spread = lax.all_to_all(partial_forces, "blk", 0, 0, tiled=True)
        mine = run_kernel(
            functools.partial(total_kernel, n_blk, n_rep),
            [],
            [spread],
            shape_of(n_rep, CAP * ROWS, BLOCK),
        )
        forces = lax.all_to_all(mine, "rep", 0, 0, tiled=True)
        out_shape = [shape_of(6, width), shape_of(6, width), shape_of(1, width)]
        if step + 1 < STEPS:
            out_shape.append(shape_of(n_blk, CAP * ROWS, BLOCK))
        kinematics, derivatives, last, *rest = run_kernel(
            functools.partial(update_kernel, step, n_blk, n_rep),
            [flat_list, flat_count],
            [forces.reshape(n_rep * CAP, ROWS, BLOCK), kinematics, derivatives, last],
            out_shape,
        )
        if rest:
            targets = rest[0]
    return (kinematics, derivatives)


def from_partner(value, distance):
    n_blk = lax.axis_size("blk")
    return lax.ppermute(value, "blk", [(i, i ^ distance) for i in range(n_blk)])


def shared_steps(kinematics, derivatives, mass, last, table, gathered, pieces, early_pieces):
    width = kinematics.shape[1]
    n_blk = lax.axis_size("blk")
    n_rep = lax.axis_size("rep")
    piece_scratch = [pltpu.VMEM((width, piece_rows), BF16), pltpu.VMEM((32, width), BF16)]
    partial_forces = run_kernel(
        first_forces_kernel,
        [table],
        [gathered, *pieces],
        shape_of(first_slots, ROWS, BLOCK),
    )
    value = partial_forces.reshape(first_slots * ROWS, BLOCK)
    value = value + from_partner(value, 1)

    def early_forces(turn, after, *more):
        return run_kernel(
            functools.partial(early_forces_kernel, turn),
            [table],
            [gathered, *early_pieces, pieces[2]],
            [shape_of(n_rep, ROWS, BLOCK), *more],
            after=after,
        )

    first_early, zero = early_forces(0, value, shape_of(first_slots * ROWS, BLOCK))
    value = (value + from_partner(value, 2)) + zero
    early = [first_early, *early_forces(1, value)]
    terms = [value] + [from_partner(value, distance) for distance in (4, 12, 8)]
    terms = [term.reshape(first_slots, ROWS, BLOCK) for term in terms]
    shares, forces = run_kernel(
        functools.partial(middle_kernel, n_rep),
        [table],
        [*terms, early[1]],
        [shape_of(n_rep, 2 * ROWS, BLOCK), shape_of(first_slots, ROWS, BLOCK)],
    )
    last_early, targets = early_forces(2, forces, shape_of(n_rep, ROWS, BLOCK))
    early.append(last_early)
    shares = lax.all_to_all(shares, "rep", 0, 0, tiled=True)
    shard = [kinematics, derivatives, last, mass]
    partial_forces, kinematics, derivatives, last = run_kernel(
        functools.partial(second_forces_kernel, n_blk),
        [table],
        [shares.reshape(n_rep * 2, ROWS, BLOCK), targets, *early, pieces[2], *shard],
        [shape_of(n_blk * 2, ROWS, BLOCK), shape_of(6, width), shape_of(6, width), shape_of(1, width)],
        [pltpu.VMEM((ROWS, width), F32)] + piece_scratch,
    )
    spread = lax.all_to_all(
        partial_forces.reshape(n_blk, 2 * ROWS, BLOCK), "blk", 0, 0, tiled=True
    )
    mine = run_kernel(
        functools.partial(flagged_total_kernel, n_blk, n_rep),
        [],
        [spread],
        shape_of(n_rep, 2 * ROWS, BLOCK),
    )
    shares = lax.all_to_all(mine, "rep", 0, 0, tiled=True)
    return run_kernel(
        last_kernel,
        [table],
        [shares.reshape(n_rep * 2, ROWS, BLOCK), kinematics, derivatives, last],
        [shape_of(6, width), shape_of(6, width)],
        [pltpu.VMEM((ROWS, width), F32)],
    )


def per_device(kinematics, derivatives, masses, last_time, block_list, block_count):
    width = kinematics.shape[1]
    n_blk = lax.axis_size("blk")
    n_rep = lax.axis_size("rep")
    mass = masses.reshape(1, width)
    last = last_time.reshape(1, width)
    table, targets = run_kernel(
        functools.partial(share_kernel, n_blk, n_rep),
        [],
        [block_list.transpose(0, 1, 3, 2), block_count, kinematics, derivatives, last],
        [jax.ShapeDtypeStruct((8, BLOCK), jnp.int32), shape_of(n_blk, 4 * ROWS, BLOCK)],
    )
    gathered = lax.all_to_all(targets, "blk", 0, 0, tiled=True)
    gathered = gathered.reshape(n_blk * 4, ROWS, BLOCK)
    piece_shapes = [
        jax.ShapeDtypeStruct((width, piece_rows), BF16),
        jax.ShapeDtypeStruct((32, width), BF16),
        shape_of(6, BLOCK),
    ]
    shard = [kinematics, derivatives, last, mass]
    pieces = run_kernel(
        functools.partial(pieces_kernel, n_blk),
        [],
        shard,
        piece_shapes,
        [pltpu.VMEM((6, width), F32)],
    )
    early_pieces = run_kernel(
        functools.partial(early_pieces_kernel, n_blk),
        [table],
        [*shard, pieces[2]],
        piece_shapes[:2],
    )
    return tuple(
        lax.cond(
            table[2, 0] > 0,
            lambda: tuple(
                shared_steps(
                    kinematics, derivatives, mass, last, table, gathered, pieces, early_pieces
                )
            ),
            lambda: tuple(
                plain_steps(kinematics, derivatives, mass, last, block_list, block_count)
            ),
        )
    )


def solution(mesh):
    return jax.shard_map(
        per_device,
        mesh=mesh,
        in_specs=(P(None, "blk"), P(None, "blk"), P("blk"), P("blk"), P(), P()),
        out_specs=(P(None, "blk"), P(None, "blk")),
        check_vma=False,
    )
```

```python
import functools

import jax
import jax.numpy as jnp
from jax import lax
from jax.experimental import pallas as pl
from jax.experimental.pallas import tpu as pltpu
from jax.sharding import PartitionSpec as P

BLOCK = 128
CAP = 2
STEPS = 2
ROWS = 8
F32 = jnp.float32
BF16 = jnp.bfloat16

step_length = 0.125
softening = 0.0025
grid_shift = 1.5 * 2.0**16
piece_rows = 128
chunk = 256
ahead_chunk = 1024
early_chunks = 2
early_pair = 2
prep_width = 512
first_slots = 12


def predict(position, velocity, acceleration, jerk_old, interval):
    new_position = position + interval * (
        velocity + interval * (acceleration * 0.5 + interval * jerk_old / 6.0)
    )
    new_velocity = velocity + interval * (acceleration + interval * jerk_old * 0.5)
    return jnp.concatenate([new_position, new_velocity], axis=0)


def correct(predicted, old_deriv, forces, interval):
    change = old_deriv[:3] - forces[:3]
    second_term = -6.0 * change - interval * (4.0 * old_deriv[3:] + 2.0 * forces[3:])
    third_term = 12.0 * change + 6.0 * interval * (old_deriv[3:] + forces[3:])
    new_position = predicted[:3] + interval * interval * (second_term / 24.0 + third_term / 120.0)
    new_velocity = predicted[3:] + interval * (second_term / 6.0 + third_term / 24.0)
    return jnp.concatenate([new_position, new_velocity], axis=0)


def round_short(value):
    return value.astype(BF16).astype(F32)


def split_three(value):
    high = round_short(value)
    rest = value - high
    middle = round_short(rest)
    return high, middle, rest - middle


def stack_three(value):
    return jnp.concatenate(split_three(value), axis=0)


def star_pieces(stars):
    position, velocity = stars[0:3], stars[3:6]
    coarse = (position + grid_shift) - grid_shift
    coarse_a = round_short(coarse)
    coarse_b = coarse - coarse_a
    fine = position - coarse
    fine_a = round_short(fine)
    fine_b = round_short(fine - fine_a)
    fine = fine_a + fine_b
    square = jnp.sum(coarse * coarse, axis=0, keepdims=True)
    cross = jnp.sum(2.0 * coarse * fine + fine * fine, axis=0, keepdims=True)
    mixed = jnp.sum(position * velocity, axis=0, keepdims=True)
    return coarse_a, coarse_b, fine_a, fine_b, square, cross, mixed


def source_pieces(stars):
    ca, cb, fa, fb, square, cross, mixed = star_pieces(stars)
    va, vb, vc = split_three(stars[3:6])
    width = stars.shape[1]
    one = jnp.ones((3, width), F32)
    rows = [ca, ca, cb, cb, stack_three(square), one, jnp.zeros((6, width), F32)]
    rows += [ca, ca, cb, cb, fa, fa, fb, fb, fa, fa, stack_three(cross), one]
    rows += [va, va, va, vb, vb, vc, stack_three(mixed), one]
    rows += [jnp.zeros((piece_rows - 84, width), F32)]
    return jnp.concatenate(rows, axis=0)


def target_pieces(stars):
    ca, cb, fa, fb, square, cross, mixed = star_pieces(stars)
    va, vb, vc = split_three(stars[3:6])
    xa, xb, xc = split_three(stars[0:3])
    width = stars.shape[1]
    one = jnp.ones((3, width), F32)
    zero = jnp.zeros((3, width), F32)
    da, db = -2.0 * ca, -2.0 * cb
    ea, eb = -2.0 * fa, -2.0 * fb
    tail = jnp.zeros((piece_rows - 84, width), F32)
    radius = [da, db, da, db, one, stack_three(square), zero, zero]
    radius += [ea, eb, ea, eb, da, db, da, db, ea, eb, one, stack_three(cross + softening)]
    radius += [zero] * 8 + [tail]
    moving = [-va, -vb, -va, -vb, zero, zero, zero, zero]
    moving += [-vc, zero, zero, zero, -va, -vb, -va, zero, zero, zero, zero, zero]
    moving += [-xa, -xb, -xc, -xa, -xb, -xa, one, stack_three(mixed), tail]
    both = [jnp.concatenate(radius, axis=0), jnp.concatenate(moving, axis=0)]
    return jnp.concatenate(both, axis=1).astype(BF16)


def block_at(number):
    return pl.ds(pl.multiple_of(number * BLOCK, BLOCK), BLOCK)


def predicted_block(kin_ref, der_ref, last_ref, where, time_now):
    kin, der = kin_ref[:, where], der_ref[:, where]
    return predict(kin[:3], kin[3:], der[:3], der[3:], time_now - last_ref[:, where])


def list_place(step, blk, rep, slot, n_blk, n_rep):
    return ((step * n_blk + blk) * n_rep + rep) * CAP + slot


def write_targets(step, n_blk, n_rep, list_ref, kin_ref, der_ref, last_ref, out_ref):
    blk, rep = lax.axis_index("blk"), lax.axis_index("rep")
    rows = []
    for slot in range(CAP):
        number = list_ref[list_place(step, blk, rep, slot, n_blk, n_rep)]
        rows.append(predicted_block(kin_ref, der_ref, last_ref, block_at(number), step * step_length))
        rows.append(jnp.zeros((ROWS - 6, BLOCK), F32))
    mine = jnp.concatenate(rows, axis=0)
    for other in range(n_blk):
        out_ref[other] = mine


def targets_kernel(step, n_blk, n_rep, list_ref, kin_ref, der_ref, last_ref, out_ref):
    write_targets(step, n_blk, n_rep, list_ref, kin_ref, der_ref, last_ref, out_ref)


def forces_kernel(
    step, n_blk, n_rep, count_ref, target_ref, kin_ref, der_ref, last_ref, mass_ref,
    out_ref, pred_ref, piece_ref, moment_ref,
):
    rep = lax.axis_index("rep")
    width = kin_ref.shape[1]
    total = jnp.zeros((6, prep_width), F32)
    for part in range(width // prep_width):
        where = pl.ds(part * prep_width, prep_width)
        stars = predicted_block(kin_ref, der_ref, last_ref, where, step * step_length)
        pred_ref[:, where] = stars
        total = total + stars
    centre = jnp.sum(total, axis=1, keepdims=True) / width
    for part in range(width // prep_width):
        where = pl.ds(part * prep_width, prep_width)
        stars = pred_ref[:, where] - centre
        piece_ref[where, :] = source_pieces(stars).T.astype(BF16)
        scaled = mass_ref[:, where] / (width * n_blk)
        ones = jnp.ones((1, prep_width), F32)
        moments = jnp.concatenate([stars, ones, jnp.zeros_like(ones)], axis=0) * scaled
        moments = jnp.concatenate([stack_three(moments), jnp.zeros((8, prep_width), F32)], axis=0)
        moment_ref[:, where] = moments.astype(BF16)

    def one_slot(place, carry):
        blk = place // CAP
        slot = place % CAP
        active = slot < count_ref[(step * n_blk + blk) * n_rep + rep]

        @pl.when(active)
        def _():
            stars = target_ref[place][0:6] - centre
            against = target_pieces(stars)
            acc = jnp.zeros((32, 2 * BLOCK), F32)
            for part in range(width // chunk):
                where = pl.ds(part * chunk, chunk)
                both = jnp.dot(piece_ref[where, :], against, preferred_element_type=F32)
                inverse = lax.rsqrt(both[:, :BLOCK])
                inverse_sq = inverse * inverse
                weight = inverse * inverse_sq
                radial = weight * (inverse_sq * both[:, BLOCK:])
                pair = jnp.concatenate([weight, radial], axis=1)
                high = pair.astype(BF16)
                low = (pair - high.astype(F32)).astype(BF16)
                moments = moment_ref[:, where]
                acc = acc + jnp.dot(moments, high, preferred_element_type=F32)
                acc = acc + jnp.dot(moments, low, preferred_element_type=F32)
            acc = acc[0:8] + acc[8:16] + acc[16:24]
            by_weight, by_radial = acc[:, :BLOCK], acc[:, BLOCK:]
            sums = by_weight[0:6] - stars * by_weight[6:7]
            pull = by_radial[0:3] - stars[0:3] * by_radial[6:7]
            out_ref[place] = jnp.concatenate(
                [sums[0:3], sums[3:6] - 3.0 * pull, jnp.zeros((ROWS - 6, BLOCK), F32)], axis=0
            )

        @pl.when(jnp.logical_not(active))
        def _():
            out_ref[place] = jnp.zeros((ROWS, BLOCK), F32)

        return carry

    lax.fori_loop(0, n_blk * CAP, one_slot, 0)


def total_kernel(n_blk, n_rep, part_ref, out_ref):
    total = part_ref[0]
    for other in range(1, n_blk):
        total = total + part_ref[other]
    for other in range(n_rep):
        out_ref[other] = total


def update_kernel(
    step, n_blk, n_rep, list_ref, count_ref, force_ref, kin_ref, der_ref, last_ref,
    new_kin_ref, new_der_ref, new_last_ref, *next_refs,
):
    blk = lax.axis_index("blk")
    time_now = step * step_length
    new_kin_ref[...] = kin_ref[...]
    new_der_ref[...] = der_ref[...]
    new_last_ref[...] = last_ref[...]

    def one_slot(place, carry):
        rep = place // CAP
        slot = place % CAP

        @pl.when(slot < count_ref[(step * n_blk + blk) * n_rep + rep])
        def _():
            number = list_ref[list_place(step, blk, rep, slot, n_blk, n_rep)]
            where = block_at(number)
            predicted = predicted_block(kin_ref, der_ref, last_ref, where, time_now)
            forces = force_ref[place][0:6]
            interval = time_now - last_ref[:, where]
            new_kin_ref[:, where] = correct(predicted, der_ref[:, where], forces, interval)
            new_der_ref[:, where] = forces
            new_last_ref[:, where] = jnp.full((1, BLOCK), time_now, F32)

        return carry

    lax.fori_loop(0, n_rep * CAP, one_slot, 0)
    if next_refs:
        write_targets(
            step + 1, n_blk, n_rep, list_ref, new_kin_ref, new_der_ref, new_last_ref, next_refs[0]
        )


def lane_iota(rows):
    return lax.broadcasted_iota(jnp.int32, (rows, BLOCK), 1)


def active_rows(n_blk, n_rep, list_ref, count_ref):
    per_row = BLOCK // n_rep
    parts = n_rep * CAP // per_row
    lanes = lane_iota(n_blk)
    steps = []
    for step in range(STEPS):
        counted = count_ref[step]
        tiled = []
        for slot in range(CAP):
            listed = jnp.where(counted > slot, list_ref[step, :, slot, :], -1)
            tiled.append(jnp.concatenate([listed] * per_row, axis=1))
        hits = []
        for part in range(parts):
            number = lanes // n_rep + part * per_row
            hit = (tiled[0] == number) | (tiled[1] == number)
            hits.append(jnp.where(hit, 1.0, 0.0))
        steps.append(jnp.concatenate(hits, axis=1))
    hits = jnp.concatenate(steps, axis=0).astype(BF16)
    width = parts * BLOCK
    rows = lax.broadcasted_iota(jnp.int32, (width, BLOCK), 0) // n_rep
    spread = jnp.where(rows == lax.broadcasted_iota(jnp.int32, (width, BLOCK), 1), 1.0, 0.0)
    return jnp.dot(hits, spread.astype(BF16), preferred_element_type=F32)


def share_blocks(n_blk, n_rep, list_ref, count_ref, table_ref):
    blk, rep = lax.axis_index("blk"), lax.axis_index("rep")
    flags = active_rows(n_blk, n_rep, list_ref, count_ref)
    first, second = flags[:n_blk], flags[n_blk:]
    in_both = first * second
    kinds = [in_both, first - in_both, second - in_both]
    earlier = lax.broadcasted_iota(jnp.int32, (BLOCK, BLOCK), 0) < lax.broadcasted_iota(
        jnp.int32, (BLOCK, BLOCK), 1
    )
    earlier = jnp.where(earlier, 1.0, 0.0).astype(BF16)
    above = lax.broadcasted_iota(jnp.int32, (n_blk, n_blk), 0) > lax.broadcasted_iota(
        jnp.int32, (n_blk, n_blk), 1
    )
    above = jnp.where(above, 1.0, 0.0).astype(BF16)
    own_row = lax.broadcasted_iota(jnp.int32, (n_blk, BLOCK), 0) == blk
    lanes = lane_iota(1)
    order = lanes * n_rep + rep
    start = jnp.zeros((1, 1), F32)
    fits = jnp.ones((1, 1), jnp.bool_)
    own_kind, own_place, own_rank, finish, owner = [], [], [], [], []
    for kind in kinds:
        short = kind.astype(BF16)
        rank = jnp.dot(short, earlier, preferred_element_type=F32)
        before = jnp.dot(above, short, preferred_element_type=F32)
        before = jnp.sum(before, axis=1, keepdims=True) + start
        amount = jnp.sum(kind, axis=1, keepdims=True)
        fits = fits & (jnp.max(amount, axis=0, keepdims=True) <= n_rep)
        ends = (before + amount).astype(jnp.int32)
        owner.append(jnp.sum(jnp.where(ends <= order, 1, 0), axis=0, keepdims=True))
        place = jnp.sum(jnp.where(own_row, before + rank, 0.0), axis=0, keepdims=True)
        own_place.append(place.astype(jnp.int32))
        own_rank.append(jnp.sum(jnp.where(own_row, rank, 0.0), axis=0, keepdims=True))
        own_kind.append(jnp.sum(jnp.where(own_row, kind, 0.0), axis=0, keepdims=True) > 0.5)
        finish.append((jnp.max(before + amount, axis=0, keepdims=True)).astype(jnp.int32))
        if len(finish) == 1:
            start = jnp.sum(amount, axis=0, keepdims=True)
    both_end = finish[0]
    total = [jnp.maximum(finish[0], finish[1]), jnp.maximum(finish[0], finish[2])]
    fits = fits & (total[0] <= n_rep * first_slots) & (total[1] <= n_rep * n_rep)
    handler = [jnp.bitwise_and(place, n_rep - 1) for place in own_place]
    home = []
    for step in range(STEPS):
        code = jnp.where(own_kind[0], handler[0] * 2, -1)
        home.append(jnp.where(own_kind[1 + step], handler[1 + step] * 2 + 1, code))
    places = []
    for step in range(STEPS):
        is_both = order < both_end
        places.append(jnp.where(is_both, owner[0] * 4, owner[1 + step] * 4 + 2 + step))
    scalars = jnp.where(lanes == 0, jnp.where(fits, 1, 0), 0)
    numbers = []
    for index in range(3):
        mine = own_kind[index] & (handler[index] == rep)
        numbers.append(jnp.sum(jnp.where(mine, lanes.astype(F32), 0.0)).astype(jnp.int32))
        spot = jnp.max(jnp.where(mine, own_place[index] // n_rep, 0), axis=1, keepdims=True)
        scalars = jnp.where(lanes == 4 + index, spot, scalars)
    for step in range(STEPS):
        amount = (total[step] - rep + n_rep - 1) // n_rep
        scalars = jnp.where(lanes == 7 + step, amount, scalars)
    amount = (both_end - rep + n_rep - 1) // n_rep
    scalars = jnp.where(lanes == 9, amount, scalars)
    moved = own_kind[0] | own_kind[1]
    moved_amount = jnp.sum(jnp.where(moved, 1, 0), axis=1, keepdims=True)
    scalars = jnp.where(lanes == 10, moved_amount, scalars)
    moved_rank = (own_rank[0] + own_rank[1]).astype(jnp.int32)
    spots = jnp.where(moved, moved_rank, moved_amount + lanes - moved_rank)
    listed = (prep_width // BLOCK) * 8
    numbers_down = lax.broadcasted_iota(jnp.int32, (listed, BLOCK), 0)
    spots_down = jnp.sum(jnp.where(numbers_down == lanes, spots, 0), axis=1, keepdims=True)
    members = jnp.sum(jnp.where(spots_down == lanes, numbers_down, 0), axis=0, keepdims=True)
    gap = jnp.zeros((1, BLOCK), jnp.int32)
    rows = [home[0], home[1], scalars, places[0], places[1], spots, members, gap]
    table_ref[...] = jnp.concatenate(rows, axis=0)
    return numbers


def share_kernel(n_blk, n_rep, list_ref, count_ref, kin_ref, der_ref, last_ref, table_ref, out_ref):
    numbers = share_blocks(n_blk, n_rep, list_ref, count_ref, table_ref)
    top = kin_ref.shape[1] // BLOCK - 1
    where = [block_at(jnp.minimum(number, top)) for number in numbers]
    gap = jnp.zeros((2, BLOCK), F32)
    rows = [
        predicted_block(kin_ref, der_ref, last_ref, where[0], 0.0),
        0.0 - last_ref[:, where[0]],
        gap[0:1],
        der_ref[:, where[0]],
        gap,
        predicted_block(kin_ref, der_ref, last_ref, where[1], 0.0),
        gap,
        predicted_block(kin_ref, der_ref, last_ref, where[2], step_length),
        gap,
    ]
    mine = jnp.concatenate(rows, axis=0)
    for other in range(n_blk):
        out_ref[other] = mine


def write_part(n_blk, width, stars, mass, where, piece_ref, moment_ref):
    piece_ref[where, :] = source_pieces(stars).T.astype(BF16)
    ones = jnp.ones((1, prep_width), F32)
    moments = jnp.concatenate([stars, ones, jnp.zeros_like(ones)], axis=0) * (mass / (width * n_blk))
    moments = jnp.concatenate([stack_three(moments), jnp.zeros((8, prep_width), F32)], axis=0)
    moment_ref[:, where] = moments.astype(BF16)


def write_pieces(n_blk, kin_ref, der_ref, last_ref, mass_ref, pred_ref, piece_ref, moment_ref):
    width = kin_ref.shape[1]
    total = jnp.zeros((6, prep_width), F32)
    for part in range(width // prep_width):
        where = pl.ds(part * prep_width, prep_width)
        stars = predicted_block(kin_ref, der_ref, last_ref, where, 0.0)
        pred_ref[:, where] = stars
        total = total + stars
    centre = jnp.sum(total, axis=1, keepdims=True) / width
    for part in range(width // prep_width):
        where = pl.ds(part * prep_width, prep_width)
        stars = pred_ref[:, where] - centre
        write_part(n_blk, width, stars, mass_ref[:, where], where, piece_ref, moment_ref)
    return centre


def write_listed(
    n_blk, parts, table_ref, centre, kin_ref, der_ref, last_ref, mass_ref, piece_ref, moment_ref
):
    blocks = prep_width // BLOCK
    for part in parts:
        places = [block_at(table_ref[6, part * blocks + index]) for index in range(blocks)]
        stars = [predicted_block(kin_ref, der_ref, last_ref, one, step_length) for one in places]
        stars = jnp.concatenate([one - centre for one in stars], axis=1)
        mass = jnp.concatenate([mass_ref[:, one] for one in places], axis=1)
        where = pl.ds(part * prep_width, prep_width)
        write_part(n_blk, kin_ref.shape[1], stars, mass, where, piece_ref, moment_ref)


def block_forces(blocks, parts, piece_ref, moment_ref):
    against = [target_pieces(stars) for stars in blocks]
    order = [(index, part) for index in range(len(blocks)) for part in parts]
    by_weight = [jnp.zeros((32, 2 * BLOCK), F32) for stars in blocks]
    by_radial = [jnp.zeros((32, 2 * BLOCK), F32) for stars in blocks]

    def meet(index, part):
        where = pl.ds(part * ahead_chunk, ahead_chunk)
        return jnp.dot(piece_ref[where, :], against[index], preferred_element_type=F32)

    def halves(value):
        high = value.astype(BF16)
        low = (value - high.astype(F32)).astype(BF16)
        return jnp.concatenate([high, low], axis=1)

    both = meet(*order[0])
    for turn, (index, part) in enumerate(order):
        ahead = meet(*order[turn + 1]) if turn + 1 < len(order) else None
        inverse = lax.rsqrt(both[:, :BLOCK])
        inverse_sq = inverse * inverse
        weight = inverse * inverse_sq
        radial = weight * (inverse_sq * both[:, BLOCK:])
        moments = moment_ref[:, pl.ds(part * ahead_chunk, ahead_chunk)]
        by_weight[index] += jnp.dot(moments, halves(weight), preferred_element_type=F32)
        by_radial[index] += jnp.dot(moments, halves(radial), preferred_element_type=F32)
        both = ahead

    def gather_up(value):
        value = value[0:8] + value[8:16] + value[16:24]
        return value[:, :BLOCK] + value[:, BLOCK:]

    results = []
    for index, stars in enumerate(blocks):
        on_weight, on_radial = gather_up(by_weight[index]), gather_up(by_radial[index])
        sums = on_weight[0:6] - stars * on_weight[6:7]
        pull = on_radial[0:3] - stars[0:3] * on_radial[6:7]
        gap = jnp.zeros((ROWS - 6, BLOCK), F32)
        results.append(jnp.concatenate([sums[0:3], sums[3:6] - 3.0 * pull, gap], axis=0))
    return results


def all_forces(begin, end, parts, stars_of, store, piece_ref, moment_ref):
    def some(first, size):
        blocks = [stars_of(first + index) for index in range(size)]
        results = block_forces(blocks, parts, piece_ref, moment_ref)
        for index, result in enumerate(results):
            store(first + index, result)

    pairs = (end - begin) // 2

    def two(pair, carry):
        some(begin + pair * 2, 2)
        return carry

    lax.fori_loop(0, pairs, two, 0)

    @pl.when(end > begin + pairs * 2)
    def _():
        some(begin + pairs * 2, 1)


def every_part(piece_ref):
    return list(range(piece_ref.shape[0] // ahead_chunk))


def pieces_kernel(
    n_blk, kin_ref, der_ref, last_ref, mass_ref, piece_ref, moment_ref, centre_ref, pred_ref
):
    centre = write_pieces(
        n_blk, kin_ref, der_ref, last_ref, mass_ref, pred_ref, piece_ref, moment_ref
    )
    centre_ref[...] = jnp.broadcast_to(centre, (6, BLOCK))


def early_parts():
    return early_chunks * ahead_chunk // prep_width


def early_pieces_kernel(
    n_blk, table_ref, kin_ref, der_ref, last_ref, mass_ref, centre_ref, piece_ref, moment_ref
):
    centre = centre_ref[...]
    parts = range(early_parts(), kin_ref.shape[1] // prep_width)
    piece_ref[pl.ds(0, early_chunks * ahead_chunk), :] = jnp.zeros(
        (early_chunks * ahead_chunk, piece_rows), BF16
    )
    moment_ref[:, pl.ds(0, early_chunks * ahead_chunk)] = jnp.zeros(
        (32, early_chunks * ahead_chunk), BF16
    )
    write_listed(
        n_blk, parts, table_ref, centre, kin_ref, der_ref, last_ref, mass_ref, piece_ref, moment_ref
    )


def late_chunks(table_ref, chunks):
    needed = (table_ref[2, 10] * BLOCK + ahead_chunk - 1) // ahead_chunk
    return jnp.minimum(jnp.maximum(needed, early_chunks), chunks)


def early_forces_kernel(
    turn, table_ref, after_ref, target_ref, piece_ref, moment_ref, centre_ref, out_ref, *more_refs
):
    out_ref[...] = jnp.zeros_like(out_ref)
    last = turn == 2
    if last:
        write_next_targets(table_ref, after_ref, target_ref, more_refs[0])
        target_ref = more_refs[0]
    else:
        for zero_ref in more_refs:
            zero_ref[...] = jnp.zeros_like(zero_ref)
    moved_end, end = table_ref[2, 9], table_ref[2, 8]
    begin = jnp.minimum(moved_end + turn * early_pair, end)

    def number(index):
        if not last:
            return begin + index
        return jnp.where(index < end - begin, begin + index, index - (end - begin))

    def stars_of(index):
        place = number(index) if last else table_ref[4, number(index)]
        return target_ref[place][0:6] - centre_ref[...]

    def store(index, result):
        out_ref[number(index)] = result

    amount = end - begin + moved_end if last else jnp.minimum(early_pair, end - begin)

    parts = every_part(piece_ref)
    late = late_chunks(table_ref, len(parts))

    for split in range(early_chunks, len(parts)):

        @pl.when(late == split)
        def _(split=split):
            all_forces(0, amount, parts[split:], stars_of, store, piece_ref, moment_ref)


def first_forces_kernel(table_ref, target_ref, piece_ref, moment_ref, centre_ref, out_ref):
    out_ref[...] = jnp.zeros_like(out_ref)

    def stars_of(index):
        return target_ref[table_ref[3, index]][0:6] - centre_ref[...]

    def store(index, result):
        out_ref[index] = result

    all_forces(0, table_ref[2, 7], every_part(piece_ref), stars_of, store, piece_ref, moment_ref)


def flag_rows():
    rows = lax.broadcasted_iota(jnp.int32, (CAP * ROWS, BLOCK), 0)
    return jnp.bitwise_and(rows, ROWS - 1) == 6


def flagged_total_kernel(n_blk, n_rep, part_ref, out_ref):
    total = part_ref[0]
    for other in range(1, n_blk):
        total = total + part_ref[other]
    total = jnp.where(flag_rows(), 1.0, total)
    for other in range(n_rep):
        out_ref[other] = total


def middle_kernel(
    n_rep, table_ref, term_a, term_b, term_c, term_d, early_ref, share_ref, force_ref
):
    force_ref[...] = term_a[...] + ((term_b[...] + term_c[...]) + term_d[...])
    own = jnp.concatenate([force_ref[table_ref[2, 4]], force_ref[table_ref[2, 5]]], axis=0)
    own = jnp.where(flag_rows(), 1.0, own)
    for other in range(n_rep):
        share_ref[other] = own


def write_next_targets(table_ref, force_ref, target_ref, next_ref):
    def one(index, carry):
        place = table_ref[4, index]
        is_both = index < table_ref[2, 9]

        @pl.when(is_both)
        def _():
            head, deriv = target_ref[place], target_ref[place + 1][0:6]
            forces = force_ref[index][0:6]
            moved = correct(head[0:6], deriv, forces, head[6:7])
            ahead = predict(moved[:3], moved[3:], forces[:3], forces[3:], step_length)
            next_ref[index] = jnp.concatenate([ahead, head[6:8]], axis=0)

        @pl.when(jnp.logical_not(is_both))
        def _():
            next_ref[index] = target_ref[place]

        return carry

    lax.fori_loop(0, table_ref[2, 8], one, 0)


def place_forces(step, table_ref, force_ref, placed_ref):
    for number in range(placed_ref.shape[1] // BLOCK):
        code = table_ref[step, number]
        tile = force_ref[jnp.maximum(code, 0)]
        tile = tile * jnp.where(code >= 0, 1.0, 0.0)
        placed_ref[:, pl.ds(number * BLOCK, BLOCK)] = tile


def moved_part(step, where, placed_ref, kin_ref, der_ref, last_ref):
    time_now = step * step_length
    placed = placed_ref[:, where]
    forces, moved = placed[0:6], placed[6:7] > 0.5
    kin, der, last = kin_ref[:, where], der_ref[:, where], last_ref[:, where]
    interval = time_now - last
    predicted = predict(kin[:3], kin[3:], der[:3], der[3:], interval)
    corrected = correct(predicted, der, forces, interval)
    return (
        jnp.where(moved, corrected, kin),
        jnp.where(moved, forces, der),
        jnp.where(moved, time_now, last),
    )


def second_forces_kernel(
    n_blk, table_ref, force_ref, target_ref, early_a, early_b, early_c, centre_ref,
    kin_ref, der_ref, last_ref, mass_ref,
    out_ref, new_kin_ref, new_der_ref, new_last_ref, placed_ref, piece_ref, moment_ref,
):
    width = kin_ref.shape[1]
    place_forces(0, table_ref, force_ref, placed_ref)
    for part in range(width // prep_width):
        where = pl.ds(part * prep_width, prep_width)
        kin, der, last = moved_part(0, where, placed_ref, kin_ref, der_ref, last_ref)
        new_kin_ref[:, where] = kin
        new_der_ref[:, where] = der
        new_last_ref[:, where] = last
    centre = centre_ref[...]
    parts = every_part(piece_ref)
    late = late_chunks(table_ref, len(parts))
    steps = ahead_chunk // prep_width

    def listed(parts):
        write_listed(
            n_blk, parts, table_ref, centre, new_kin_ref, new_der_ref, new_last_ref, mass_ref,
            piece_ref, moment_ref,
        )

    listed(range(early_parts()))

    for more in range(early_chunks, len(parts)):

        @pl.when(late > more)
        def _(more=more):
            listed(range(more * steps, (more + 1) * steps))

    out_ref[...] = jnp.zeros_like(out_ref)

    def stars_of(index):
        return target_ref[index][0:6] - centre

    def store(index, result):
        place = table_ref[4, index]
        early = (early_a[index] + early_b[index]) + early_c[index]
        out_ref[(place // 4) * 2 + place % 2] = result + early

    for split in range(early_chunks, len(parts) + 1):

        @pl.when(late == split)
        def _(split=split):
            all_forces(0, table_ref[2, 8], parts[:split], stars_of, store, piece_ref, moment_ref)


def last_kernel(
    table_ref, force_ref, kin_ref, der_ref, last_ref, new_kin_ref, new_der_ref, placed_ref
):
    place_forces(1, table_ref, force_ref, placed_ref)
    for part in range(kin_ref.shape[1] // prep_width):
        where = pl.ds(part * prep_width, prep_width)
        kin, der, last = moved_part(1, where, placed_ref, kin_ref, der_ref, last_ref)
        new_kin_ref[:, where] = kin
        new_der_ref[:, where] = der


def shape_of(*sizes):
    return jax.ShapeDtypeStruct(sizes, F32)


def run_kernel(body, scalars, arrays, out_shape, scratch=(), after=None):
    scalar_specs = [pl.BlockSpec(memory_space=pltpu.SMEM)] * len(scalars)
    if after is not None:
        arrays = [after, *arrays]
    return pl.pallas_call(
        body,
        out_shape=out_shape,
        in_specs=scalar_specs
        + [pl.BlockSpec(memory_space=pltpu.VMEM)] * len(arrays),
        out_specs=jax.tree.map(lambda leaf: pl.BlockSpec(memory_space=pltpu.VMEM), out_shape),
        scratch_shapes=list(scratch),
        compiler_params=pltpu.CompilerParams(vmem_limit_bytes=32 * 2**20),
    )(*scalars, *arrays)


def plain_steps(kinematics, derivatives, mass, last, block_list, block_count):
    width = kinematics.shape[1]
    n_blk = lax.axis_size("blk")
    n_rep = lax.axis_size("rep")
    flat_list = block_list.reshape(-1)
    flat_count = block_count.reshape(-1)
    targets = run_kernel(
        functools.partial(targets_kernel, 0, n_blk, n_rep),
        [flat_list],
        [kinematics, derivatives, last],
        shape_of(n_blk, CAP * ROWS, BLOCK),
    )
    for step in range(STEPS):
        gathered = lax.all_to_all(targets, "blk", 0, 0, tiled=True)
        partial_forces = run_kernel(
            functools.partial(forces_kernel, step, n_blk, n_rep),
            [flat_count],
            [gathered.reshape(n_blk * CAP, ROWS, BLOCK), kinematics, derivatives, last, mass],
            shape_of(n_blk * CAP, ROWS, BLOCK),
            [
                pltpu.VMEM((6, width), F32),
                pltpu.VMEM((width, piece_rows), BF16),
                pltpu.VMEM((32, width), BF16),
            ],
        )
        partial_forces = partial_forces.reshape(n_blk, CAP * ROWS, BLOCK)
        spread = lax.all_to_all(partial_forces, "blk", 0, 0, tiled=True)
        mine = run_kernel(
            functools.partial(total_kernel, n_blk, n_rep),
            [],
            [spread],
            shape_of(n_rep, CAP * ROWS, BLOCK),
        )
        forces = lax.all_to_all(mine, "rep", 0, 0, tiled=True)
        out_shape = [shape_of(6, width), shape_of(6, width), shape_of(1, width)]
        if step + 1 < STEPS:
            out_shape.append(shape_of(n_blk, CAP * ROWS, BLOCK))
        kinematics, derivatives, last, *rest = run_kernel(
            functools.partial(update_kernel, step, n_blk, n_rep),
            [flat_list, flat_count],
            [forces.reshape(n_rep * CAP, ROWS, BLOCK), kinematics, derivatives, last],
            out_shape,
        )
        if rest:
            targets = rest[0]
    return (kinematics, derivatives)


def from_partner(value, distance):
    n_blk = lax.axis_size("blk")
    return lax.ppermute(value, "blk", [(i, i ^ distance) for i in range(n_blk)])


def shared_steps(kinematics, derivatives, mass, last, table, gathered, pieces, early_pieces):
    width = kinematics.shape[1]
    n_blk = lax.axis_size("blk")
    n_rep = lax.axis_size("rep")
    piece_scratch = [pltpu.VMEM((width, piece_rows), BF16), pltpu.VMEM((32, width), BF16)]
    partial_forces = run_kernel(
        first_forces_kernel,
        [table],
        [gathered, *pieces],
        shape_of(first_slots, ROWS, BLOCK),
    )
    value = partial_forces.reshape(first_slots * ROWS, BLOCK)
    value = value + from_partner(value, 1)

    def early_forces(turn, after, *more):
        return run_kernel(
            functools.partial(early_forces_kernel, turn),
            [table],
            [gathered, *early_pieces, pieces[2]],
            [shape_of(n_rep, ROWS, BLOCK), *more],
            after=after,
        )

    first_early, zero = early_forces(0, value, shape_of(first_slots * ROWS, BLOCK))
    value = (value + from_partner(value, 2)) + zero
    early = [first_early, *early_forces(1, value)]
    terms = [value] + [from_partner(value, distance) for distance in (4, 12, 8)]
    terms = [term.reshape(first_slots, ROWS, BLOCK) for term in terms]
    shares, forces = run_kernel(
        functools.partial(middle_kernel, n_rep),
        [table],
        [*terms, early[1]],
        [shape_of(n_rep, 2 * ROWS, BLOCK), shape_of(first_slots, ROWS, BLOCK)],
    )
    last_early, targets = early_forces(2, forces, shape_of(n_rep, ROWS, BLOCK))
    early.append(last_early)
    shares = lax.all_to_all(shares, "rep", 0, 0, tiled=True)
    shard = [kinematics, derivatives, last, mass]
    partial_forces, kinematics, derivatives, last = run_kernel(
        functools.partial(second_forces_kernel, n_blk),
        [table],
        [shares.reshape(n_rep * 2, ROWS, BLOCK), targets, *early, pieces[2], *shard],
        [shape_of(n_blk * 2, ROWS, BLOCK), shape_of(6, width), shape_of(6, width), shape_of(1, width)],
        [pltpu.VMEM((ROWS, width), F32)] + piece_scratch,
    )
    spread = lax.all_to_all(
        partial_forces.reshape(n_blk, 2 * ROWS, BLOCK), "blk", 0, 0, tiled=True
    )
    mine = run_kernel(
        functools.partial(flagged_total_kernel, n_blk, n_rep),
        [],
        [spread],
        shape_of(n_rep, 2 * ROWS, BLOCK),
    )
    shares = lax.all_to_all(mine, "rep", 0, 0, tiled=True)
    return run_kernel(
        last_kernel,
        [table],
        [shares.reshape(n_rep * 2, ROWS, BLOCK), kinematics, derivatives, last],
        [shape_of(6, width), shape_of(6, width)],
        [pltpu.VMEM((ROWS, width), F32)],
    )


def per_device(kinematics, derivatives, masses, last_time, block_list, block_count):
    width = kinematics.shape[1]
    n_blk = lax.axis_size("blk")
    n_rep = lax.axis_size("rep")
    mass = masses.reshape(1, width)
    last = last_time.reshape(1, width)
    table, targets = run_kernel(
        functools.partial(share_kernel, n_blk, n_rep),
        [],
        [block_list.transpose(0, 1, 3, 2), block_count, kinematics, derivatives, last],
        [jax.ShapeDtypeStruct((8, BLOCK), jnp.int32), shape_of(n_blk, 4 * ROWS, BLOCK)],
    )
    gathered = lax.all_to_all(targets, "blk", 0, 0, tiled=True)
    gathered = gathered.reshape(n_blk * 4, ROWS, BLOCK)
    piece_shapes = [
        jax.ShapeDtypeStruct((width, piece_rows), BF16),
        jax.ShapeDtypeStruct((32, width), BF16),
        shape_of(6, BLOCK),
    ]
    shard = [kinematics, derivatives, last, mass]
    pieces = run_kernel(
        functools.partial(pieces_kernel, n_blk),
        [],
        shard,
        piece_shapes,
        [pltpu.VMEM((6, width), F32)],
    )
    early_pieces = run_kernel(
        functools.partial(early_pieces_kernel, n_blk),
        [table],
        [*shard, pieces[2]],
        piece_shapes[:2],
    )
    return tuple(
        lax.cond(
            table[2, 0] > 0,
            lambda: tuple(
                shared_steps(
                    kinematics, derivatives, mass, last, table, gathered, pieces, early_pieces
                )
            ),
            lambda: tuple(
                plain_steps(kinematics, derivatives, mass, last, block_list, block_count)
            ),
        )
    )


def solution(mesh):
    return jax.shard_map(
        per_device,
        mesh=mesh,
        in_specs=(P(None, "blk"), P(None, "blk"), P("blk"), P("blk"), P(), P()),
        out_specs=(P(None, "blk"), P(None, "blk")),
        check_vma=False,
    )
```
